32 devices in a mesh: dp: 8 (over z, y), fsdp: 4 (over x, core).
Axes of the slice: x: 2, y: 2, z: 4, core: 2. Of those that a mesh axis runs over, the one named last changes fastest.
Arguments:
- patches: bfloat16 [16384, 768], P(('dp', 'fsdp')), may hold values from -6 to 6
- order: int32 [128, 196], P(('dp', 'fsdp')), may hold values from 0 to 195, each once within a row
- grad_latent: float32 [16384, 768], P(('dp', 'fsdp')), may hold values from -6 to 6
- grad_out: float32 [16384, 768], P(('dp', 'fsdp')), may hold values from -6 to 6
- pos_embed: bfloat16 [196, 768], P(None, ('dp', 'fsdp')), may hold values from -6 to 6
- ln_gain: bfloat16 [2, 2, 768], P(None, None, ('dp', 'fsdp')), may hold values from 0.099609375 to 1.8984375
- ln_bias: bfloat16 [2, 2, 768], P(None, None, ('dp', 'fsdp')), may hold values from -2 to 2
- w_qkv: bfloat16 [2, 768, 2304], P(None, ('dp', 'fsdp')), may hold values from -0.21875 to 0.21875
- b_qkv: bfloat16 [2, 1536], P(None, ('dp', 'fsdp')), may hold values from -2 to 2
- w_proj: bfloat16 [2, 768, 768], P(None, ('dp', 'fsdp')), may hold values from -0.875 to 0.875
- b_proj: bfloat16 [2, 768], P(None, ('dp', 'fsdp')), may hold values from -2 to 2
- w_fc1: bfloat16 [2, 768, 3072], P(None, ('dp', 'fsdp')), may hold values from -0.21875 to 0.21875
- b_fc1: bfloat16 [2, 3072], P(None, ('dp', 'fsdp')), may hold values from -2 to 2
- w_fc2: bfloat16 [2, 3072, 768], P(None, ('dp', 'fsdp')), may hold values from -0.15625 to 0.15625
- b_fc2: bfloat16 [2, 768], P(None, ('dp', 'fsdp')), may hold values from -2 to 2
- layer_scale: bfloat16 [2, 2, 768], P(None, None, ('dp', 'fsdp')), may hold values from 0.5 to 1.5
Outputs:
- latent: bfloat16 [16384, 768], P(('dp', 'fsdp'))
- regressed: bfloat16 [16384, 768], P(('dp', 'fsdp'))
- grad_patches: float32 [16384, 768], P(('dp', 'fsdp'))
- grad_pos: float32 [196, 768], P(None, ('dp', 'fsdp'))
- grad_ln_gain: float32 [2, 2, 768], P(None, None, ('dp', 'fsdp'))
- grad_ln_bias: float32 [2, 2, 768], P(None, None, ('dp', 'fsdp'))
- grad_w_qkv: float32 [2, 768, 2304], P(None, ('dp', 'fsdp'))
- grad_b_qkv: float32 [2, 1536], P(None, ('dp', 'fsdp'))
- grad_w_proj: float32 [2, 768, 768], P(None, ('dp', 'fsdp'))
- grad_b_proj: float32 [2, 768], P(None, ('dp', 'fsdp'))
- grad_w_fc1: float32 [2, 768, 3072], P(None, ('dp', 'fsdp'))
- grad_b_fc1: float32 [2, 3072], P(None, ('dp', 'fsdp'))
- grad_w_fc2: float32 [2, 3072, 768], P(None, ('dp', 'fsdp'))
- grad_b_fc2: float32 [2, 768], P(None, ('dp', 'fsdp'))
- grad_layer_scale: float32 [2, 2, 768], P(None, None, ('dp', 'fsdp'))
The draws below stay inside these ranges and needn't reach their ends.
Inputs may be any that keep to these rules, and one draw needn't show every extreme that they name: Each row of order holds every patch number of the image once; its first 98 entries are the visible patches and the rest the masked ones.
All inputs are finite; a program needn't handle non-finite values.
Results may differ from the reference program's by a relative error of at most 0.013.
Values may be sent and summed in bfloat16 or wider, within the bound.
A program may use at most 256 MiB of HBM per device.

```python
import math
import jax
import jax.numpy as jnp
from jax import lax

D = 768
HEADS = 12
HEAD_DIM = 64
FF = 3072
VIS = 98
SET = 128
PATCHES = 196
IMAGES = 128
ROWS = 16384


def with_spikes(drawn, rng, source, target, shards_of, factor):
    owner, partner = [(jnp.arange(drawn.shape[dim]) // (drawn.shape[dim] // shards_of)).reshape([-1 if axis == dim else 1 for axis in range(drawn.ndim)]) for dim in (source, target)]
    chosen = jax.random.permutation(rng, shards_of)[partner]
    strong = (owner == chosen) | (owner == (partner + shards_of // 2) % shards_of)
    return jnp.where(strong, factor * drawn, drawn)


def shard_levels(key, dims, shards, least, high):
    level, own = 1.0, jax.random.fold_in(key, 6)
    for dim, blocks in shards:
        steps = jnp.exp(jax.random.uniform(jax.random.fold_in(own, dim), (blocks,), jnp.float32, least / len(shards), high / len(shards)))
        level = level * jnp.repeat(steps, dims[dim] // blocks).reshape([-1 if axis == dim else 1 for axis in range(len(dims))])
    return level


def noise(own_key, dims, deviation, limit, pieces=(), dtype=jnp.bfloat16):
    loudness = shard_levels(own_key, dims, pieces, -0.22, 0.18) if pieces else 1.0
    drawn = jax.random.normal(own_key, dims, jnp.float32) * deviation * loudness
    return jnp.minimum(jnp.maximum(drawn, -limit), limit).astype(dtype)


def bell_draw_with(key, shape, scale, most, shards, heavy, kind=jnp.bfloat16):
    array = scale * jax.random.normal(key, shape, jnp.float32)
    if shards:
        array = array * shard_levels(key, shape, shards, -0.22, 0.18)
    return jnp.clip(with_spikes(array, jax.random.fold_in(key, 3), *heavy), -most, most).astype(kind)


def setup_inputs(seed: int = 0) -> dict:
    key_list = jax.random.split(jax.random.key(seed), 17)
    patches = noise(key_list[0], (ROWS, D), 1.0, 6.0, ((0, 32),))
    order = jax.vmap(lambda own: jax.random.permutation(own, PATCHES))(jax.random.split(key_list[1], IMAGES)).reshape((IMAGES, PATCHES)).astype(jnp.int32)
    grad_latent = bell_draw_with(key_list[2], (ROWS, D), 1.0, 6.0, ((0, 32),), (0, 1, 32, 2.75), jnp.float32)
    grad_out = bell_draw_with(key_list[3], (ROWS, D), 1.0, 6.0, ((0, 32),), (0, 1, 32, 2.75), jnp.float32)
    pos_embed = noise(key_list[4], (PATCHES, D), 1.0, 6.0, ((1, 32),))
    ln_gain = jnp.clip(1.0 + 0.18 * jax.random.normal(key_list[5], (2, 2, D), jnp.float32), 0.099609375, 1.8984375).astype(jnp.bfloat16)
    ln_bias = noise(key_list[6], (2, 2, D), 0.3, 2.0, ((2, 32),))
    w_qkv = noise(key_list[7], (2, D, 3 * D), D ** -0.5, 0.21875, ((1, 32),))
    b_qkv = noise(key_list[8], (2, 2 * D), 0.3, 2.0, ((1, 32),))
    w_proj = noise(key_list[9], (2, D, D), (D // 16) ** -0.5, 0.875, ((1, 32),))
    b_proj = noise(key_list[10], (2, D), 0.3, 2.0, ((1, 32),))
    w_fc1 = noise(key_list[11], (2, D, FF), D ** -0.5, 0.21875, ((1, 32),))
    b_fc1 = noise(key_list[12], (2, FF), 0.3, 2.0, ((1, 32),))
    w_fc2 = noise(key_list[13], (2, FF, D), (FF // 2) ** -0.5, 0.15625, ((1, 32),))
    b_fc2 = noise(key_list[14], (2, D), 0.3, 2.0, ((1, 32),))
    layer_scale = jnp.clip(0.5 + 1.0 * jax.random.uniform(key_list[15], (2, 2, D), jnp.float32) ** shard_levels(key_list[15], (2, 2, D), ((2, 32),), -0.2, 0.2), 0.5, 1.5).astype(jnp.bfloat16)
    return {"patches": patches, "order": order, "grad_latent": grad_latent, "grad_out": grad_out, "pos_embed": pos_embed, "ln_gain": ln_gain, "ln_bias": ln_bias, "w_qkv": w_qkv, "b_qkv": b_qkv, "w_proj": w_proj, "b_proj": b_proj, "w_fc1": w_fc1, "b_fc1": b_fc1, "w_fc2": w_fc2, "b_fc2": b_fc2, "layer_scale": layer_scale}


@jax.custom_vjp
def low(v):
    return lax.optimization_barrier(v.astype(jnp.bfloat16)).astype(jnp.float32)

@jax.custom_vjp
def low_back(v):
    return v

def low_keep(v):
    return (low(v), None)

def low_pass(kept, grad):
    return (grad,)

def back_keep(v):
    return (v, None)

def back_low(kept, grad):
    return (low(grad),)
low.defvjp(low_keep, low_pass)
low_back.defvjp(back_keep, back_low)

def rounded_both(value):
    return low(low_back(value))

def product(left, right):
    return jnp.matmul(left, right, precision=lax.Precision.HIGHEST)

def layer_norm(value, gain, shift):
    center = lax.optimization_barrier(jnp.mean(value, axis=-1, keepdims=True))
    centered = value - center
    spread = lax.optimization_barrier(jnp.mean(centered * centered, axis=-1, keepdims=True))
    return centered * lax.rsqrt(spread + 1e-06) * gain + shift

def attention(query_in, key_in, key_live, weights):
    w_qkv, b_qkv, w_proj, b_proj = weights
    images, query_rows, model = query_in.shape
    key_rows = key_in.shape[1]
    queries = rounded_both(product(query_in, w_qkv[:, :model]) + b_qkv[:model])
    keys = rounded_both(product(key_in, w_qkv[:, model:2 * model]))
    values = rounded_both(product(key_in, w_qkv[:, 2 * model:]) + b_qkv[model:])
    queries = queries.reshape(images, query_rows, HEADS, HEAD_DIM)
    keys = keys.reshape(images, key_rows, HEADS, HEAD_DIM)
    values = values.reshape(images, key_rows, HEADS, HEAD_DIM)
    scores = jnp.einsum('gqhe,gkhe->ghqk', queries, keys, precision=lax.Precision.HIGHEST)
    scores = low_back(scores * (1.0 / math.sqrt(HEAD_DIM)))
    scores = jnp.where(key_live, scores, -1e+30)
    softmax_out = low(jax.nn.softmax(scores, axis=-1))
    mixed = jnp.einsum('ghqk,gkhe->gqhe', softmax_out, values, precision=lax.Precision.HIGHEST)
    mixed = rounded_both(mixed.reshape(images, query_rows, model))
    return low_back(product(mixed, w_proj) + b_proj)

def feed(value, weights):
    gains, shifts, w_fc1, b_fc1, w_fc2, b_fc2 = weights
    inner_in = low(layer_norm(value, gains[1], shifts[1]))
    hidden = low_back(product(inner_in, w_fc1) + b_fc1)
    active = low(jax.nn.gelu(hidden, approximate=True))
    return low_back(product(active, w_fc2) + b_fc2)

def split_block(stacked, block):
    gains, shifts, w_qkv, b_qkv, w_proj, b_proj, w_fc1, b_fc1, w_fc2, b_fc2, scales = tuple((piece[block] for piece in stacked))
    return (gains, shifts, (w_qkv, b_qkv, w_proj, b_proj), (gains, shifts, w_fc1, b_fc1, w_fc2, b_fc2), scales)

def lookup(index, pos_table):
    live = jnp.arange(SET) < VIS
    padded = jnp.pad(index, ((0, 0), (0, SET - VIS)))
    chosen = (padded[:, :, None] == jnp.arange(PATCHES)[None, None, :]) & live[None, :, None]
    return product(chosen.astype(jnp.float32), pos_table)

def forward(patch_rows, pos_table, stacked, order_rows):
    live = jnp.arange(SET) < VIS
    start = patch_rows + lookup(order_rows[:, :VIS], pos_table)
    gains, shifts, attn_weights, feed_weights, scales = split_block(stacked, 0)
    normed = low(layer_norm(start, gains[0], shifts[0]))
    middle = start + scales[0] * attention(normed, normed, live, attn_weights)
    latent_f = middle + scales[1] * feed(middle, feed_weights)
    query_start = lookup(order_rows[:, VIS:], pos_table)
    gains, shifts, attn_weights, feed_weights, scales = split_block(stacked, 1)
    normed_q = low(layer_norm(query_start, gains[0], shifts[0]))
    normed_k = low(layer_norm(jnp.concatenate([latent_f, query_start], axis=1), gains[0], shifts[0]))
    key_live = jnp.concatenate([live, live])
    middle = query_start + scales[0] * attention(normed_q, normed_k, key_live, attn_weights)
    regressed_f = middle + scales[1] * feed(middle, feed_weights)
    return (latent_f, regressed_f)

def reference(patches, order, grad_latent, grad_out, pos_embed, ln_gain, ln_bias, w_qkv, b_qkv, w_proj, b_proj, w_fc1, b_fc1, w_fc2, b_fc2, layer_scale):
    stacked = tuple((piece.astype(jnp.float32) for piece in (ln_gain, ln_bias, w_qkv, b_qkv, w_proj, b_proj, w_fc1, b_fc1, w_fc2, b_fc2, layer_scale)))
    pos_table = pos_embed.astype(jnp.float32)
    group = math.gcd(IMAGES, 32)
    count = IMAGES // group
    live = (jnp.arange(SET) < VIS).astype(jnp.float32)[:, None]
    inputs = (patches.astype(jnp.float32).reshape(count, group, SET, D), order.reshape(count, group, PATCHES), grad_latent.reshape(count, group, SET, D) * live, grad_out.reshape(count, group, SET, D) * live)

    def one_group(carry, item):
        patch_rows, order_rows, cot_latent, cot_out = item
        outputs, pullback = jax.vjp(lambda rows, table, weights: forward(rows, table, weights, order_rows), patch_rows, pos_table, stacked)
        grad_rows, grad_table, grad_weights = pullback((cot_latent, cot_out))
        summed = (carry[0] + grad_table, tuple((total + part for total, part in zip(carry[1], grad_weights))))
        return (summed, (outputs[0], outputs[1], grad_rows))
    initial = (jnp.zeros(pos_table.shape, jnp.float32), tuple((jnp.zeros(piece.shape, jnp.float32) for piece in stacked)))
    (grad_pos, grad_weights), (latent_f, regressed_f, grad_rows) = lax.scan(one_group, initial, inputs)
    latent = latent_f.reshape(ROWS, D).astype(jnp.bfloat16)
    regressed = regressed_f.reshape(ROWS, D).astype(jnp.bfloat16)
    grad_patches = grad_rows.reshape(ROWS, D)
    return (latent, regressed, grad_patches, grad_pos, grad_weights[0], grad_weights[1], grad_weights[2], grad_weights[3], grad_weights[4], grad_weights[5], grad_weights[6], grad_weights[7], grad_weights[8], grad_weights[9], grad_weights[10])
```

```python
import functools
import math

import jax
import jax.numpy as jnp
from jax import lax
from jax.experimental import pallas as pl
from jax.experimental.pallas import tpu as pltpu
from jax.sharding import PartitionSpec as P

HEAD_DIM = 64
VIS = 98
SET = 128
PATCHES = 196


MESH = pl.DeviceIdType.MESH
WIDE = jnp.float32
LOW = jnp.bfloat16


def lanes(start, size):
    return pl.ds(pl.multiple_of(start, 128), size)


class Place:
    def __init__(self, line):
        dp, fsdp = lax.axis_index("dp"), lax.axis_index("fsdp")
        self.line = line
        self.z, self.y = dp // 2, dp % 2
        self.x, self.core = fsdp // 2, fsdp % 2
        z, y, x, core = self.z, self.y, self.x, self.core
        first_y = jnp.where(core == 0, 1 - y, y)
        first_x = jnp.where(core == 0, x, 1 - x)
        second_y = jnp.where(core == 0, y, 1 - y)
        second_x = jnp.where(core == 0, 1 - x, x)
        self.own = 2 * y + x
        self.first = 2 * first_y + first_x
        self.second = 2 * second_y + second_x
        self.across = 2 * (1 - y) + (1 - x)
        self.twin = self.at(z, y, x, 1 - core)
        self.near = self.at(z, first_y, first_x, core)
        self.far = self.at(z, second_y, second_x, core)
        self.above = [
            self.at(lax.rem(z + step, line), y, x, core) for step in range(1, line)
        ]

    def at(self, z, y, x, core):
        return (2 * z + y, 2 * x + core)

    def greet(self):
        barrier = pltpu.get_barrier_semaphore()
        others = [self.twin, self.near, self.far] + self.above
        for other in others:
            pl.semaphore_signal(barrier, inc=1, device_id=other, device_id_type=MESH)
        pl.semaphore_wait(barrier, len(others))


class Copies:
    def __init__(self, send, recv):
        self.send, self.recv, self.used, self.sent = send, recv, 0, []

    def remote(self, source, target, device):
        copy = pltpu.make_async_remote_copy(
            src_ref=source,
            dst_ref=target,
            send_sem=self.send.at[self.used],
            recv_sem=self.recv.at[self.used],
            device_id=device,
            device_id_type=MESH,
        )
        self.used += 1
        copy.start()
        self.sent.append(copy)
        return copy

    def local(self, source, target):
        copy = pltpu.make_async_copy(source, target, self.send.at[self.used])
        self.used += 1
        copy.start()
        return copy

    def drain(self):
        for copy in self.sent:
            copy.wait_send()


def gather_body(line, items, *refs):
    count = len(items)
    shards, fulls = refs[:count], refs[count : 2 * count]
    theirs, stages = refs[2 * count : 3 * count], refs[3 * count : 4 * count]
    send, recv = refs[4 * count :]
    place = Place(line)
    copies = Copies(send, recv)
    place.greet()
    swaps = [copies.remote(shards[i], theirs[i], place.twin) for i in range(count)]
    halves = [shape[2] // 2 for shape in items]
    columns = [lanes(place.core * half, half) for half in halves]

    def stage(i):
        swaps[i].wait_recv()
        rows = items[i][1]
        for which, (low_ref, high_ref) in ((0, (shards[i], theirs[i])), (1, (theirs[i], shards[i]))):
            @pl.when(place.core == which)
            def _():
                part = pl.ds(which * halves[i], halves[i])
                both = jnp.concatenate(
                    [low_ref[:, part].astype(WIDE), high_ref[:, part].astype(WIDE)], axis=0
                )
                stages[i][...] = both.astype(LOW)

    def group(i, which):
        return fulls[i].at[:, which, :, columns[i]]

    def spread(i):
        target = fulls[i].at[place.z, place.own, :, columns[i]]
        own = copies.local(stages[i], target)
        return [own] + [copies.remote(stages[i], target, device) for device in place.above]

    def settle(i, started):
        started[0].wait()
        for copy in started[1:]:
            copy.wait_recv()

    def send_on(i, which, devices):
        return [copies.remote(group(i, which), group(i, which), device) for device in devices]

    ahead = 2
    spreads = {}
    last = []
    for i in range(min(ahead, count)):
        stage(i)
        spreads[i] = spread(i)
    own_sends = {}
    for i in range(count):
        settle(i, spreads[i])
        own_sends[i] = send_on(i, place.own, [place.near, place.far, place.twin])
        if i + ahead < count:
            stage(i + ahead)
            spreads[i + ahead] = spread(i + ahead)
        near, far, twin = own_sends[i]
        near.wait_recv()
        onward = send_on(i, place.first, [place.far, place.twin])
        last.append((far, twin, onward))
        if i >= 1:
            finish = last[i - 1]
            finish[0].wait_recv()
            finish[2][0].wait_recv()
            more = send_on(i - 1, place.second, [place.twin]) + send_on(i - 1, place.across, [place.twin])
            last[i - 1] = [finish[1], finish[2][1]] + more
    finish = last[count - 1]
    finish[0].wait_recv()
    finish[2][0].wait_recv()
    more = send_on(count - 1, place.second, [place.twin]) + send_on(count - 1, place.across, [place.twin])
    last[count - 1] = [finish[1], finish[2][1]] + more
    for group_last in last:
        for copy in group_last:
            copy.wait_recv()
    copies.drain()


def gather_all(shards, line):
    items = [shard.shape for shard in shards]
    items = [(line, 2 * rows, wide) for rows, wide in items]
    total = len(items) * (1 + line + 3 + 2 + 2)
    return pl.pallas_call(
        functools.partial(gather_body, line, items),
        out_shape=[jax.ShapeDtypeStruct((line, 4, rows, wide), LOW) for _, rows, wide in items],
        in_specs=[pl.BlockSpec(memory_space=pltpu.VMEM)] * len(items),
        out_specs=[pl.BlockSpec(memory_space=pl.ANY)] * len(items),
        scratch_shapes=[pltpu.VMEM(shard.shape, LOW) for shard in shards]
        + [pltpu.VMEM((rows, wide // 2), LOW) for _, rows, wide in items]
        + [pltpu.SemaphoreType.DMA((total,)), pltpu.SemaphoreType.DMA((total,))],
        name="gather_all",
        compiler_params=pltpu.CompilerParams(
            collective_id=0, has_side_effects=True, vmem_limit_bytes=24 << 20
        ),
    )(*shards)


def reduce_body(line, items, *refs):
    count = len(items)
    grads, outs = refs[:count], refs[count : 2 * count]
    per = 9
    scratch = refs[2 * count : 2 * count + per * count]
    send, recv = refs[2 * count + per * count :]
    place = Place(line)
    copies = Copies(send, recv)
    place.greet()

    def buffers(i):
        return scratch[per * i : per * (i + 1)]

    def begin(i):
        mine, twins = buffers(i)[:2]
        half = items[i][2] // 2
        away = copies.remote(
            grads[i].at[:, :, :, lanes((1 - place.core) * half, half)], twins, place.twin
        )
        here = copies.local(grads[i].at[:, :, :, lanes(place.core * half, half)], mine)
        return away, here

    def pair_add(i, started):
        mine, twins = buffers(i)[:2]
        started[0].wait_recv()
        started[1].wait()

        def step(k, _):
            a, b = k // 4, k % 4
            mine[a, b] = (mine[a, b].astype(WIDE) + twins[a, b].astype(WIDE)).astype(LOW)
            return 0

        lax.fori_loop(0, line * 4, step, 0)

    def scatter_far(i):
        mine, _, through, direct = buffers(i)[:4]
        return [
            copies.remote(mine.at[:, place.across], through, place.far),
            copies.remote(mine.at[:, place.second], direct, place.far),
        ]

    def scatter_near(i, started):
        mine, _, through, _, joined = buffers(i)[:5]
        started[0].wait_recv()

        def step(k, _):
            through[k] = (through[k].astype(WIDE) + mine[k, place.first].astype(WIDE)).astype(LOW)
            return 0

        lax.fori_loop(0, line, step, 0)
        return copies.remote(through, joined, place.near)

    def scatter_line(i, far, near):
        mine, _, _, direct, joined, owned, arrived = buffers(i)[:7]
        far[1].wait_recv()
        near.wait_recv()

        def step(k, _):
            owned[k] = (
                mine[k, place.own].astype(WIDE) + direct[k].astype(WIDE) + joined[k].astype(WIDE)
            ).astype(LOW)
            return 0

        lax.fori_loop(0, line, step, 0)
        return [
            copies.remote(
                owned.at[lax.rem(place.z + step + 1, line)], arrived.at[step], place.above[step]
            )
            for step in range(line - 1)
        ]

    def swap(i, started):
        owned, arrived, final, other = buffers(i)[5:]
        for copy in started:
            copy.wait_recv()
        total = owned[place.z].astype(WIDE)
        for step in range(line - 1):
            total = total + arrived[step].astype(WIDE)
        final[...] = total
        rows = items[i][1] // 2
        return copies.remote(
            final.at[pl.ds(pl.multiple_of((1 - place.core) * rows, 8), rows)], other, place.twin
        )

    def finish(i, started):
        final, other = buffers(i)[7:]
        rows, half = items[i][1] // 2, items[i][2] // 2
        outs[i][:, lanes(place.core * half, half)] = final[
            pl.ds(pl.multiple_of(place.core * rows, 8), rows)
        ]
        started.wait_recv()
        outs[i][:, lanes((1 - place.core) * half, half)] = other[...]

    begun, far, near, lined, swapped = {}, {}, {}, {}, {}
    for i in range(min(2, count)):
        begun[i] = begin(i)
    for t in range(count + 4):
        if t < count:
            pair_add(t, begun[t])
            far[t] = scatter_far(t)
            if t + 2 < count:
                begun[t + 2] = begin(t + 2)
        if 0 <= t - 1 < count:
            near[t - 1] = scatter_near(t - 1, far[t - 1])
        if 0 <= t - 2 < count:
            lined[t - 2] = scatter_line(t - 2, far[t - 2], near[t - 2])
        if 0 <= t - 3 < count:
            swapped[t - 3] = swap(t - 3, lined[t - 3])
        if 0 <= t - 4 < count:
            finish(t - 4, swapped[t - 4])
    copies.drain()


def reduce_all(grads, line):
    items = [(line, grad.shape[0] // (4 * line), grad.shape[1]) for grad in grads]
    views = [
        grad.reshape(line, 4, rows, wide) for grad, (_, rows, wide) in zip(grads, items)
    ]
    scratch = []
    for _, rows, wide in items:
        half = wide // 2
        scratch += [
            pltpu.VMEM((line, 4, rows, half), LOW),
            pltpu.VMEM((line, 4, rows, half), LOW),
            pltpu.VMEM((line, rows, half), LOW),
            pltpu.VMEM((line, rows, half), LOW),
            pltpu.VMEM((line, rows, half), LOW),
            pltpu.VMEM((line, rows, half), LOW),
            pltpu.VMEM((line - 1, rows, half), LOW),
            pltpu.VMEM((rows, half), WIDE),
            pltpu.VMEM((rows // 2, half), WIDE),
        ]
    total = len(items) * (line + 5)
    return pl.pallas_call(
        functools.partial(reduce_body, line, items),
        out_shape=[jax.ShapeDtypeStruct((rows // 2, wide), WIDE) for _, rows, wide in items],
        in_specs=[pl.BlockSpec(memory_space=pl.ANY)] * len(items),
        out_specs=[pl.BlockSpec(memory_space=pltpu.VMEM)] * len(items),
        scratch_shapes=scratch
        + [pltpu.SemaphoreType.DMA((total,)), pltpu.SemaphoreType.DMA((total,))],
        name="reduce_all",
        compiler_params=pltpu.CompilerParams(
            collective_id=1, has_side_effects=True, vmem_limit_bytes=60 << 20
        ),
    )(*views)


def norm_forward(value, gain, shift):
    center = jnp.mean(value, axis=-1, keepdims=True)
    centered = value - center
    inverse = lax.rsqrt(jnp.mean(centered * centered, axis=-1, keepdims=True) + 1e-06)
    normed = centered * inverse
    return (normed * gain + shift, normed, inverse)


def norm_backward(grad, normed, inverse, gain):
    scaled = grad * gain
    first_mean = jnp.mean(scaled, axis=-1, keepdims=True)
    second_mean = jnp.mean(scaled * normed, axis=-1, keepdims=True)
    back = inverse * (scaled - first_mean - normed * second_mean)
    return (back, jnp.sum(grad * normed, axis=0), jnp.sum(grad, axis=0))


def unpack(pieces):
    gains, shifts, w_qkv, b_qkv, w_proj, b_proj, w_fc1, b_fc1, w_fc2, b_fc2, scales = pieces
    wide = jnp.float32
    return (
        gains.astype(wide),
        shifts.astype(wide),
        w_qkv,
        b_qkv.astype(wide),
        w_proj,
        b_proj.astype(wide),
        w_fc1,
        b_fc1.astype(wide),
        w_fc2,
        b_fc2.astype(wide),
        scales.astype(wide),
    )


def fetch(block, arrays):
    ln_gain, ln_bias, w_qkv, b_qkv, w_proj, b_proj, w_fc1, b_fc1, w_fc2, b_fc2, layer_scale = arrays
    gathered = (
        lax.all_gather(ln_gain[block], ("dp", "fsdp"), axis=1, tiled=True),
        lax.all_gather(ln_bias[block], ("dp", "fsdp"), axis=1, tiled=True),
        lax.all_gather(w_qkv[block], ("dp", "fsdp"), axis=0, tiled=True),
        lax.all_gather(b_qkv[block], ("dp", "fsdp"), axis=0, tiled=True),
        lax.all_gather(w_proj[block], ("dp", "fsdp"), axis=0, tiled=True),
        lax.all_gather(b_proj[block], ("dp", "fsdp"), axis=0, tiled=True),
        lax.all_gather(w_fc1[block], ("dp", "fsdp"), axis=0, tiled=True),
        lax.all_gather(b_fc1[block], ("dp", "fsdp"), axis=0, tiled=True),
        lax.all_gather(w_fc2[block], ("dp", "fsdp"), axis=0, tiled=True),
        lax.all_gather(b_fc2[block], ("dp", "fsdp"), axis=0, tiled=True),
        lax.all_gather(layer_scale[block], ("dp", "fsdp"), axis=1, tiled=True),
    )
    return unpack(gathered)


def column_sum(value):
    return jnp.sum(value.astype(jnp.float32), axis=0)


def outer_rows(left, right):
    return jnp.einsum("rd,rf->df", left, right, preferred_element_type=jnp.float32)


def attend_scores(queries, keys, key_live):
    scores = jnp.einsum("gqhe,gkhe->ghqk", queries, keys, preferred_element_type=jnp.float32) * (
        1.0 / math.sqrt(HEAD_DIM)
    )
    return jnp.where(key_live, scores, -1e30)


def attend_forward(query_in, key_in, images, key_live, weights):
    w_qkv, b_qkv, w_proj, b_proj = (weights[2], weights[3], weights[4], weights[5])
    model = query_in.shape[1]
    heads = model // HEAD_DIM
    queries = (
        jnp.dot(query_in, w_qkv[:, :model], preferred_element_type=jnp.float32) + b_qkv[:model]
    ).astype(jnp.bfloat16)
    paired = jnp.dot(key_in, w_qkv[:, model:], preferred_element_type=jnp.float32)
    keys = paired[:, :model].astype(jnp.bfloat16).reshape(images, -1, heads, HEAD_DIM)
    values = (
        (paired[:, model:] + b_qkv[model:])
        .astype(jnp.bfloat16)
        .reshape(images, -1, heads, HEAD_DIM)
    )
    queries = queries.reshape(images, -1, heads, HEAD_DIM)
    scores = attend_scores(queries, keys, key_live)
    highest_score = jnp.max(scores, axis=-1, keepdims=True)
    weighted = jnp.exp(scores - highest_score)
    summed = jnp.sum(weighted, axis=-1, keepdims=True)
    softmax_out = (weighted / summed).astype(jnp.bfloat16)
    mixed = jnp.einsum("ghqk,gkhe->gqhe", softmax_out, values, preferred_element_type=jnp.float32)
    mixed = mixed.reshape(-1, model).astype(jnp.bfloat16)
    branch = jnp.dot(mixed, w_proj, preferred_element_type=jnp.float32) + b_proj
    return (branch, (queries, keys, values, highest_score + jnp.log(summed), mixed))


def attend_backward(grad_branch, query_in, key_in, key_live, kept, weights):
    w_qkv, w_proj = (weights[2], weights[4])
    queries, keys, values, log_total, mixed = kept
    model = query_in.shape[1]
    grad_low = grad_branch.astype(jnp.bfloat16)
    grad_w_proj = outer_rows(mixed, grad_low)
    grad_b_proj = column_sum(grad_low)
    grad_mixed = (
        jnp.dot(grad_low, w_proj.T, preferred_element_type=jnp.float32)
        .astype(jnp.bfloat16)
        .reshape(queries.shape)
    )
    softmax_out = jnp.exp(attend_scores(queries, keys, key_live) - log_total)
    grad_values = jnp.einsum(
        "ghqk,gqhe->gkhe",
        softmax_out.astype(jnp.bfloat16),
        grad_mixed,
        preferred_element_type=jnp.float32,
    )
    grad_soft = jnp.einsum(
        "gqhe,gkhe->ghqk", grad_mixed, values, preferred_element_type=jnp.float32
    )
    grad_scores = (
        softmax_out * (grad_soft - jnp.sum(grad_soft * softmax_out, axis=-1, keepdims=True))
    ).astype(jnp.bfloat16)
    factor = 1.0 / math.sqrt(HEAD_DIM)
    grad_queries = (
        (
            jnp.einsum("ghqk,gkhe->gqhe", grad_scores, keys, preferred_element_type=jnp.float32)
            * factor
        )
        .astype(jnp.bfloat16)
        .reshape(-1, model)
    )
    grad_keys = (
        (
            jnp.einsum("ghqk,gqhe->gkhe", grad_scores, queries, preferred_element_type=jnp.float32)
            * factor
        )
        .astype(jnp.bfloat16)
        .reshape(-1, model)
    )
    grad_values = grad_values.astype(jnp.bfloat16).reshape(-1, model)
    grad_pairs = jnp.concatenate([grad_keys, grad_values], axis=1)
    grad_w_qkv = jnp.concatenate(
        [outer_rows(query_in, grad_queries), outer_rows(key_in, grad_pairs)], axis=1
    )
    grad_b_qkv = jnp.concatenate([column_sum(grad_queries), column_sum(grad_values)])
    grad_query_in = jnp.dot(grad_queries, w_qkv[:, :model].T, preferred_element_type=jnp.float32)
    grad_key_in = jnp.dot(grad_pairs, w_qkv[:, model:].T, preferred_element_type=jnp.float32)
    return (grad_query_in, grad_key_in, (grad_w_qkv, grad_b_qkv, grad_w_proj, grad_b_proj))


def feed_forward(middle, weights):
    gains, shifts, w_fc1, b_fc1, w_fc2, b_fc2 = (
        weights[0],
        weights[1],
        weights[6],
        weights[7],
        weights[8],
        weights[9],
    )
    normed_out, normed, inverse = norm_forward(middle, gains[1], shifts[1])
    inner_in = normed_out.astype(jnp.bfloat16)
    hidden = jnp.dot(inner_in, w_fc1, preferred_element_type=jnp.float32) + b_fc1
    active = jax.nn.gelu(hidden, approximate=True).astype(jnp.bfloat16)
    branch = jnp.dot(active, w_fc2, preferred_element_type=jnp.float32) + b_fc2
    return (branch, (normed, inverse, inner_in, hidden, active))


def feed_backward(grad_branch, kept, weights):
    gains, w_fc1, w_fc2 = (weights[0], weights[6], weights[8])
    normed, inverse, inner_in, hidden, active = kept
    grad_low = grad_branch.astype(jnp.bfloat16)
    grad_w_fc2 = outer_rows(active, grad_low)
    grad_b_fc2 = column_sum(grad_low)
    grad_active = jnp.dot(grad_low, w_fc2.T, preferred_element_type=jnp.float32)
    gelu_back = jax.vjp(functools.partial(jax.nn.gelu, approximate=True), hidden)[1]
    grad_hidden = gelu_back(grad_active)[0].astype(jnp.bfloat16)
    grad_w_fc1 = outer_rows(inner_in, grad_hidden)
    grad_b_fc1 = column_sum(grad_hidden)
    grad_normed = jnp.dot(grad_hidden, w_fc1.T, preferred_element_type=jnp.float32)
    grad_middle, grad_gain, grad_shift = norm_backward(grad_normed, normed, inverse, gains[1])
    return (grad_middle, grad_gain, grad_shift, (grad_w_fc1, grad_b_fc1, grad_w_fc2, grad_b_fc2))


def pack(pos, ln_gain, ln_bias, scales, b_proj, b_fc2, b_qkv, b_fc1):
    rows = pos.shape[1]

    def turned(array):
        return jnp.moveaxis(array.reshape(-1, array.shape[-1]), 1, 0)

    def folded(array):
        return turned(array.reshape(2, -1, rows))

    columns = [turned(pos), turned(ln_gain), turned(ln_bias), turned(scales)]
    columns += [turned(b_proj), turned(b_fc2), folded(b_qkv), folded(b_fc1)]
    joined = jnp.concatenate([column.astype(LOW) for column in columns], axis=1)
    return jnp.pad(joined, ((0, 0), (0, 256 - joined.shape[1])))


def unpack_rows(extra, patches, devices, fold):
    at = patches
    turned = extra.T
    pos = turned[:patches]
    outs = []
    for _ in range(3):
        outs.append(turned[at : at + 4].reshape(2, 2, -1))
        at += 4
    for _ in range(2):
        outs.append(turned[at : at + 2])
        at += 2
    for pieces in fold:
        part = turned[at : at + 2 * pieces].reshape(2, pieces, devices, -1)
        outs.append(jnp.swapaxes(part, 1, 2).reshape(2, -1))
        at += 2 * pieces
    return [pos] + outs


def repack(pos, ln_gain, ln_bias, scales, b_proj, b_fc2, b_qkv, b_fc1, devices):
    rows = pos.shape[1] // devices

    def turned(array):
        return jnp.moveaxis(array.reshape(-1, array.shape[-1]), 1, 0)

    def folded(array):
        part = jnp.swapaxes(array.reshape(2, devices, -1, rows), 1, 2)
        return turned(part.reshape(-1, devices * rows))

    columns = [turned(pos), turned(ln_gain), turned(ln_bias), turned(scales)]
    columns += [turned(b_proj), turned(b_fc2), folded(b_qkv), folded(b_fc1)]
    joined = jnp.concatenate([column.astype(LOW) for column in columns], axis=1)
    return jnp.pad(joined, ((0, 0), (0, 256 - joined.shape[1])))


def local(
    kernels,
    devices,
    patches,
    order,
    grad_latent,
    grad_out,
    pos_embed,
    ln_gain,
    ln_bias,
    w_qkv,
    b_qkv,
    w_proj,
    b_proj,
    w_fc1,
    b_fc1,
    w_fc2,
    b_fc2,
    layer_scale,
):
    arrays = (
        ln_gain,
        ln_bias,
        w_qkv,
        b_qkv,
        w_proj,
        b_proj,
        w_fc1,
        b_fc1,
        w_fc2,
        b_fc2,
        layer_scale,
    )
    images = order.shape[0]
    model = patches.shape[1]
    highest = lax.Precision.HIGHEST
    live = jnp.arange(SET) < VIS
    live_rows = jnp.tile(live, images).astype(jnp.float32)[:, None]
    patch_slots = jnp.arange(PATCHES)

    def picker(index):
        padded = jnp.pad(index, ((0, 0), (0, SET - VIS)))
        chosen = (padded[:, :, None] == patch_slots[None, None, :]) & live[None, :, None]
        return chosen.astype(jnp.float32).reshape(-1, PATCHES)

    pick_visible = picker(order[:, :VIS])
    pick_masked = picker(order[:, VIS:])
    if kernels:
        line = devices // 8
        extra = pack(pos_embed, ln_gain, ln_bias, layer_scale, b_proj, b_fc2, b_qkv, b_fc1)
        wide = gather_all(
            [extra] + [array[block] for block in (0, 1) for array in (w_qkv, w_proj, w_fc1, w_fc2)],
            line,
        )
        wide = [array.reshape(-1, array.shape[-1]) for array in wide]
        fold = (b_qkv.shape[1] // pos_embed.shape[1], b_fc1.shape[1] // pos_embed.shape[1])
        pos, gains, shifts, scales, proj_b, fc2_b, qkv_b, fc1_b = unpack_rows(
            wide[0], PATCHES, devices, fold
        )
        blocks = []
        for block in (0, 1):
            qkv, proj, fc1, fc2 = wide[1 + 4 * block : 5 + 4 * block]
            blocks.append(
                unpack(
                    (
                        gains[block],
                        shifts[block],
                        qkv,
                        qkv_b[block],
                        proj,
                        proj_b[block],
                        fc1,
                        fc1_b[block],
                        fc2,
                        fc2_b[block],
                        scales[block],
                    )
                )
            )
        pos_table = pos.astype(jnp.float32)
        enc_weights, reg_weights = blocks
    else:
        pos_table = lax.all_gather(pos_embed, ("dp", "fsdp"), axis=1, tiled=True).astype(jnp.float32)
        enc_weights, reg_weights = fetch(0, arrays), fetch(1, arrays)
    start = patches.astype(jnp.float32) + jnp.dot(pick_visible, pos_table, precision=highest)
    enc_out, enc_normed, enc_inverse = norm_forward(start, enc_weights[0][0], enc_weights[1][0])
    enc_attn_in = enc_out.astype(jnp.bfloat16)
    enc_branch, enc_attn_kept = attend_forward(enc_attn_in, enc_attn_in, images, live, enc_weights)
    enc_middle = start + enc_weights[10][0] * enc_branch
    enc_feed, enc_feed_kept = feed_forward(enc_middle, enc_weights)
    latent_f = enc_middle + enc_weights[10][1] * enc_feed
    query_start = jnp.dot(pick_masked, pos_table, precision=highest)
    query_out, query_normed, query_inverse = norm_forward(
        query_start, reg_weights[0][0], reg_weights[1][0]
    )
    latent_out, latent_normed, latent_inverse = norm_forward(
        latent_f, reg_weights[0][0], reg_weights[1][0]
    )
    query_in = query_out.astype(jnp.bfloat16)
    key_in = jnp.concatenate(
        [
            latent_out.astype(jnp.bfloat16).reshape(images, SET, model),
            query_in.reshape(images, SET, model),
        ],
        axis=1,
    ).reshape(-1, model)
    key_live = jnp.concatenate([live, live])
    reg_branch, reg_attn_kept = attend_forward(query_in, key_in, images, key_live, reg_weights)
    reg_middle = query_start + reg_weights[10][0] * reg_branch
    reg_feed, reg_feed_kept = feed_forward(reg_middle, reg_weights)
    regressed_f = reg_middle + reg_weights[10][1] * reg_feed
    reg_back = reg_weights
    grad_final = grad_out * live_rows
    reg_scale_late = jnp.sum(grad_final * reg_feed, axis=0)
    grad_from_feed, reg_gain_late, reg_shift_late, reg_feed_grads = feed_backward(
        reg_back[10][1] * grad_final, reg_feed_kept, reg_back
    )
    grad_reg_middle = grad_final + grad_from_feed
    reg_scale_early = jnp.sum(grad_reg_middle * reg_branch, axis=0)
    grad_query_in, grad_key_in, reg_attn_grads = attend_backward(
        reg_back[10][0] * grad_reg_middle, query_in, key_in, key_live, reg_attn_kept, reg_back
    )
    grad_key_in = grad_key_in.reshape(images, 2 * SET, model)
    grad_query_norm = grad_query_in + grad_key_in[:, SET:].reshape(-1, model)
    grad_latent_norm = grad_key_in[:, :SET].reshape(-1, model)
    back_query, reg_gain_query, reg_shift_query = norm_backward(
        grad_query_norm, query_normed, query_inverse, reg_back[0][0]
    )
    back_latent, reg_gain_key, reg_shift_key = norm_backward(
        grad_latent_norm, latent_normed, latent_inverse, reg_back[0][0]
    )
    grad_query_start = grad_reg_middle + back_query
    reg_grads = (
        (
            jnp.stack([reg_gain_query + reg_gain_key, reg_gain_late]),
            jnp.stack([reg_shift_query + reg_shift_key, reg_shift_late]),
        )
        + reg_attn_grads
        + reg_feed_grads
        + (jnp.stack([reg_scale_early, reg_scale_late]),)
    )
    enc_back = enc_weights
    grad_finish = grad_latent * live_rows + back_latent
    enc_scale_late = jnp.sum(grad_finish * enc_feed, axis=0)
    grad_from_feed, enc_gain_late, enc_shift_late, enc_feed_grads = feed_backward(
        enc_back[10][1] * grad_finish, enc_feed_kept, enc_back
    )
    grad_enc_middle = grad_finish + grad_from_feed
    enc_scale_early = jnp.sum(grad_enc_middle * enc_branch, axis=0)
    grad_as_query, grad_as_key, enc_attn_grads = attend_backward(
        enc_back[10][0] * grad_enc_middle, enc_attn_in, enc_attn_in, live, enc_attn_kept, enc_back
    )
    back_start, enc_gain_early, enc_shift_early = norm_backward(
        grad_as_query + grad_as_key, enc_normed, enc_inverse, enc_back[0][0]
    )
    grad_start = grad_enc_middle + back_start
    grad_table = jnp.dot(pick_visible.T, grad_start, precision=highest) + jnp.dot(
        pick_masked.T, grad_query_start, precision=highest
    )
    enc_grads = (
        (jnp.stack([enc_gain_early, enc_gain_late]), jnp.stack([enc_shift_early, enc_shift_late]))
        + enc_attn_grads
        + enc_feed_grads
        + (jnp.stack([enc_scale_early, enc_scale_late]),)
    )
    if kernels:
        both = [
            jnp.stack([enc_grads[k], reg_grads[k]]) for k in (0, 1, 10, 5, 9, 3, 7)
        ]
        extra = repack(grad_table, *both, devices)
        order_of = [2, 4, 6, 8]
        shards = reduce_all(
            [reg_grads[k].astype(LOW) for k in order_of]
            + [enc_grads[k].astype(LOW) for k in order_of]
            + [extra],
            line,
        )
        pos_shard, gains, shifts, scales, proj_b, fc2_b, qkv_b, fc1_b = unpack_rows(
            shards[8], PATCHES, 1, fold
        )
        qkv, proj, fc1, fc2 = [jnp.stack([shards[4 + k], shards[k]]) for k in range(4)]
        weight_shards = (gains, shifts, qkv, qkv_b, proj, proj_b, fc1, fc1_b, fc2, fc2_b, scales)
    else:
        reg_shards = (
            lax.psum_scatter(reg_grads[0], ("dp", "fsdp"), scatter_dimension=1, tiled=True),
            lax.psum_scatter(reg_grads[1], ("dp", "fsdp"), scatter_dimension=1, tiled=True),
            lax.psum_scatter(reg_grads[2], ("dp", "fsdp"), scatter_dimension=0, tiled=True),
            lax.psum_scatter(reg_grads[3], ("dp", "fsdp"), scatter_dimension=0, tiled=True),
            lax.psum_scatter(reg_grads[4], ("dp", "fsdp"), scatter_dimension=0, tiled=True),
            lax.psum_scatter(reg_grads[5], ("dp", "fsdp"), scatter_dimension=0, tiled=True),
            lax.psum_scatter(reg_grads[6], ("dp", "fsdp"), scatter_dimension=0, tiled=True),
            lax.psum_scatter(reg_grads[7], ("dp", "fsdp"), scatter_dimension=0, tiled=True),
            lax.psum_scatter(reg_grads[8], ("dp", "fsdp"), scatter_dimension=0, tiled=True),
            lax.psum_scatter(reg_grads[9], ("dp", "fsdp"), scatter_dimension=0, tiled=True),
            lax.psum_scatter(reg_grads[10], ("dp", "fsdp"), scatter_dimension=1, tiled=True),
        )
        enc_shards = (
            lax.psum_scatter(grad_table, ("dp", "fsdp"), scatter_dimension=1, tiled=True),
            lax.psum_scatter(enc_grads[0], ("dp", "fsdp"), scatter_dimension=1, tiled=True),
            lax.psum_scatter(enc_grads[1], ("dp", "fsdp"), scatter_dimension=1, tiled=True),
            lax.psum_scatter(enc_grads[2], ("dp", "fsdp"), scatter_dimension=0, tiled=True),
            lax.psum_scatter(enc_grads[3], ("dp", "fsdp"), scatter_dimension=0, tiled=True),
            lax.psum_scatter(enc_grads[4], ("dp", "fsdp"), scatter_dimension=0, tiled=True),
            lax.psum_scatter(enc_grads[5], ("dp", "fsdp"), scatter_dimension=0, tiled=True),
            lax.psum_scatter(enc_grads[6], ("dp", "fsdp"), scatter_dimension=0, tiled=True),
            lax.psum_scatter(enc_grads[7], ("dp", "fsdp"), scatter_dimension=0, tiled=True),
            lax.psum_scatter(enc_grads[8], ("dp", "fsdp"), scatter_dimension=0, tiled=True),
            lax.psum_scatter(enc_grads[9], ("dp", "fsdp"), scatter_dimension=0, tiled=True),
            lax.psum_scatter(enc_grads[10], ("dp", "fsdp"), scatter_dimension=1, tiled=True),
        )
        pos_shard = enc_shards[0]
        weight_shards = tuple(
            (jnp.stack([early, late]) for early, late in zip(enc_shards[1:], reg_shards))
        )
    return (
        latent_f.astype(jnp.bfloat16),
        regressed_f.astype(jnp.bfloat16),
        grad_start,
        pos_shard,
    ) + weight_shards


def solution(mesh):
    in_specs = (
        P(("dp", "fsdp"), None),
        P(("dp", "fsdp"), None),
        P(("dp", "fsdp"), None),
        P(("dp", "fsdp"), None),
        P(None, ("dp", "fsdp")),
        P(None, None, ("dp", "fsdp")),
        P(None, None, ("dp", "fsdp")),
        P(None, ("dp", "fsdp"), None),
        P(None, ("dp", "fsdp")),
        P(None, ("dp", "fsdp"), None),
        P(None, ("dp", "fsdp")),
        P(None, ("dp", "fsdp"), None),
        P(None, ("dp", "fsdp")),
        P(None, ("dp", "fsdp"), None),
        P(None, ("dp", "fsdp")),
        P(None, None, ("dp", "fsdp")),
    )
    out_specs = (
        P(("dp", "fsdp"), None),
        P(("dp", "fsdp"), None),
        P(("dp", "fsdp"), None),
        P(None, ("dp", "fsdp")),
        P(None, None, ("dp", "fsdp")),
        P(None, None, ("dp", "fsdp")),
        P(None, ("dp", "fsdp"), None),
        P(None, ("dp", "fsdp")),
        P(None, ("dp", "fsdp"), None),
        P(None, ("dp", "fsdp")),
        P(None, ("dp", "fsdp"), None),
        P(None, ("dp", "fsdp")),
        P(None, ("dp", "fsdp"), None),
        P(None, ("dp", "fsdp")),
        P(None, None, ("dp", "fsdp")),
    )
    devices = mesh.shape["dp"] * mesh.shape["fsdp"]

    def step(*args):
        rows = args[7].shape[1]
        kernels = mesh.shape["fsdp"] == 4 and rows // (devices // 2) % 16 == 0
        run = jax.shard_map(
            functools.partial(local, kernels, devices),
            mesh=mesh,
            in_specs=in_specs,
            out_specs=out_specs,
            check_vma=False,
        )
        return run(*args)

    return step
```

```python
import functools
import math

import jax
import jax.numpy as jnp
import numpy as np
from jax import lax
from jax.experimental import pallas as pl
from jax.experimental.pallas import tpu as pltpu
from jax.sharding import PartitionSpec as P

HEAD_DIM = 64
VIS = 98
SET = 128
PATCHES = 196

MESH = pl.DeviceIdType.MESH
WIDE = jnp.float32
LOW = jnp.bfloat16


def lanes(start, size):
    return pl.ds(pl.multiple_of(start, 128), size)


class Place:
    def __init__(self, line):
        dp, fsdp = lax.axis_index("dp"), lax.axis_index("fsdp")
        self.line = line
        self.z, self.y = dp // 2, dp % 2
        self.x, self.core = fsdp // 2, fsdp % 2
        z, y, x, core = self.z, self.y, self.x, self.core
        first_y = jnp.where(core == 0, 1 - y, y)
        first_x = jnp.where(core == 0, x, 1 - x)
        second_y = jnp.where(core == 0, y, 1 - y)
        second_x = jnp.where(core == 0, 1 - x, x)
        self.own = 2 * y + x
        self.first = 2 * first_y + first_x
        self.second = 2 * second_y + second_x
        self.across = 2 * (1 - y) + (1 - x)
        self.twin = self.at(z, y, x, 1 - core)
        self.near = self.at(z, first_y, first_x, core)
        self.far = self.at(z, second_y, second_x, core)
        self.above = [
            self.at(lax.rem(z + step, line), y, x, core) for step in range(1, line)
        ]

    def at(self, z, y, x, core):
        return (2 * z + y, 2 * x + core)

    def greet(self):
        barrier = pltpu.get_barrier_semaphore()
        others = [self.twin, self.near, self.far] + self.above
        for other in others:
            pl.semaphore_signal(barrier, inc=1, device_id=other, device_id_type=MESH)
        pl.semaphore_wait(barrier, len(others))


class Copies:
    def __init__(self, send, recv):
        self.send, self.recv, self.used, self.sent = send, recv, 0, []

    def remote(self, source, target, device):
        copy = pltpu.make_async_remote_copy(
            src_ref=source,
            dst_ref=target,
            send_sem=self.send.at[self.used],
            recv_sem=self.recv.at[self.used],
            device_id=device,
            device_id_type=MESH,
        )
        self.used += 1
        copy.start()
        self.sent.append(copy)
        return copy

    def local(self, source, target):
        copy = pltpu.make_async_copy(source, target, self.send.at[self.used])
        self.used += 1
        copy.start()
        return copy

    def drain(self):
        for copy in self.sent:
            copy.wait_send()


def gather_steps(line, items, sources, shards, theirs, fulls, stages, send, recv, bring):
    count = len(items)
    place = Place(line)
    copies = Copies(send, recv)
    place.greet()
    swaps = [copies.remote(source, their, place.twin) for source, their in zip(sources, theirs)]
    arrived = set()
    sizes = [wide // 2 for _, _, _, wide in items]
    columns = [lanes(item[2] + place.core * half, half) for item, half in zip(items, sizes)]

    def stage(i):
        array, rows, first, _ = items[i]
        own, their = shards[array](), theirs[array]
        if array not in arrived:
            arrived.add(array)
            swaps[array].wait_recv()
        for which, (low_ref, high_ref) in ((0, (own, their)), (1, (their, own))):

            @pl.when(place.core == which)
            def _():
                part = pl.ds(first + which * sizes[i], sizes[i])
                both = jnp.concatenate(
                    [low_ref[:, part].astype(WIDE), high_ref[:, part].astype(WIDE)], axis=0
                )
                stages[i][...] = both.astype(LOW)

    def group(i, which):
        return fulls[items[i][0]].at[:, which, :, columns[i]]

    def spread(i):
        target = fulls[items[i][0]].at[place.z, place.own, :, columns[i]]
        own = copies.local(stages[i], target)
        return [own] + [copies.remote(stages[i], target, device) for device in place.above]

    def send_on(i, which, devices):
        return [copies.remote(group(i, which), group(i, which), device) for device in devices]

    def share(i, far, twin, onward):
        far.wait_recv()
        onward[0].wait_recv()
        more = send_on(i, place.second, [place.twin]) + send_on(i, place.across, [place.twin])
        return [twin, onward[1]] + more

    def complete(i, started):
        for copy in started:
            copy.wait_recv()
        bring(i)

    ahead = 4
    start = 9.0
    spreads, last, shared = {}, {}, {}
    for i in range(min(ahead, count)):
        stage(i)
        spreads[i] = spread(i)
    for i in range(count):
        unit = line * items[i][1] * sizes[i] * 2 / LINK
        yield start
        spreads[i][0].wait()
        for copy in spreads[i][1:]:
            copy.wait_recv()
        near, far, twin = send_on(i, place.own, [place.near, place.far, place.twin])
        if i + ahead < count:
            stage(i + ahead)
            spreads[i + ahead] = spread(i + ahead)
        if i >= 2:
            complete(i - 2, shared[i - 2])
        yield start + 2.4 * unit
        near.wait_recv()
        last[i] = (far, twin, send_on(i, place.first, [place.far, place.twin]))
        if i >= 1:
            yield start + 2.6 * unit
            shared[i - 1] = share(i - 1, *last[i - 1])
        start += 3 * unit
    yield start
    if count >= 2:
        complete(count - 2, shared[count - 2])
    complete(count - 1, share(count - 1, *last[count - 1]))
    yield start
    copies.drain()


class Names:
    def __getattr__(self, word):
        return word


N = Names()
LINK = 92e3
TWIN = 4e5


class Pace:
    def __init__(self, steps):
        self.steps, self.now = steps, 0.0
        self.due = next(steps)

    def advance(self):
        self.now = max(self.now, self.due)
        self.due = next(self.steps, None)

    def spend(self, time):
        self.now += time
        while self.due is not None and self.due <= self.now:
            self.advance()

    def until(self, reached):
        while not reached():
            self.advance()

    def finish(self):
        while self.due is not None:
            self.advance()
TILE = 256
ROOT = math.sqrt(2.0 / math.pi)
CUBE = 0.044715


def dot_nn(left, right):
    return lax.dot_general(left, right, (((1,), (0,)), ((), ())), preferred_element_type=WIDE)


def dot_nt(left, right):
    return lax.dot_general(left, right, (((1,), (1,)), ((), ())), preferred_element_type=WIDE)


def dot_tn(left, right):
    return lax.dot_general(left, right, (((0,), (0,)), ((), ())), preferred_element_type=WIDE)


def each(count, step, first=0, unroll=1):
    def run(k, carry):
        step(k)
        return carry

    lax.fori_loop(first, first + count, run, 0, unroll=unroll)


def row_blocks(total, block, step):
    each(total // block, lambda k: step(pl.ds(pl.multiple_of(k * block, block), block)), unroll=2)


def row(ref, k):
    return ref[pl.ds(k, 1), :]


def flat(value):
    return value.reshape(-1, value.shape[-1])


def add_rows(ref, k, value):
    ref[pl.ds(k, 1), :] += jnp.sum(value.astype(WIDE), axis=0, keepdims=True)


def live_rows(block, wide):
    return lax.broadcasted_iota(jnp.int32, (block, wide), 0) % SET < VIS


def selection(slots, wide):
    rows = lax.broadcasted_iota(jnp.int32, (32, wide), 0)
    return (lax.broadcasted_iota(jnp.int32, (32, wide), 1) == rows + slots).astype(LOW)


def picks(index, wide):
    return (index == lax.broadcasted_iota(jnp.int32, (index.shape[0], wide), 1)).astype(LOW)


def fold_tables(model, rows, parts):
    entry = np.arange(model)
    source = rows * (entry // (parts * rows)) + entry % rows
    spots = (np.arange(model // parts)[:, None] == source[None, :]).astype(np.float32)
    column = entry % (parts * rows) // rows
    which = (np.arange(8)[:, None] == column[None, :]).astype(np.float32)
    return jnp.asarray(spots, LOW), jnp.asarray(which, WIDE)


class Buffers:
    def __init__(self, refs, sems):
        self.refs, self.sems, self.used = refs, sems, 0
        self.loading, self.saving = {}, []

    def __getitem__(self, name):
        if name in self.loading:
            self.loading.pop(name).wait()
        return self.refs[name]

    def copy(self, source, target):
        copy = pltpu.make_async_copy(source, target, self.sems.at[self.used])
        self.used += 1
        copy.start()
        return copy

    def load(self, name, source, target=None):
        self.loading[name] = self.copy(source, self.refs[name] if target is None else target)

    def wait(self, *names):
        for name in names:
            if name in self.loading:
                self.loading.pop(name).wait()

    def save(self, name, target):
        self.saving.append((name, self.copy(self.refs[name], target)))

    def saved(self, name):
        self.settle([entry for entry in self.saving if entry[0] == name])

    def settle(self, entries):
        for entry in entries:
            if any(entry is other for other in self.saving):
                entry[1].wait()
        self.saving = [other for other in self.saving if not any(other is entry for entry in entries)]

    def drain(self):
        for name in list(self.loading):
            self.loading.pop(name).wait()
        for _, copy in self.saving:
            copy.wait()


def call(body, ins, small, outs, scratch, sems, extra, name, collective, vmem):
    names = list(ins) + list(small) + list(outs) + list(scratch)

    def kernel(*refs):
        named = dict(zip(names, refs[: len(names)]))
        body(Buffers(named, refs[len(names)]), *refs[len(names) + 1 :])

    anywhere = pl.BlockSpec(memory_space=pl.ANY)
    results = pl.pallas_call(
        kernel,
        out_shape=list(outs.values()),
        in_specs=[anywhere] * len(ins) + [pl.BlockSpec(memory_space=pltpu.VMEM)] * len(small),
        out_specs=[anywhere] * len(outs),
        scratch_shapes=[pltpu.VMEM(*shape) for shape in scratch.values()]
        + [pltpu.SemaphoreType.DMA((sems,))]
        + extra,
        name=name,
        compiler_params=pltpu.CompilerParams(
            collective_id=collective, has_side_effects=True, vmem_limit_bytes=vmem
        ),
    )(*ins.values(), *small.values())
    return dict(zip(outs, results))


def norm_block(value, gain, shift):
    centered = value - jnp.mean(value, axis=-1, keepdims=True)
    inverse = lax.rsqrt(jnp.mean(centered * centered, axis=-1, keepdims=True) + 1e-06)
    normed = centered * inverse
    return normed * gain + shift, normed, inverse


def norm_back(value, grad, gain, sums, gain_row, shift_row):
    _, normed, inverse = norm_block(value, gain, 0.0)
    add_rows(sums, gain_row, grad * normed)
    add_rows(sums, shift_row, grad)
    scaled = grad * gain
    first = jnp.mean(scaled, axis=-1, keepdims=True)
    second = jnp.mean(scaled * normed, axis=-1, keepdims=True)
    return inverse * (scaled - first - normed * second)


def halves(value):
    low = lax.broadcasted_iota(jnp.int32, value.shape, 1) < HEAD_DIM
    zero = jnp.zeros_like(value)
    return jnp.concatenate([jnp.where(low, value, zero), jnp.where(low, zero, value)], axis=0)


def rejoin(value):
    rows = value.shape[0] // 2
    low = lax.broadcasted_iota(jnp.int32, (rows, value.shape[1]), 1) < HEAD_DIM
    return jnp.where(low, value[:rows], value[rows:])


def spot(k, pairs):
    return pl.ds(pl.multiple_of(k // pairs * SET, SET), SET), lanes(k % pairs * 128, 128)


def stacked(refs, at):
    parts = [ref[at[0], at[1]] for ref in refs]
    return parts[0] if len(parts) == 1 else jnp.concatenate(parts, axis=0)


def soft(keys, queries):
    scores = dot_nt(keys, queries) * (1.0 / math.sqrt(HEAD_DIM))
    scores = jnp.where(live_rows(*scores.shape), scores, -1e30)
    weighted = jnp.exp(scores - jnp.max(scores, axis=0, keepdims=True))
    return weighted / jnp.sum(weighted, axis=0, keepdims=True)


def in_pieces(count, piece, step, between):
    for first in range(0, count, piece):
        each(piece, step, first, piece)
        between()


def attend(queries, keys, values, mixed, between):
    pairs = queries.shape[1] // 128

    def step(k):
        at = spot(k, pairs)
        weights = soft(stacked(keys, at), halves(queries[at[0], at[1]])).astype(LOW)
        mixed[at[0], at[1]] = rejoin(dot_tn(weights, stacked(values, at))).astype(LOW)

    in_pieces(queries.shape[0] // SET * pairs, 4, step, between)


def attend_back(grad_mixed, queries, keys, values, grad_queries, grad_keys, grad_values, between):
    pairs = queries.shape[1] // 128
    factor = 1.0 / math.sqrt(HEAD_DIM)

    def step(k):
        at = spot(k, pairs)
        key, value = stacked(keys, at), stacked(values, at)
        query, grad = halves(queries[at[0], at[1]]), halves(grad_mixed[at[0], at[1]])
        weights = soft(key, query)
        back_value = dot_nn(weights.astype(LOW), grad).astype(LOW)
        grad_soft = dot_nt(value, grad)
        inner = jnp.sum(grad_soft * weights, axis=0, keepdims=True)
        grad_scores = (weights * (grad_soft - inner)).astype(LOW)
        back_key = (dot_nn(grad_scores, query) * factor).astype(LOW)
        grad_queries[at[0], at[1]] = (rejoin(dot_tn(grad_scores, key)) * factor).astype(LOW)
        for which in range(len(keys)):
            part = slice(which * SET, (which + 1) * SET)
            grad_keys[which][at[0], at[1]] = back_key[part]
            grad_values[which][at[0], at[1]] = back_value[part]

    in_pieces(queries.shape[0] // SET * pairs, 4, step, between)


def project(source, weight, start, bias, target):
    def step(k):
        part = lanes(k * TILE, TILE)
        value = dot_nn(source[...], flat(weight[:, :, :, lanes(start + k * TILE, TILE)]))
        if bias is not None:
            value = value + bias[:, part]
        target[:, part] = value.astype(LOW)

    each(target.shape[1] // TILE, step, unroll=3)


def residual(source, weight, bias, scale, before, after, branch, first, count):
    def step(k):
        part = lanes(k * TILE, TILE)
        value = dot_nn(source[...], flat(weight[:, :, :, part])) + bias[:, part]
        branch[:, part] = value.astype(LOW)
        after[:, part] = before[:, part] + scale[:, part] * value

    each(count, step, first, count)


def rise(source, weight, bias, active, slope, first, count):
    per = source.shape[1] // TILE

    def step(k):
        part = lanes(k * TILE, TILE)
        own = bias[pl.ds(k // per, 1), lanes(k % per * TILE, TILE)]
        value = dot_nn(source[...], flat(weight[:, :, :, part])) + own
        square = value * value
        curve = jnp.tanh(value * (ROOT + (ROOT * CUBE) * square))
        half = 0.5 + 0.5 * curve
        active[:, part] = (value * half).astype(LOW)
        bend = value * (half - half * curve) * (ROOT + (3.0 * ROOT * CUBE) * square)
        slope[:, part] = (half + bend).astype(LOW)

    each(count, step, first, count)


def small_vectors(b, parts):
    extra, vec = b[N.extra], b[N.vec]
    pick = selection(PATCHES, extra.shape[1])
    vec[...] = dot_nt(pick, extra[...])
    at = 16
    for count, spots, which in ((parts[0], b[N.spots_q], b[N.which_q]), (parts[1], b[N.spots_f], b[N.which_f])):
        rows = spots.shape[0]
        found = []
        for chunk in range(count):
            held = dot_nt(pick, extra[pl.ds(chunk * rows, rows), :]).astype(LOW)
            found.append(dot_nn(held, spots[...]))
        for block in range(2):
            for chunk in range(count):
                base = at + block * count
                total = sum(
                    found[chunk][base + j : base + j + 1] * which[j : j + 1, :] for j in range(count)
                )
                vec[base + chunk : base + chunk + 1, :] = total
        at += 2 * count


def forward_compute(b, need, spend, keep, release):
    rows, model = b[N.start].shape
    need(N.extra, 0, 0)
    b[N.extra][...] = flat(b[N.extra4][...])
    small_vectors(b, (2, 4))
    vec, extra = b[N.vec], b[N.extra]
    keep(N.vec)
    spend(2)

    def vector(k):
        return vec.at[pl.ds(k, 1)]

    def open_rows(r):
        wide = extra.shape[1]
        start = b[N.patches][r, :].astype(WIDE) + dot_nt(picks(b[N.vis][r, :], wide), extra[...])
        b[N.start][r, :] = start
        b[N.a0][r, :] = norm_block(start, row(vec, 0), row(vec, 4))[0].astype(LOW)
        query = dot_nt(picks(b[N.hid][r, :], wide), extra[...])
        b[N.query][r, :] = query
        b[N.aq][r, :] = norm_block(query, row(vec, 2), row(vec, 6))[0].astype(LOW)

    b[N.patches]
    row_blocks(rows, 64, open_rows)
    for name in (N.start, N.a0, N.query, N.aq):
        keep(name)
    spend(4)

    def norm_into(source, target, gain, shift):
        def step(r):
            b[target][r, :] = norm_block(b[source][r, :], row(vec, gain), row(vec, shift))[0].astype(LOW)

        row_blocks(rows, 64, step)
        keep(target)
        spend(1)

    def low_into(source, target):
        def step(r):
            b[target][r, :] = b[source][r, :].astype(LOW)

        row_blocks(rows, 64, step)
        keep(target)

    def attention(block, sources, keys, values, before, after):
        query, mixed, branch = N.q + str(block), N.mix + str(block), N.br + str(block)
        for part, bias in enumerate((16 + 2 * block, None, 17 + 2 * block)):
            need(N.qkv, block, part)
            targets = ([query], keys, values)[part]
            for source, target in zip(sources[part], targets):
                shift = None if bias is None else vector(bias)
                project(b[source], b[N.w_qkv], part * model, shift, b[target])
                keep(target)
                spend(1)
        release(N.qkv)
        attend(
            b[query], [b[name] for name in keys], [b[name] for name in values], b[mixed],
            lambda: spend(1.5),
        )
        keep(mixed)
        need(N.proj, block, 0)
        residual(
            b[mixed], b[N.w_proj], vector(12 + block), vector(8 + 2 * block), b[before], b[after], b[branch],
            0, model // TILE,
        )
        release(N.proj)
        keep(branch)
        keep(after)
        spend(1.2)

    def feed(block, before, after, inner):
        branch = N.fd + str(block)
        norm_into(before, inner, 2 * block + 1, 4 + 2 * block + 1)
        b.saved(N.active)
        b.saved(N.slope)
        hidden = b[N.active].shape[1]
        for piece in range(hidden // model):
            need(N.fc1, block, piece)
            rise(
                b[inner], b[N.w_fc1], vec.at[pl.ds(20 + 4 * block, 4)], b[N.active], b[N.slope],
                piece * (model // TILE), model // TILE,
            )
            spend(2.2)
        release(N.fc1)
        keep(N.active, block)
        keep(N.slope, block)
        for piece in range(model // TILE):
            need(N.fc2, block, piece)
            residual(
                b[N.active], b[N.w_fc2], vector(14 + block), vector(8 + 2 * block + 1), b[before], b[after],
                b[branch], piece, 1,
            )
            spend(1.3)
        release(N.fc2)
        keep(branch)

    attention(0, ([N.a0], [N.a0], [N.a0]), [N.k0], [N.v0], N.start, N.mid0)
    feed(0, N.mid0, N.lat, N.a20)
    keep(N.lat)
    low_into(N.lat, N.latent)
    norm_into(N.lat, N.ak, 2, 6)
    both = [N.ak, N.aq]
    attention(1, ([N.aq], both, both), [N.k1, N.k2], [N.v1, N.v2], N.query, N.mid1)
    feed(1, N.mid1, N.reg, N.a21)
    low_into(N.reg, N.regressed)


KEPT_WIDE = (N.start, N.query, N.mid0, N.lat, N.mid1)
KEPT_LOW = (
    N.a0, N.aq, N.a20, N.ak, N.a21, N.q0, N.k0, N.v0, N.mix0, N.br0, N.fd0,
    N.q1, N.k1, N.v1, N.k2, N.v2, N.mix1, N.br1, N.fd1, N.latent, N.regressed,
)


def shape_of(*args):
    return jax.ShapeDtypeStruct(*args)


def cut(shapes):
    model = shapes[N.proj][1]
    pieces = []
    for kind, wide in ((N.qkv, model), (N.proj, model), (N.fc1, model), (N.fc2, TILE)):
        pieces += [(kind, k, k * wide, wide) for k in range(shapes[kind][1] // wide)]
    return pieces


def forward(patches, vis, hid, extra_shard, weights, line, tables):
    rows, model = patches.shape
    kinds = (N.qkv, N.proj, N.fc1, N.fc2)
    shapes = {kind: (2 * weight.shape[1], weight.shape[2]) for kind, weight in zip(kinds, weights)}
    shapes[N.extra] = (2 * extra_shard.shape[0], extra_shard.shape[1])
    hidden = shapes[N.fc1][1]
    whole = {kind: (line, 4) + shape for kind, shape in shapes.items()}
    arrays = [(N.extra, 0)] + [(kind, block) for block in (0, 1) for kind in kinds]
    names = [kind + str(block) for kind, block in arrays]
    items = [(0, N.extra, 0, 0, 0, shapes[N.extra][1])]
    for block in (0, 1):
        for kind, piece, first, wide in cut(shapes):
            items.append((arrays.index((kind, block)), kind, block, piece, first, wide))
    outs = {name: shape_of(whole[kind], LOW) for name, (kind, _) in zip(names, arrays)}
    outs[N.vec_out] = shape_of((32, model), WIDE)
    for name in KEPT_WIDE:
        outs[name + N._out] = shape_of((rows, model), WIDE)
    for name in KEPT_LOW:
        outs[name + N._out] = shape_of((rows, model), LOW)
    for block in (0, 1):
        for name in (N.active, N.slope):
            outs[name + str(block) + N._out] = shape_of((rows, hidden), LOW)
    scratch = {name: ((rows, model), WIDE) for name in KEPT_WIDE + (N.reg,)}
    scratch.update({name: ((rows, model), LOW) for name in KEPT_LOW + (N.patches,)})
    scratch[N.active] = scratch[N.slope] = ((rows, hidden), LOW)
    scratch[N.vec] = ((32, model), WIDE)
    scratch[N.extra4] = (whole[N.extra], LOW)
    scratch[N.extra] = ((model, shapes[N.extra][1]), LOW)
    for kind in kinds:
        scratch[N.w_ + kind] = (whole[kind], LOW)
    for name, (kind, _) in zip(names, arrays):
        held = (shapes[kind][0] // 2, shapes[kind][1])
        scratch[N.own_ + name] = scratch[N.their_ + name] = (held, LOW)
    for i, (a, kind, _, _, _, wide) in enumerate(items):
        scratch[N.stage + str(i)] = ((shapes[kind][0], wide // 2), LOW)
    ins = {N.patches_in: patches, N.extra_in: extra_shard}
    ins.update({kind + N._in: weight for kind, weight in zip(kinds, weights)})
    small = {N.vis: vis, N.hid: hid}
    small.update(dict(zip((N.spots_q, N.which_q, N.spots_f, N.which_f), tables)))
    pairs = len(arrays) + len(items) * (line + 8)
    extra = [pltpu.SemaphoreType.DMA((pairs,)), pltpu.SemaphoreType.DMA((pairs,))]

    def body(b, send, recv):
        sources = [b[N.extra_in]] + [b[kind + N._in].at[block] for kind, block in arrays[1:]]
        b.load(N.own_ + names[0], sources[0])
        b.load(N.patches, b[N.patches_in])
        for name, source in list(zip(names, sources))[1:]:
            b.load(N.own_ + name, source)
        free, held, loaded = {(N.extra, 0)} | {(kind, 0) for kind in kinds}, [], {}

        def bring(i):
            a, kind, block, piece, first, wide = items[i]
            if (kind, block) not in free:
                held.append(i)
                return
            part = (slice(None),) * 3 + (pl.ds(first, wide),)
            target = b.refs[N.extra4 if kind == N.extra else N.w_ + kind].at[part]
            b.load(N.item + str(i), b[names[a]].at[part], target)
            loaded[(kind, block, piece)] = N.item + str(i)

        shards = [lambda name=name: b[N.own_ + name] for name in names]
        steps = gather_steps(
            line, [(a, shapes[kind][0], first, wide) for a, kind, _, _, first, wide in items], sources, shards,
            [b[N.their_ + name] for name in names], [b[name] for name in names],
            [b[N.stage + str(i)] for i in range(len(items))], send, recv, bring,
        )
        pace = Pace(steps)

        def need(kind, block, piece):
            pace.until(lambda: (kind, block, piece) in loaded)
            b.wait(loaded[(kind, block, piece)])

        def release(kind):
            free.add((kind, 1))
            for i in [i for i in held if items[i][1] == kind]:
                held.remove(i)
                bring(i)

        def keep(name, block=None):
            b.save(name, b[name + ("" if block is None else str(block)) + N._out])

        forward_compute(b, need, pace.spend, keep, release)
        pace.finish()
        b.drain()

    return call(body, ins, small, outs, scratch, 128, extra, N.forward, 0, 63 << 20)


class Reducer:
    def __init__(self, line, items, slots, grads, outs, shared, single, send, recv, credit):
        self.line, self.items, self.slots = line, items, slots
        self.grads, self.outs, self.shared, self.single = grads, outs, shared, single
        self.credit = credit
        self.place = Place(line)
        self.copies = Copies(send, recv)
        self.place.greet()
        self.ready, self.begun, self.state = set(), {}, {}
        self.next, self.due = [0] * 5, {}
        self.now = self.link_free = self.line_free = 0.0
        self.sends = {i: [] for i in range(len(items))}
        self.steps = [self.pair, self.near, self.along, self.swap, self.finish]

    def remote(self, i, source, target, device):
        copy = self.copies.remote(source, target, device)
        self.sends[i].append(copy)
        return copy

    def unit(self, i):
        return self.line * self.items[i][0] * self.half(i) * 2

    def half(self, i):
        return self.items[i][2] // 2

    def columns(self, i, core):
        return lanes(self.items[i][1] + core * self.half(i), self.half(i))

    def earlier(self, i):
        return [j for j in range(i) if self.slots[j] == self.slots[i]]

    def later(self, i):
        return [j for j in range(i + 1, len(self.items)) if self.slots[j] == self.slots[i]]

    def buffers(self, i):
        mine, twins, owned, final, other = self.shared[self.slots[i]]
        through, direct, joined, arrived = self.single[i]
        return mine, twins, through, direct, joined, owned, arrived, final, other

    def begin(self, i):
        place = self.place
        mine, twins = self.buffers(i)[:2]
        if self.earlier(i):
            pl.semaphore_wait(self.credit.at[self.slots[i]], 1)
        away = self.remote(
            i, self.grads[i].at[:, :, :, self.columns(i, 1 - place.core)], twins, place.twin
        )
        here = self.copies.local(self.grads[i].at[:, :, :, self.columns(i, place.core)], mine)
        self.begun[i] = (away, here)
        self.due[0, i] = self.now + 2.0 + 4 * self.unit(i) / TWIN

    def begin_some(self):
        i = len(self.begun)
        while i < len(self.items) and i in self.ready and i <= self.next[0] + 2:
            if any(j >= self.next[4] for j in self.earlier(i)):
                return
            self.begin(i)
            i += 1

    def pair(self, i):
        place = self.place
        mine, twins, through, direct = self.buffers(i)[:4]
        away, here = self.begun[i]
        away.wait_recv()
        here.wait()

        def step(k):
            a, c = k // 4, k % 4
            mine[a, c] = (mine[a, c].astype(WIDE) + twins[a, c].astype(WIDE)).astype(LOW)

        each(self.line * 4, step, unroll=2)
        self.state[i] = [
            self.remote(i, mine.at[:, place.across], through, place.far),
            self.remote(i, mine.at[:, place.second], direct, place.far),
        ]
        unit = self.unit(i) / LINK
        start = max(self.now, self.link_free)
        self.link_free = start + 3 * unit
        self.due[1, i] = start + 1.0 + 1.6 * unit
        self.now += 0.5 + self.unit(i) / 1e6

    def near(self, i):
        place = self.place
        mine, _, through, _, joined = self.buffers(i)[:5]
        self.state[i][0].wait_recv()

        def step(k):
            through[k] = (through[k].astype(WIDE) + mine[k, place.first].astype(WIDE)).astype(LOW)

        each(self.line, step)
        self.state[i].append(self.remote(i, through, joined, place.near))
        self.due[2, i] = self.now + 1.0 + 1.6 * self.unit(i) / LINK
        self.now += 0.3

    def along(self, i):
        place, line = self.place, self.line
        mine, _, _, direct, joined, owned, arrived = self.buffers(i)[:7]
        self.state[i][1].wait_recv()
        self.state[i][2].wait_recv()

        def step(k):
            total = mine[k, place.own].astype(WIDE) + direct[k].astype(WIDE) + joined[k].astype(WIDE)
            owned[k] = total.astype(LOW)

        each(line, step)
        self.state[i] = [
            self.remote(
                i, owned.at[lax.rem(place.z + k + 1, line)], arrived.at[k], place.above[k]
            )
            for k in range(line - 1)
        ]
        start = max(self.now, self.line_free)
        self.line_free = start + 2 * self.unit(i) / LINK
        self.due[3, i] = self.line_free + 1.0
        self.now += 0.3

    def swap(self, i):
        place, rows = self.place, self.items[i][0] // 2
        owned, arrived, final, other = self.buffers(i)[5:]
        for copy in self.state[i]:
            copy.wait_recv()
        total = owned[place.z].astype(WIDE)
        for k in range(self.line - 1):
            total = total + arrived[k].astype(WIDE)
        final[...] = total
        away = pl.ds(pl.multiple_of((1 - place.core) * rows, 8), rows)
        self.state[i] = [self.remote(i, final.at[away], other, place.twin)]
        self.due[4, i] = self.now + 2.0
        self.now += 0.2

    def finish(self, i):
        place = self.place
        final, other = self.buffers(i)[7:]
        rows = self.items[i][0] // 2
        own = pl.ds(pl.multiple_of(place.core * rows, 8), rows)
        self.outs[i][:, self.columns(i, place.core)] = final[own]
        self.state[i][0].wait_recv()
        self.outs[i][:, self.columns(i, 1 - place.core)] = other[...]
        for copy in self.sends[i]:
            copy.wait_send()
        if self.later(i):
            pl.semaphore_signal(
                self.credit.at[self.slots[i]], inc=1, device_id=place.twin, device_id_type=MESH
            )

    def able(self):
        found = []
        for stage in range(5):
            i = self.next[stage]
            if (i in self.begun) if stage == 0 else (i < self.next[stage - 1]):
                found.append((self.due[stage, i], -stage))
        return sorted(found)

    def run(self, stage):
        self.now = max(self.now, self.due[stage, self.next[stage]])
        self.steps[stage](self.next[stage])
        self.next[stage] += 1
        self.begin_some()

    def spend(self, time):
        self.now += time
        self.begin_some()
        while True:
            found = [entry for entry in self.able() if entry[0] <= self.now]
            if not found:
                return
            self.run(-found[0][1])

    def complete(self):
        self.begin_some()
        while self.next[4] < len(self.items):
            self.run(-self.able()[0][1])


def backward_compute(b, block, keys, spend, emit):
    rows, model = b[N.res].shape
    vec, sums = b[N.vec], b[N.sums]
    scale_row, feed_bias = 8 + 2 * block, 14 + block

    def close_rows(r):
        grad = b[N.res][r, :]
        if block:
            grad = jnp.where(live_rows(128, model), grad, 0.0)
            b[N.res][r, :] = grad
        add_rows(sums, scale_row + 1, grad * b[N.fd][r, :].astype(WIDE))
        low = (row(vec, scale_row + 1) * grad).astype(LOW)
        b[N.gm][r, :] = low
        add_rows(sums, feed_bias, low)

    b[N.res], b[N.fd]
    row_blocks(rows, 128, close_rows)
    spend(2.5)

    def turn(value, start=0):
        b[N.turn][:, start : start + rows] = value.T

    def weight_grad(right, first, stage, depth):
        def step(k):
            value = dot_nn(b[N.turn][:, :depth], right[:, lanes(first + k * TILE, TILE)])
            shape = stage.shape[:-1] + (TILE,)
            stage[..., lanes(k * TILE, TILE)] = value.reshape(shape).astype(LOW)

        each(model // TILE, step, unroll=3)

    active = b[N.active]
    chunks = active.shape[1] // model
    for chunk in range(chunks):
        turn(active[:, chunk * model : (chunk + 1) * model])
        b.saved(N.stage2)
        weight_grad(b[N.gm], 0, b[N.stage2], rows)
        emit(N.fc2, chunk, N.stage2)
        spend(2.2)
    turn(b[N.inner][...])
    w_fc1, w_fc2, slope = b[N.w_fc1], b[N.w_fc2], b[N.slope]
    for chunk in range(chunks):
        part = slice(chunk * model, (chunk + 1) * model)

        def hidden_rows(r):
            value = dot_nt(b[N.gm][r, :], flat(w_fc2[chunk]))
            low = (value * slope[r, part].astype(WIDE)).astype(LOW)
            active[r, part] = low
            add_rows(sums, 20 + 4 * block + chunk, low)

        row_blocks(rows, 256, hidden_rows)
        stage = N.stage + str(chunk % 2)
        b.saved(stage)
        weight_grad(active, chunk * model, b[stage], rows)
        emit(N.fc1, chunk, stage)
        spend(3.2)

        def inner_rows(r):
            value = dot_nt(active[r, part], flat(w_fc1[:, :, :, part]))
            if chunk:
                value = b[N.acc][r, :] + value
            b[N.acc][r, :] = value

        row_blocks(rows, 256, inner_rows)
        spend(1.4)
    b.load(N.w_qkv, b[N.qkv_full], w_fc1.at[:, :, :, : 3 * model])
    b.load(N.w_proj, b[N.proj_full], w_fc1.at[:, :, :, 3 * model :])
    branch = b[N.br]

    def middle_rows(r):
        back = norm_back(
            b[N.mid][r, :], b[N.acc][r, :], row(vec, 2 * block + 1), sums, 2 * block + 1, 4 + 2 * block + 1
        )
        grad = b[N.res][r, :] + back
        b[N.res][r, :] = grad
        add_rows(sums, scale_row, grad * branch[r, :].astype(WIDE))
        low = (row(vec, scale_row) * grad).astype(LOW)
        b[N.gm][r, :] = low
        add_rows(sums, 12 + block, low)

    b[N.mid]
    row_blocks(rows, 64, middle_rows)
    b.load(N.mid, b[N.begin_in])
    spend(3)
    turn(b[N.mix][...])
    b.saved(N.stage0)
    weight_grad(b[N.gm], 0, b[N.stage0], rows)
    emit(N.proj, 0, N.stage0)
    spend(2.2)
    b.wait(N.w_qkv, N.w_proj)
    w_qkv, w_proj = w_fc1.at[:, :, :, : 3 * model], w_fc1.at[:, :, :, 3 * model :]

    def mixed_rows(r):
        b[N.mix][r, :] = dot_nt(b[N.gm][r, :], flat(w_proj[...])).astype(LOW)

    row_blocks(rows, 256, mixed_rows)
    spend(1.2)
    query, key, value = b[N.query], b[N.key], b[N.value]
    b.wait(N.key2, N.value2)
    queries = b[N.aq] if block else b[N.a0]
    key_parts = [key.at[pl.ds(k * rows, rows)] for k in range(keys)]
    value_parts = [value.at[pl.ds(k * rows, rows)] for k in range(keys)]
    attend_back(
        b[N.mix], query, key_parts, value_parts, query, key_parts, value_parts,
        lambda: spend(1.7 + 0.5 * keys),
    )

    def bias_rows(r):
        add_rows(sums, 16 + 2 * block, query[r, :])
        for k in range(keys):
            add_rows(sums, 17 + 2 * block, value_parts[k][r, :])

    row_blocks(rows, 128, bias_rows)
    if block:
        turn(b[N.ak][...])
        turn(queries[...], rows)
    else:
        turn(queries[...])
    for chunk, right in ((1, key), (2, value)):
        stage = N.stage + str(chunk % 2)
        b.saved(stage)
        weight_grad(right, 0, b[stage], keys * rows)
        emit(N.qkv, chunk, stage)
        spend(1 + 1.3 * keys)
    if block:
        turn(queries[...])
    b.saved(N.stage1)
    weight_grad(query, 0, b[N.stage1], rows)
    emit(N.qkv, 0, N.stage1)
    spend(2.2)

    def back(k, parts):
        def step(r):
            total = 0.0
            for ref, chunk in parts:
                total = total + dot_nt(ref[r, :], flat(w_qkv[:, :, :, chunk * model : (chunk + 1) * model]))
            b[N.acc][r, :] = total

        row_blocks(rows, 256, step)

    gain, shift = 2 * block, 4 + 2 * block
    back(0, [(query, 0), (key_parts[keys - 1], 1), (value_parts[keys - 1], 2)])
    spend(3.3)
    b[N.mid]

    def start_rows(r):
        grad = b[N.res][r, :] + norm_back(b[N.mid][r, :], b[N.acc][r, :], row(vec, gain), sums, gain, shift)
        b[N.res][r, :] = grad
        b[N.gm][r, :] = grad.astype(LOW)

    row_blocks(rows, 64, start_rows)
    spend(2.5)
    table = dot_tn(b[N.gm][...], picks(b[N.spots][...], b[N.table].shape[1]))
    if block:
        b[N.table][...] = table
        b.load(N.mid, b[N.lat_in])
        b.load(N.res, b[N.grad_latent])
        back(0, [(key_parts[0], 1), (value_parts[0], 2)])
        b[N.mid], b[N.res]

        def latent_pair(k):
            for part in range(2):
                r = pl.ds(pl.multiple_of(k * SET + part * 64, 64), 64)
                grad = b[N.res][r, :]
                live = lax.broadcasted_iota(jnp.int32, grad.shape, 0) + part * 64 < VIS
                b[N.res][r, :] = jnp.where(live, grad, 0.0) + norm_back(
                    b[N.mid][r, :], b[N.acc][r, :], row(vec, gain), sums, gain, shift
                )

        each(rows // SET, latent_pair)
    else:
        b[N.table][...] += table


def table_of_sums(b, parts):
    table, sums = b[N.table], b[N.sums]
    pick = selection(PATCHES, table.shape[1])
    plain = lax.broadcasted_iota(jnp.int32, sums.shape, 0) < 16
    table[...] += dot_tn(jnp.where(plain, sums[...], 0.0).astype(LOW), pick)
    at = 16
    lines = lax.broadcasted_iota(jnp.int32, sums.shape, 0)
    for count, spots, which in ((parts[0], b[N.spots_q], b[N.which_q]), (parts[1], b[N.spots_f], b[N.which_f])):
        rows = spots.shape[0]
        for chunk in range(count):
            spread = jnp.zeros(sums.shape, WIDE)
            for block in range(2):
                base = at + block * count
                for j in range(count):
                    entry = sums[base + chunk : base + chunk + 1, :] * which[j : j + 1, :]
                    spread = spread + jnp.where(lines == base + j, entry, 0.0)
            held = dot_nt(spots[...], spread.astype(LOW)).astype(LOW)
            table[pl.ds(chunk * rows, rows), :] += dot_nn(held, pick)
        at += 2 * count


def backward(block, f, carried, spots, line, tables, pending, here):
    rows, model = f[N.mid0_out].shape
    hidden = f[N.active0_out].shape[1]
    wide = f[N.extra0].shape[3]
    keys = 1 + block
    shapes = {
        N.fc2: (hidden // (4 * line), model),
        N.fc1: (model // (4 * line), hidden),
        N.proj: (model // (4 * line), model),
        N.qkv: (model // (4 * line), 3 * model),
        N.extra: (model // (4 * line), wide),
    }
    whole = {kind: (line, 4) + shape for kind, shape in shapes.items()}
    pieces = {kind: [] for kind in shapes}
    for kind, piece, first, columns in cut(shapes):
        pieces[kind].append((piece, first, columns))
    pieces[N.extra] = [(0, 0, wide)]
    pieces[N.qkv] = pieces[N.qkv][1:] + pieces[N.qkv][:1]
    made = [N.fc2, N.fc1, N.proj, N.qkv]
    order_of = [kind for kind, _ in pending] + here
    sources = [N.pending + str(k) for k in range(len(pending))] + [N.g_ + kind for kind in here]
    items, owners, parts, counts, slots = [], [], [], {}, []
    for k, kind in enumerate(order_of):
        for piece, first, columns in pieces[kind]:
            items.append((shapes[kind][0], first, columns))
            owners.append(k)
            parts.append(piece)
            shape = (shapes[kind][0], columns // 2)
            counts[shape] = counts.get(shape, 0) + 1
            slots.append((shape, (counts[shape] - 1) % 4))
    held = sorted(set(slots))
    slots = [held.index(slot) for slot in slots]
    ins = {N.pending + str(k): grad for k, (_, grad) in enumerate(pending)}
    ins[N.res_in] = carried[N.res]
    for kind in made:
        ins[kind + N._full] = f[kind + str(block)]
    if block:
        ins[N.grad_latent] = carried[N.grad_latent]
        loads = {N.fd: N.fd1, N.active: N.active1, N.slope: N.slope1, N.inner: N.a21, N.mid: N.mid1}
        loads.update({N.br: N.br1, N.mix: N.mix1, N.query: N.q1, N.aq: N.aq, N.ak: N.ak})
        ins[N.begin_in], ins[N.lat_in] = f[N.query_out], f[N.lat_out]
        ins[N.k2_in], ins[N.v2_in] = f[N.k2_out], f[N.v2_out]
        loads.update({N.key: N.k1, N.value: N.v1})
    else:
        loads = {N.fd: N.fd0, N.active: N.active0, N.slope: N.slope0, N.inner: N.a20, N.mid: N.mid0}
        loads.update({N.br: N.br0, N.mix: N.mix0, N.query: N.q0, N.key: N.k0, N.value: N.v0, N.a0: N.a0})
        ins[N.begin_in] = f[N.start_out]
        ins[N.table_in], ins[N.sums_in] = carried[N.table], carried[N.sums]
    for name, source in loads.items():
        ins[name + N._in] = f[source + N._out]
    ins[N.vec_in] = f[N.vec_out]
    small = {N.spots: spots}
    if not block:
        small.update(dict(zip((N.spots_q, N.which_q, N.spots_f, N.which_f), tables)))
    outs = {N.g_ + kind: shape_of(whole[kind], LOW) for kind in made + ([] if block else [N.extra])}
    for k, kind in enumerate(order_of):
        outs[N.out + str(k)] = shape_of((shapes[kind][0] // 2, shapes[kind][1]), WIDE)
    outs[N.res_out] = shape_of((rows, model), WIDE)
    if block:
        outs[N.table_out] = shape_of((model, wide), WIDE)
        outs[N.sums_out] = shape_of((32, model), WIDE)
    scratch = {name: ((rows, model), WIDE) for name in (N.res, N.acc, N.mid)}
    for name in (N.fd, N.inner, N.br, N.mix, N.query, N.gm) + ((N.aq, N.ak) if block else (N.a0,)):
        scratch[name] = ((rows, model), LOW)
    scratch[N.key] = scratch[N.value] = ((keys * rows, model), LOW)
    scratch[N.turn] = ((model, keys * rows), LOW)
    scratch[N.active] = scratch[N.slope] = ((rows, hidden), LOW)
    scratch[N.w_fc1], scratch[N.w_fc2] = (whole[N.fc1], LOW), (whole[N.fc2], LOW)
    scratch[N.stage0] = scratch[N.stage1] = (whole[N.proj], LOW)
    scratch[N.stage2] = (whole[N.fc2][1:], LOW)
    scratch[N.vec] = scratch[N.sums] = ((32, model), WIDE)
    scratch[N.table] = ((model, wide), WIDE)
    if not block:
        scratch[N.table4] = (whole[N.extra], LOW)
    for k, kind in enumerate(order_of):
        scratch[N.shard + str(k)] = ((shapes[kind][0] // 2, shapes[kind][1]), WIDE)
    extra = []
    for (r, half), _ in held:
        extra += [pltpu.VMEM((line, 4, r, half), LOW)] * 2
        extra += [pltpu.VMEM((line, r, half), LOW), pltpu.VMEM((r, half), WIDE)]
        extra += [pltpu.VMEM((r // 2, half), WIDE)]
    for r, _, columns in items:
        half = columns // 2
        extra += [pltpu.VMEM((line, r, half), LOW)] * 3 + [pltpu.VMEM((line - 1, r, half), LOW)]
    pairs = len(items) * (line + 5)
    extra += [pltpu.SemaphoreType.DMA((pairs,))] * 2 + [pltpu.SemaphoreType.REGULAR((len(held),))]

    def body(b, *refs):
        shared = [refs[5 * k : 5 * k + 5] for k in range(len(held))]
        rest = refs[5 * len(held) :]
        single = [rest[4 * k : 4 * k + 4] for k in range(len(items))]
        send, recv, credit = rest[-3:]
        b.load(N.res, b[N.res_in])
        b.load(N.fd, b[N.fd_in])
        b.load(N.vec, b[N.vec_in])
        if not block:
            b.load(N.sums, b[N.sums_in])
            b.load(N.table, b[N.table_in])
        b.load(N.active, b[N.active_in])
        b.load(N.w_fc2, b[N.fc2_full])
        b.load(N.slope, b[N.slope_in])
        b.load(N.inner, b[N.inner_in])
        b.load(N.w_fc1, b[N.fc1_full])
        for name in loads:
            if name in (N.mid, N.br, N.mix, N.query, N.aq, N.ak, N.a0):
                b.load(name, b[name + N._in])
        for name in (N.key, N.value):
            b.load(name, b[name + N._in], b.refs[name].at[pl.ds(0, rows)])
        if block:
            b.load(N.key2, b[N.k2_in], b.refs[N.key].at[pl.ds(rows, rows)])
            b.load(N.value2, b[N.v2_in], b.refs[N.value].at[pl.ds(rows, rows)])
            b[N.sums][...] = jnp.zeros(b[N.sums].shape, WIDE)
        reducer = Reducer(
            line, items, slots, [b[sources[k]] for k in owners], [b[N.shard + str(k)] for k in owners],
            shared, single, send, recv, credit,
        )
        reducer.ready.update(i for i, k in enumerate(owners) if k < len(pending))
        waiting = []

        def settle(count):
            for _ in range(count):
                kind, chunk, entry = waiting.pop(0)
                b.settle([entry])
                for i, k in enumerate(owners):
                    if k < len(pending) or order_of[k] != kind:
                        continue
                    if kind != N.fc2 and parts[i] == chunk or kind == N.fc2 and chunk == hidden // model - 1:
                        reducer.ready.add(i)

        def emit(kind, chunk, stage):
            out = b[N.g_ + kind]
            target = out.at[chunk] if kind == N.fc2 else out
            if kind in (N.fc1, N.qkv):
                target = out.at[:, :, :, pl.ds(chunk * model, model)]
            b.save(stage, target)
            waiting.append((kind, chunk, b.saving[-1]))
            fresh[0] += 1

        fresh = [0]

        def spend(time):
            settle(len(waiting) - fresh[0])
            reducer.spend(time)
            fresh[0] = 0

        backward_compute(b, block, keys, spend, emit)
        b.save(N.res, b[N.res_out])
        if block:
            b.save(N.table, b[N.table_out])
            b.save(N.sums, b[N.sums_out])
        else:
            table_of_sums(b, (2, 4))
            b[N.table4][...] = b[N.table][...].astype(LOW).reshape(b[N.table4].shape)
            emit(N.extra, 0, N.table4)
        settle(len(waiting))
        reducer.complete()
        for k in range(len(order_of)):
            b.save(N.shard + str(k), b[N.out + str(k)])
        b.drain()

    name = N.backward_regressor if block else N.backward_encoder
    return call(body, ins, small, outs, scratch, 128, extra, name, 1 + block, 64 << 20), order_of


def pack(pos, ln_gain, ln_bias, scales, b_proj, b_fc2, b_qkv, b_fc1):
    rows = pos.shape[1]

    def turned(array):
        return jnp.moveaxis(array.reshape(-1, array.shape[-1]), 1, 0)

    def folded(array):
        return turned(array.reshape(2, -1, rows))

    columns = [turned(pos), turned(ln_gain), turned(ln_bias), turned(scales)]
    columns += [turned(b_proj), turned(b_fc2), folded(b_qkv), folded(b_fc1)]
    joined = jnp.concatenate([column.astype(LOW) for column in columns], axis=1)
    return jnp.pad(joined, ((0, 0), (0, 256 - joined.shape[1])))


def unpack_rows(extra, patches, devices, fold):
    at = patches
    turned = extra.T
    pos = turned[:patches]
    outs = []
    for _ in range(3):
        outs.append(turned[at : at + 4].reshape(2, 2, -1))
        at += 4
    for _ in range(2):
        outs.append(turned[at : at + 2])
        at += 2
    for pieces in fold:
        part = turned[at : at + 2 * pieces].reshape(2, pieces, devices, -1)
        outs.append(jnp.swapaxes(part, 1, 2).reshape(2, -1))
        at += 2 * pieces
    return [pos] + outs


def fused(
    devices, patches, order, grad_latent, grad_out, pos_embed, ln_gain, ln_bias, w_qkv, b_qkv, w_proj, b_proj,
    w_fc1, b_fc1, w_fc2, b_fc2, layer_scale,
):
    line = devices // 8
    model = patches.shape[1]
    own = pos_embed.shape[1]

    def places(index):
        return jnp.pad(index, ((0, 0), (0, SET - VIS)), constant_values=-1).reshape(-1, 1)

    vis, hid = places(order[:, :VIS]), places(order[:, VIS:])
    extra = pack(pos_embed, ln_gain, ln_bias, layer_scale, b_proj, b_fc2, b_qkv, b_fc1)
    fold = (b_qkv.shape[1] // own, b_fc1.shape[1] // own)
    tables = fold_tables(model, own, fold[0]) + fold_tables(model, own, fold[1])
    kept = forward(patches, vis, hid, extra, (w_qkv, w_proj, w_fc1, w_fc2), line, tables)
    late, late_kinds = backward(
        1, kept, {N.res: grad_out, N.grad_latent: grad_latent}, hid, line, tables, [], [N.fc2, N.fc1]
    )
    pending = [(kind, late[N.g_ + kind]) for kind in (N.proj, N.qkv)]
    carried = {N.res: late[N.res_out], N.table: late[N.table_out], N.sums: late[N.sums_out]}
    everything = [N.fc2, N.fc1, N.proj, N.qkv, N.extra]
    early, early_kinds = backward(0, kept, carried, vis, line, tables, pending, everything)
    reg = {kind: late[N.out + str(k)] for k, kind in enumerate(late_kinds)}
    reg.update({kind: early[N.out + str(k)] for k, (kind, _) in enumerate(pending)})
    enc = {kind: early[N.out + str(k)] for k, kind in enumerate(early_kinds) if k >= len(pending)}
    pos_shard, gains, shifts, scales, proj_b, fc2_b, qkv_b, fc1_b = unpack_rows(
        enc[N.extra], PATCHES, 1, fold
    )
    qkv, proj, fc1, fc2 = [jnp.stack([enc[kind], reg[kind]]) for kind in (N.qkv, N.proj, N.fc1, N.fc2)]
    return (
        kept[N.latent_out], kept[N.regressed_out], early[N.res_out], pos_shard,
        gains, shifts, qkv, qkv_b, proj, proj_b, fc1, fc1_b, fc2, fc2_b, scales,
    )


def norm_forward(value, gain, shift):
    center = jnp.mean(value, axis=-1, keepdims=True)
    centered = value - center
    inverse = lax.rsqrt(jnp.mean(centered * centered, axis=-1, keepdims=True) + 1e-06)
    normed = centered * inverse
    return (normed * gain + shift, normed, inverse)


def norm_backward(grad, normed, inverse, gain):
    scaled = grad * gain
    first_mean = jnp.mean(scaled, axis=-1, keepdims=True)
    second_mean = jnp.mean(scaled * normed, axis=-1, keepdims=True)
    back = inverse * (scaled - first_mean - normed * second_mean)
    return (back, jnp.sum(grad * normed, axis=0), jnp.sum(grad, axis=0))


def unpack(pieces):
    gains, shifts, w_qkv, b_qkv, w_proj, b_proj, w_fc1, b_fc1, w_fc2, b_fc2, scales = pieces
    wide = jnp.float32
    return (
        gains.astype(wide),
        shifts.astype(wide),
        w_qkv,
        b_qkv.astype(wide),
        w_proj,
        b_proj.astype(wide),
        w_fc1,
        b_fc1.astype(wide),
        w_fc2,
        b_fc2.astype(wide),
        scales.astype(wide),
    )


def fetch(block, arrays):
    ln_gain, ln_bias, w_qkv, b_qkv, w_proj, b_proj, w_fc1, b_fc1, w_fc2, b_fc2, layer_scale = arrays
    gathered = (
        lax.all_gather(ln_gain[block], ("dp", "fsdp"), axis=1, tiled=True),
        lax.all_gather(ln_bias[block], ("dp", "fsdp"), axis=1, tiled=True),
        lax.all_gather(w_qkv[block], ("dp", "fsdp"), axis=0, tiled=True),
        lax.all_gather(b_qkv[block], ("dp", "fsdp"), axis=0, tiled=True),
        lax.all_gather(w_proj[block], ("dp", "fsdp"), axis=0, tiled=True),
        lax.all_gather(b_proj[block], ("dp", "fsdp"), axis=0, tiled=True),
        lax.all_gather(w_fc1[block], ("dp", "fsdp"), axis=0, tiled=True),
        lax.all_gather(b_fc1[block], ("dp", "fsdp"), axis=0, tiled=True),
        lax.all_gather(w_fc2[block], ("dp", "fsdp"), axis=0, tiled=True),
        lax.all_gather(b_fc2[block], ("dp", "fsdp"), axis=0, tiled=True),
        lax.all_gather(layer_scale[block], ("dp", "fsdp"), axis=1, tiled=True),
    )
    return unpack(gathered)


def column_sum(value):
    return jnp.sum(value.astype(jnp.float32), axis=0)


def outer_rows(left, right):
    return jnp.einsum("rd,rf->df", left, right, preferred_element_type=jnp.float32)


def attend_scores(queries, keys, key_live):
    scores = jnp.einsum("gqhe,gkhe->ghqk", queries, keys, preferred_element_type=jnp.float32) * (
        1.0 / math.sqrt(HEAD_DIM)
    )
    return jnp.where(key_live, scores, -1e30)


def attend_forward(query_in, key_in, images, key_live, weights):
    w_qkv, b_qkv, w_proj, b_proj = (weights[2], weights[3], weights[4], weights[5])
    model = query_in.shape[1]
    heads = model // HEAD_DIM
    queries = (
        jnp.dot(query_in, w_qkv[:, :model], preferred_element_type=jnp.float32) + b_qkv[:model]
    ).astype(jnp.bfloat16)
    paired = jnp.dot(key_in, w_qkv[:, model:], preferred_element_type=jnp.float32)
    keys = paired[:, :model].astype(jnp.bfloat16).reshape(images, -1, heads, HEAD_DIM)
    values = (
        (paired[:, model:] + b_qkv[model:])
        .astype(jnp.bfloat16)
        .reshape(images, -1, heads, HEAD_DIM)
    )
    queries = queries.reshape(images, -1, heads, HEAD_DIM)
    scores = attend_scores(queries, keys, key_live)
    highest_score = jnp.max(scores, axis=-1, keepdims=True)
    weighted = jnp.exp(scores - highest_score)
    summed = jnp.sum(weighted, axis=-1, keepdims=True)
    softmax_out = (weighted / summed).astype(jnp.bfloat16)
    mixed = jnp.einsum("ghqk,gkhe->gqhe", softmax_out, values, preferred_element_type=jnp.float32)
    mixed = mixed.reshape(-1, model).astype(jnp.bfloat16)
    branch = jnp.dot(mixed, w_proj, preferred_element_type=jnp.float32) + b_proj
    return (branch, (queries, keys, values, highest_score + jnp.log(summed), mixed))


def attend_backward(grad_branch, query_in, key_in, key_live, kept, weights):
    w_qkv, w_proj = (weights[2], weights[4])
    queries, keys, values, log_total, mixed = kept
    model = query_in.shape[1]
    grad_low = grad_branch.astype(jnp.bfloat16)
    grad_w_proj = outer_rows(mixed, grad_low)
    grad_b_proj = column_sum(grad_low)
    grad_mixed = (
        jnp.dot(grad_low, w_proj.T, preferred_element_type=jnp.float32)
        .astype(jnp.bfloat16)
        .reshape(queries.shape)
    )
    softmax_out = jnp.exp(attend_scores(queries, keys, key_live) - log_total)
    grad_values = jnp.einsum(
        "ghqk,gqhe->gkhe",
        softmax_out.astype(jnp.bfloat16),
        grad_mixed,
        preferred_element_type=jnp.float32,
    )
    grad_soft = jnp.einsum(
        "gqhe,gkhe->ghqk", grad_mixed, values, preferred_element_type=jnp.float32
    )
    grad_scores = (
        softmax_out * (grad_soft - jnp.sum(grad_soft * softmax_out, axis=-1, keepdims=True))
    ).astype(jnp.bfloat16)
    factor = 1.0 / math.sqrt(HEAD_DIM)
    grad_queries = (
        (
            jnp.einsum("ghqk,gkhe->gqhe", grad_scores, keys, preferred_element_type=jnp.float32)
            * factor
        )
        .astype(jnp.bfloat16)
        .reshape(-1, model)
    )
    grad_keys = (
        (
            jnp.einsum("ghqk,gqhe->gkhe", grad_scores, queries, preferred_element_type=jnp.float32)
            * factor
        )
        .astype(jnp.bfloat16)
        .reshape(-1, model)
    )
    grad_values = grad_values.astype(jnp.bfloat16).reshape(-1, model)
    grad_pairs = jnp.concatenate([grad_keys, grad_values], axis=1)
    grad_w_qkv = jnp.concatenate(
        [outer_rows(query_in, grad_queries), outer_rows(key_in, grad_pairs)], axis=1
    )
    grad_b_qkv = jnp.concatenate([column_sum(grad_queries), column_sum(grad_values)])
    grad_query_in = jnp.dot(grad_queries, w_qkv[:, :model].T, preferred_element_type=jnp.float32)
    grad_key_in = jnp.dot(grad_pairs, w_qkv[:, model:].T, preferred_element_type=jnp.float32)
    return (grad_query_in, grad_key_in, (grad_w_qkv, grad_b_qkv, grad_w_proj, grad_b_proj))


def feed_forward(middle, weights):
    gains, shifts, w_fc1, b_fc1, w_fc2, b_fc2 = (
        weights[0],
        weights[1],
        weights[6],
        weights[7],
        weights[8],
        weights[9],
    )
    normed_out, normed, inverse = norm_forward(middle, gains[1], shifts[1])
    inner_in = normed_out.astype(jnp.bfloat16)
    hidden = jnp.dot(inner_in, w_fc1, preferred_element_type=jnp.float32) + b_fc1
    active = jax.nn.gelu(hidden, approximate=True).astype(jnp.bfloat16)
    branch = jnp.dot(active, w_fc2, preferred_element_type=jnp.float32) + b_fc2
    return (branch, (normed, inverse, inner_in, hidden, active))


def feed_backward(grad_branch, kept, weights):
    gains, w_fc1, w_fc2 = (weights[0], weights[6], weights[8])
    normed, inverse, inner_in, hidden, active = kept
    grad_low = grad_branch.astype(jnp.bfloat16)
    grad_w_fc2 = outer_rows(active, grad_low)
    grad_b_fc2 = column_sum(grad_low)
    grad_active = jnp.dot(grad_low, w_fc2.T, preferred_element_type=jnp.float32)
    gelu_back = jax.vjp(functools.partial(jax.nn.gelu, approximate=True), hidden)[1]
    grad_hidden = gelu_back(grad_active)[0].astype(jnp.bfloat16)
    grad_w_fc1 = outer_rows(inner_in, grad_hidden)
    grad_b_fc1 = column_sum(grad_hidden)
    grad_normed = jnp.dot(grad_hidden, w_fc1.T, preferred_element_type=jnp.float32)
    grad_middle, grad_gain, grad_shift = norm_backward(grad_normed, normed, inverse, gains[1])
    return (grad_middle, grad_gain, grad_shift, (grad_w_fc1, grad_b_fc1, grad_w_fc2, grad_b_fc2))


def local(
    patches,
    order,
    grad_latent,
    grad_out,
    pos_embed,
    ln_gain,
    ln_bias,
    w_qkv,
    b_qkv,
    w_proj,
    b_proj,
    w_fc1,
    b_fc1,
    w_fc2,
    b_fc2,
    layer_scale,
):
    arrays = (
        ln_gain,
        ln_bias,
        w_qkv,
        b_qkv,
        w_proj,
        b_proj,
        w_fc1,
        b_fc1,
        w_fc2,
        b_fc2,
        layer_scale,
    )
    images = order.shape[0]
    model = patches.shape[1]
    highest = lax.Precision.HIGHEST
    live = jnp.arange(SET) < VIS
    live_rows = jnp.tile(live, images).astype(jnp.float32)[:, None]
    patch_slots = jnp.arange(PATCHES)

    def picker(index):
        padded = jnp.pad(index, ((0, 0), (0, SET - VIS)))
        chosen = (padded[:, :, None] == patch_slots[None, None, :]) & live[None, :, None]
        return chosen.astype(jnp.float32).reshape(-1, PATCHES)

    pick_visible = picker(order[:, :VIS])
    pick_masked = picker(order[:, VIS:])
    pos_table = lax.all_gather(pos_embed, ("dp", "fsdp"), axis=1, tiled=True).astype(jnp.float32)
    enc_weights, reg_weights = fetch(0, arrays), fetch(1, arrays)
    start = patches.astype(jnp.float32) + jnp.dot(pick_visible, pos_table, precision=highest)
    enc_out, enc_normed, enc_inverse = norm_forward(start, enc_weights[0][0], enc_weights[1][0])
    enc_attn_in = enc_out.astype(jnp.bfloat16)
    enc_branch, enc_attn_kept = attend_forward(enc_attn_in, enc_attn_in, images, live, enc_weights)
    enc_middle = start + enc_weights[10][0] * enc_branch
    enc_feed, enc_feed_kept = feed_forward(enc_middle, enc_weights)
    latent_f = enc_middle + enc_weights[10][1] * enc_feed
    query_start = jnp.dot(pick_masked, pos_table, precision=highest)
    query_out, query_normed, query_inverse = norm_forward(
        query_start, reg_weights[0][0], reg_weights[1][0]
    )
    latent_out, latent_normed, latent_inverse = norm_forward(
        latent_f, reg_weights[0][0], reg_weights[1][0]
    )
    query_in = query_out.astype(jnp.bfloat16)
    key_in = jnp.concatenate(
        [
            latent_out.astype(jnp.bfloat16).reshape(images, SET, model),
            query_in.reshape(images, SET, model),
        ],
        axis=1,
    ).reshape(-1, model)
    key_live = jnp.concatenate([live, live])
    reg_branch, reg_attn_kept = attend_forward(query_in, key_in, images, key_live, reg_weights)
    reg_middle = query_start + reg_weights[10][0] * reg_branch
    reg_feed, reg_feed_kept = feed_forward(reg_middle, reg_weights)
    regressed_f = reg_middle + reg_weights[10][1] * reg_feed
    reg_back = reg_weights
    grad_final = grad_out * live_rows
    reg_scale_late = jnp.sum(grad_final * reg_feed, axis=0)
    grad_from_feed, reg_gain_late, reg_shift_late, reg_feed_grads = feed_backward(
        reg_back[10][1] * grad_final, reg_feed_kept, reg_back
    )
    grad_reg_middle = grad_final + grad_from_feed
    reg_scale_early = jnp.sum(grad_reg_middle * reg_branch, axis=0)
    grad_query_in, grad_key_in, reg_attn_grads = attend_backward(
        reg_back[10][0] * grad_reg_middle, query_in, key_in, key_live, reg_attn_kept, reg_back
    )
    grad_key_in = grad_key_in.reshape(images, 2 * SET, model)
    grad_query_norm = grad_query_in + grad_key_in[:, SET:].reshape(-1, model)
    grad_latent_norm = grad_key_in[:, :SET].reshape(-1, model)
    back_query, reg_gain_query, reg_shift_query = norm_backward(
        grad_query_norm, query_normed, query_inverse, reg_back[0][0]
    )
    back_latent, reg_gain_key, reg_shift_key = norm_backward(
        grad_latent_norm, latent_normed, latent_inverse, reg_back[0][0]
    )
    grad_query_start = grad_reg_middle + back_query
    reg_grads = (
        (
            jnp.stack([reg_gain_query + reg_gain_key, reg_gain_late]),
            jnp.stack([reg_shift_query + reg_shift_key, reg_shift_late]),
        )
        + reg_attn_grads
        + reg_feed_grads
        + (jnp.stack([reg_scale_early, reg_scale_late]),)
    )
    enc_back = enc_weights
    grad_finish = grad_latent * live_rows + back_latent
    enc_scale_late = jnp.sum(grad_finish * enc_feed, axis=0)
    grad_from_feed, enc_gain_late, enc_shift_late, enc_feed_grads = feed_backward(
        enc_back[10][1] * grad_finish, enc_feed_kept, enc_back
    )
    grad_enc_middle = grad_finish + grad_from_feed
    enc_scale_early = jnp.sum(grad_enc_middle * enc_branch, axis=0)
    grad_as_query, grad_as_key, enc_attn_grads = attend_backward(
        enc_back[10][0] * grad_enc_middle, enc_attn_in, enc_attn_in, live, enc_attn_kept, enc_back
    )
    back_start, enc_gain_early, enc_shift_early = norm_backward(
        grad_as_query + grad_as_key, enc_normed, enc_inverse, enc_back[0][0]
    )
    grad_start = grad_enc_middle + back_start
    grad_table = jnp.dot(pick_visible.T, grad_start, precision=highest) + jnp.dot(
        pick_masked.T, grad_query_start, precision=highest
    )
    enc_grads = (
        (jnp.stack([enc_gain_early, enc_gain_late]), jnp.stack([enc_shift_early, enc_shift_late]))
        + enc_attn_grads
        + enc_feed_grads
        + (jnp.stack([enc_scale_early, enc_scale_late]),)
    )
    reg_shards = (
        lax.psum_scatter(reg_grads[0], ("dp", "fsdp"), scatter_dimension=1, tiled=True),
        lax.psum_scatter(reg_grads[1], ("dp", "fsdp"), scatter_dimension=1, tiled=True),
        lax.psum_scatter(reg_grads[2], ("dp", "fsdp"), scatter_dimension=0, tiled=True),
        lax.psum_scatter(reg_grads[3], ("dp", "fsdp"), scatter_dimension=0, tiled=True),
        lax.psum_scatter(reg_grads[4], ("dp", "fsdp"), scatter_dimension=0, tiled=True),
        lax.psum_scatter(reg_grads[5], ("dp", "fsdp"), scatter_dimension=0, tiled=True),
        lax.psum_scatter(reg_grads[6], ("dp", "fsdp"), scatter_dimension=0, tiled=True),
        lax.psum_scatter(reg_grads[7], ("dp", "fsdp"), scatter_dimension=0, tiled=True),
        lax.psum_scatter(reg_grads[8], ("dp", "fsdp"), scatter_dimension=0, tiled=True),
        lax.psum_scatter(reg_grads[9], ("dp", "fsdp"), scatter_dimension=0, tiled=True),
        lax.psum_scatter(reg_grads[10], ("dp", "fsdp"), scatter_dimension=1, tiled=True),
    )
    enc_shards = (
        lax.psum_scatter(grad_table, ("dp", "fsdp"), scatter_dimension=1, tiled=True),
        lax.psum_scatter(enc_grads[0], ("dp", "fsdp"), scatter_dimension=1, tiled=True),
        lax.psum_scatter(enc_grads[1], ("dp", "fsdp"), scatter_dimension=1, tiled=True),
        lax.psum_scatter(enc_grads[2], ("dp", "fsdp"), scatter_dimension=0, tiled=True),
        lax.psum_scatter(enc_grads[3], ("dp", "fsdp"), scatter_dimension=0, tiled=True),
        lax.psum_scatter(enc_grads[4], ("dp", "fsdp"), scatter_dimension=0, tiled=True),
        lax.psum_scatter(enc_grads[5], ("dp", "fsdp"), scatter_dimension=0, tiled=True),
        lax.psum_scatter(enc_grads[6], ("dp", "fsdp"), scatter_dimension=0, tiled=True),
        lax.psum_scatter(enc_grads[7], ("dp", "fsdp"), scatter_dimension=0, tiled=True),
        lax.psum_scatter(enc_grads[8], ("dp", "fsdp"), scatter_dimension=0, tiled=True),
        lax.psum_scatter(enc_grads[9], ("dp", "fsdp"), scatter_dimension=0, tiled=True),
        lax.psum_scatter(enc_grads[10], ("dp", "fsdp"), scatter_dimension=1, tiled=True),
    )
    pos_shard = enc_shards[0]
    weight_shards = tuple(
        (jnp.stack([early, late]) for early, late in zip(enc_shards[1:], reg_shards))
    )
    return (
        latent_f.astype(jnp.bfloat16),
        regressed_f.astype(jnp.bfloat16),
        grad_start,
        pos_shard,
    ) + weight_shards


def solution(mesh):
    in_specs = (
        P(("dp", "fsdp"), None),
        P(("dp", "fsdp"), None),
        P(("dp", "fsdp"), None),
        P(("dp", "fsdp"), None),
        P(None, ("dp", "fsdp")),
        P(None, None, ("dp", "fsdp")),
        P(None, None, ("dp", "fsdp")),
        P(None, ("dp", "fsdp"), None),
        P(None, ("dp", "fsdp")),
        P(None, ("dp", "fsdp"), None),
        P(None, ("dp", "fsdp")),
        P(None, ("dp", "fsdp"), None),
        P(None, ("dp", "fsdp")),
        P(None, ("dp", "fsdp"), None),
        P(None, ("dp", "fsdp")),
        P(None, None, ("dp", "fsdp")),
    )
    out_specs = (
        P(("dp", "fsdp"), None),
        P(("dp", "fsdp"), None),
        P(("dp", "fsdp"), None),
        P(None, ("dp", "fsdp")),
        P(None, None, ("dp", "fsdp")),
        P(None, None, ("dp", "fsdp")),
        P(None, ("dp", "fsdp"), None),
        P(None, ("dp", "fsdp")),
        P(None, ("dp", "fsdp"), None),
        P(None, ("dp", "fsdp")),
        P(None, ("dp", "fsdp"), None),
        P(None, ("dp", "fsdp")),
        P(None, ("dp", "fsdp"), None),
        P(None, ("dp", "fsdp")),
        P(None, None, ("dp", "fsdp")),
    )
    devices = mesh.shape["dp"] * mesh.shape["fsdp"]

    def step(*args):
        rows = args[7].shape[1]
        kernels = mesh.shape["fsdp"] == 4 and rows // (devices // 2) % 16 == 0
        run = jax.shard_map(
            functools.partial(fused, devices) if kernels else local,
            mesh=mesh,
            in_specs=in_specs,
            out_specs=out_specs,
            check_vma=False,
        )
        return run(*args)

    return step
```

```python
import functools
import math

import jax
import jax.numpy as jnp
import numpy as np
from jax import lax
from jax.experimental import pallas as pl
from jax.experimental.pallas import tpu as pltpu
from jax.sharding import PartitionSpec as P

HEAD_DIM = 64
VIS = 98
SET = 128
PATCHES = 196

MESH = pl.DeviceIdType.MESH
WIDE = jnp.float32
LOW = jnp.bfloat16


def lanes(start, size):
    return pl.ds(pl.multiple_of(start, 128), size)


class Place:
    def __init__(self, line):
        dp, fsdp = lax.axis_index("dp"), lax.axis_index("fsdp")
        self.line = line
        self.z, self.y = dp // 2, dp % 2
        self.x, self.core = fsdp // 2, fsdp % 2
        z, y, x, core = self.z, self.y, self.x, self.core
        first_y = jnp.where(core == 0, 1 - y, y)
        first_x = jnp.where(core == 0, x, 1 - x)
        second_y = jnp.where(core == 0, y, 1 - y)
        second_x = jnp.where(core == 0, 1 - x, x)
        self.own = 2 * y + x
        self.first = 2 * first_y + first_x
        self.second = 2 * second_y + second_x
        self.across = 2 * (1 - y) + (1 - x)
        self.twin = self.at(z, y, x, 1 - core)
        self.near = self.at(z, first_y, first_x, core)
        self.far = self.at(z, second_y, second_x, core)
        self.above = [
            self.at(lax.rem(z + step, line), y, x, core) for step in range(1, line)
        ]

    def at(self, z, y, x, core):
        return (2 * z + y, 2 * x + core)

    def greet(self):
        barrier = pltpu.get_barrier_semaphore()
        others = [self.twin, self.near, self.far] + self.above
        for other in others:
            pl.semaphore_signal(barrier, inc=1, device_id=other, device_id_type=MESH)
        pl.semaphore_wait(barrier, len(others))


class Copies:
    def __init__(self, send, recv):
        self.send, self.recv, self.used, self.sent = send, recv, 0, []

    def remote(self, source, target, device):
        copy = pltpu.make_async_remote_copy(
            src_ref=source,
            dst_ref=target,
            send_sem=self.send.at[self.used],
            recv_sem=self.recv.at[self.used],
            device_id=device,
            device_id_type=MESH,
        )
        self.used += 1
        copy.start()
        self.sent.append(copy)
        return copy

    def local(self, source, target):
        copy = pltpu.make_async_copy(source, target, self.send.at[self.used])
        self.used += 1
        copy.start()
        return copy

    def drain(self):
        for copy in self.sent:
            copy.wait_send()


def gather_steps(line, items, sources, shards, theirs, fulls, stages, send, recv, bring):
    count = len(items)
    place = Place(line)
    copies = Copies(send, recv)
    place.greet()
    swaps = [copies.remote(source, their, place.twin) for source, their in zip(sources, theirs)]
    arrived = set()
    sizes = [wide // 2 for _, _, _, wide in items]
    columns = [lanes(item[2] + place.core * half, half) for item, half in zip(items, sizes)]

    def stage(i):
        array, rows, first, _ = items[i]
        own, their = shards[array](), theirs[array]
        if array not in arrived:
            arrived.add(array)
            swaps[array].wait_recv()
        for which, (low_ref, high_ref) in ((0, (own, their)), (1, (their, own))):

            @pl.when(place.core == which)
            def _():
                part = pl.ds(first + which * sizes[i], sizes[i])
                both = jnp.concatenate(
                    [low_ref[:, part].astype(WIDE), high_ref[:, part].astype(WIDE)], axis=0
                )
                stages[i][...] = both.astype(LOW)

    def group(i, which):
        return fulls[items[i][0]].at[:, which, :, columns[i]]

    def spread(i):
        target = fulls[items[i][0]].at[place.z, place.own, :, columns[i]]
        own = copies.local(stages[i], target)
        return [own] + [copies.remote(stages[i], target, device) for device in place.above]

    def send_on(i, which, devices):
        return [copies.remote(group(i, which), group(i, which), device) for device in devices]

    def share(i, far, twin, onward):
        far.wait_recv()
        onward[0].wait_recv()
        more = send_on(i, place.second, [place.twin]) + send_on(i, place.across, [place.twin])
        return [twin, onward[1]] + more

    def complete(i, started):
        for copy in started:
            copy.wait_recv()
        bring(i)

    ahead, lead = 5, 2
    start = 9.0
    spreads, owned, last, shared = {}, {}, {}, {}

    def own_sends(i):
        if i + ahead < count:
            stage(i + ahead)
            spreads[i + ahead] = spread(i + ahead)
        spreads[i][0].wait()
        for copy in spreads[i][1:]:
            copy.wait_recv()
        owned[i] = send_on(i, place.own, [place.near, place.far, place.twin])

    for i in range(min(ahead, count)):
        stage(i)
        spreads[i] = spread(i)
    for i in range(min(lead, count)):
        yield start
        own_sends(i)
    for i in range(count + 2):
        if i < count:
            start += 3 * line * items[i][1] * sizes[i] * 2 / RATE
            if i + lead < count:
                yield start - 1.5
                own_sends(i + lead)
            yield start
            near, far, twin = owned[i]
            near.wait_recv()
            last[i] = (far, twin, send_on(i, place.first, [place.far, place.twin]))
        else:
            yield start + 2
        if 0 <= i - 1 < count:
            shared[i - 1] = share(i - 1, *last[i - 1])
        if 0 <= i - 2 < count:
            complete(i - 2, shared[i - 2])
    yield start
    copies.drain()


class Names:
    def __getattr__(self, word):
        return word


N = Names()
LINK = 64e3
RATE = 92e3
TWIN = 4e5


class Pace:
    def __init__(self, steps):
        self.steps, self.now = steps, 0.0
        self.due = next(steps)

    def advance(self):
        self.now = max(self.now, self.due)
        self.due = next(self.steps, None)

    def spend(self, time):
        self.now += time
        while self.due is not None and self.due <= self.now:
            self.advance()

    def until(self, reached):
        while not reached():
            self.advance()

    def finish(self):
        while self.due is not None:
            self.advance()
TILE = 256
ROOT = math.sqrt(2.0 / math.pi)
CUBE = 0.044715


def dot_nn(left, right):
    return lax.dot_general(left, right, (((1,), (0,)), ((), ())), preferred_element_type=WIDE)


def dot_nt(left, right):
    return lax.dot_general(left, right, (((1,), (1,)), ((), ())), preferred_element_type=WIDE)


def dot_tn(left, right):
    return lax.dot_general(left, right, (((0,), (0,)), ((), ())), preferred_element_type=WIDE)


def each(count, step, first=0, unroll=1):
    def run(k, carry):
        step(k)
        return carry

    lax.fori_loop(first, first + count, run, 0, unroll=unroll)


def row_blocks(total, block, step):
    each(total // block, lambda k: step(pl.ds(pl.multiple_of(k * block, block), block)), unroll=2)


def row(ref, k):
    return ref[pl.ds(k, 1), :]


def flat(value):
    return value.reshape(-1, value.shape[-1])


def add_rows(ref, k, value):
    ref[pl.ds(k, 1), :] += jnp.sum(value.astype(WIDE), axis=0, keepdims=True)


def live_rows(block, wide):
    return lax.broadcasted_iota(jnp.int32, (block, wide), 0) % SET < VIS


def selection(slots, wide):
    rows = lax.broadcasted_iota(jnp.int32, (32, wide), 0)
    return (lax.broadcasted_iota(jnp.int32, (32, wide), 1) == rows + slots).astype(LOW)


def picks(index, wide):
    return (index == lax.broadcasted_iota(jnp.int32, (index.shape[0], wide), 1)).astype(LOW)


def fold_tables(model, rows, parts):
    entry = np.arange(model)
    source = rows * (entry // (parts * rows)) + entry % rows
    spots = (np.arange(model // parts)[:, None] == source[None, :]).astype(np.float32)
    column = entry % (parts * rows) // rows
    which = (np.arange(8)[:, None] == column[None, :]).astype(np.float32)
    return jnp.asarray(spots, LOW), jnp.asarray(which, WIDE)


class Buffers:
    def __init__(self, refs, sems):
        self.refs, self.sems, self.used = refs, sems, 0
        self.loading, self.saving = {}, []

    def __getitem__(self, name):
        if name in self.loading:
            self.loading.pop(name).wait()
        return self.refs[name]

    def copy(self, source, target):
        copy = pltpu.make_async_copy(source, target, self.sems.at[self.used])
        self.used += 1
        copy.start()
        return copy

    def load(self, name, source, target=None):
        self.loading[name] = self.copy(source, self.refs[name] if target is None else target)

    def wait(self, *names):
        for name in names:
            if name in self.loading:
                self.loading.pop(name).wait()

    def save(self, name, target):
        self.saving.append((name, self.copy(self.refs[name], target)))

    def saved(self, name):
        self.settle([entry for entry in self.saving if entry[0] == name])

    def settle(self, entries):
        for entry in entries:
            if any(entry is other for other in self.saving):
                entry[1].wait()
        self.saving = [other for other in self.saving if not any(other is entry for entry in entries)]

    def drain(self):
        for name in list(self.loading):
            self.loading.pop(name).wait()
        for _, copy in self.saving:
            copy.wait()


def call(body, ins, small, outs, scratch, sems, extra, name, collective, vmem):
    names = list(ins) + list(small) + list(outs) + list(scratch)

    def kernel(*refs):
        named = dict(zip(names, refs[: len(names)]))
        body(Buffers(named, refs[len(names)]), *refs[len(names) + 1 :])

    anywhere = pl.BlockSpec(memory_space=pl.ANY)
    results = pl.pallas_call(
        kernel,
        out_shape=list(outs.values()),
        in_specs=[anywhere] * len(ins) + [pl.BlockSpec(memory_space=pltpu.VMEM)] * len(small),
        out_specs=[anywhere] * len(outs),
        scratch_shapes=[pltpu.VMEM(*shape) for shape in scratch.values()]
        + [pltpu.SemaphoreType.DMA((sems,))]
        + extra,
        name=name,
        compiler_params=pltpu.CompilerParams(
            collective_id=collective, has_side_effects=True, vmem_limit_bytes=vmem
        ),
    )(*ins.values(), *small.values())
    return dict(zip(outs, results))


def norm_block(value, gain, shift):
    centered = value - jnp.mean(value, axis=-1, keepdims=True)
    inverse = lax.rsqrt(jnp.mean(centered * centered, axis=-1, keepdims=True) + 1e-06)
    normed = centered * inverse
    return normed * gain + shift, normed, inverse


def norm_back(value, grad, gain, sums, gain_row, shift_row):
    _, normed, inverse = norm_block(value, gain, 0.0)
    add_rows(sums, gain_row, grad * normed)
    add_rows(sums, shift_row, grad)
    scaled = grad * gain
    first = jnp.mean(scaled, axis=-1, keepdims=True)
    second = jnp.mean(scaled * normed, axis=-1, keepdims=True)
    return inverse * (scaled - first - normed * second)


def halves(value):
    low = lax.broadcasted_iota(jnp.int32, value.shape, 1) < HEAD_DIM
    zero = jnp.zeros_like(value)
    return jnp.concatenate([jnp.where(low, value, zero), jnp.where(low, zero, value)], axis=0)


def rejoin(value):
    rows = value.shape[0] // 2
    low = lax.broadcasted_iota(jnp.int32, (rows, value.shape[1]), 1) < HEAD_DIM
    return jnp.where(low, value[:rows], value[rows:])


def spot(k, pairs):
    return pl.ds(pl.multiple_of(k // pairs * SET, SET), SET), lanes(k % pairs * 128, 128)


def stacked(refs, at):
    parts = [ref[at[0], at[1]] for ref in refs]
    return parts[0] if len(parts) == 1 else jnp.concatenate(parts, axis=0)


def soft(keys, queries):
    scores = dot_nt(keys, queries) * (1.0 / math.sqrt(HEAD_DIM))
    scores = jnp.where(live_rows(*scores.shape), scores, -1e30)
    weighted = jnp.exp(scores - jnp.max(scores, axis=0, keepdims=True))
    return weighted / jnp.sum(weighted, axis=0, keepdims=True)


def in_pieces(count, piece, step, between):
    for first in range(0, count, piece):
        each(piece, step, first, piece)
        between()


def attend(queries, keys, values, mixed, between):
    pairs = queries.shape[1] // 128

    def step(k):
        at = spot(k, pairs)
        weights = soft(stacked(keys, at), halves(queries[at[0], at[1]])).astype(LOW)
        mixed[at[0], at[1]] = rejoin(dot_tn(weights, stacked(values, at))).astype(LOW)

    in_pieces(queries.shape[0] // SET * pairs, 4, step, between)


def attend_back(grad_mixed, queries, keys, values, grad_queries, grad_keys, grad_values, between):
    pairs = queries.shape[1] // 128
    factor = 1.0 / math.sqrt(HEAD_DIM)

    def step(k):
        at = spot(k, pairs)
        key, value = stacked(keys, at), stacked(values, at)
        query, grad = halves(queries[at[0], at[1]]), halves(grad_mixed[at[0], at[1]])
        weights = soft(key, query)
        back_value = dot_nn(weights.astype(LOW), grad).astype(LOW)
        grad_soft = dot_nt(value, grad)
        inner = jnp.sum(grad_soft * weights, axis=0, keepdims=True)
        grad_scores = (weights * (grad_soft - inner)).astype(LOW)
        back_key = (dot_nn(grad_scores, query) * factor).astype(LOW)
        grad_queries[at[0], at[1]] = (rejoin(dot_tn(grad_scores, key)) * factor).astype(LOW)
        for which in range(len(keys)):
            part = slice(which * SET, (which + 1) * SET)
            grad_keys[which][at[0], at[1]] = back_key[part]
            grad_values[which][at[0], at[1]] = back_value[part]

    in_pieces(queries.shape[0] // SET * pairs, 4, step, between)


def project(source, weight, start, bias, target):
    def step(k):
        part = lanes(k * TILE, TILE)
        value = dot_nn(source[...], flat(weight[:, :, :, lanes(start + k * TILE, TILE)]))
        if bias is not None:
            value = value + bias[:, part]
        target[:, part] = value.astype(LOW)

    each(target.shape[1] // TILE, step, unroll=3)


def residual(source, weight, bias, scale, before, after, branch, first, count):
    def step(k):
        part = lanes(k * TILE, TILE)
        value = dot_nn(source[...], flat(weight[:, :, :, part])) + bias[:, part]
        branch[:, part] = value.astype(LOW)
        after[:, part] = before[:, part] + scale[:, part] * value

    each(count, step, first, count)


def rise(source, weight, bias, active, slope, first, count):
    per = source.shape[1] // TILE

    def step(k):
        part = lanes(k * TILE, TILE)
        own = bias[pl.ds(k // per, 1), lanes(k % per * TILE, TILE)]
        value = dot_nn(source[...], flat(weight[:, :, :, part])) + own
        square = value * value
        curve = jnp.tanh(value * (ROOT + (ROOT * CUBE) * square))
        half = 0.5 + 0.5 * curve
        active[:, part] = (value * half).astype(LOW)
        bend = value * (half - half * curve) * (ROOT + (3.0 * ROOT * CUBE) * square)
        slope[:, part] = (half + bend).astype(LOW)

    each(count, step, first, count)


def small_vectors(b, parts):
    extra, vec = b[N.extra], b[N.vec]
    pick = selection(PATCHES, extra.shape[1])
    vec[...] = dot_nt(pick, extra[...])
    at = 16
    for count, spots, which in ((parts[0], b[N.spots_q], b[N.which_q]), (parts[1], b[N.spots_f], b[N.which_f])):
        rows = spots.shape[0]
        found = []
        for chunk in range(count):
            held = dot_nt(pick, extra[pl.ds(chunk * rows, rows), :]).astype(LOW)
            found.append(dot_nn(held, spots[...]))
        for block in range(2):
            for chunk in range(count):
                base = at + block * count
                total = sum(
                    found[chunk][base + j : base + j + 1] * which[j : j + 1, :] for j in range(count)
                )
                vec[base + chunk : base + chunk + 1, :] = total
        at += 2 * count


def forward_compute(b, need, spend, keep, release):
    rows, model = b[N.start].shape
    need(N.extra, 0, 0)
    b[N.extra][...] = flat(b[N.extra4][...])
    small_vectors(b, (2, 4))
    vec, extra = b[N.vec], b[N.extra]
    keep(N.vec)
    spend(2)

    def vector(k):
        return vec.at[pl.ds(k, 1)]

    def open_rows(r):
        wide = extra.shape[1]
        start = b[N.patches][r, :].astype(WIDE) + dot_nt(picks(b[N.vis][r, :], wide), extra[...])
        b[N.start][r, :] = start
        b[N.a0][r, :] = norm_block(start, row(vec, 0), row(vec, 4))[0].astype(LOW)
        query = dot_nt(picks(b[N.hid][r, :], wide), extra[...])
        b[N.query][r, :] = query
        b[N.aq][r, :] = norm_block(query, row(vec, 2), row(vec, 6))[0].astype(LOW)

    b[N.patches]
    row_blocks(rows, 64, open_rows)
    for name in (N.start, N.a0, N.query, N.aq):
        keep(name)
    spend(4)

    def norm_into(source, target, gain, shift):
        def step(r):
            b[target][r, :] = norm_block(b[source][r, :], row(vec, gain), row(vec, shift))[0].astype(LOW)

        row_blocks(rows, 64, step)
        keep(target)
        spend(1)

    def low_into(source, target):
        def step(r):
            b[target][r, :] = b[source][r, :].astype(LOW)

        row_blocks(rows, 64, step)
        keep(target)

    def attention(block, sources, keys, values, before, after):
        query, mixed, branch = N.q + str(block), N.mix + str(block), N.br + str(block)
        for part, bias in enumerate((16 + 2 * block, None, 17 + 2 * block)):
            need(N.qkv, block, part)
            targets = ([query], keys, values)[part]
            for source, target in zip(sources[part], targets):
                shift = None if bias is None else vector(bias)
                project(b[source], b[N.w_qkv], part * model, shift, b[target])
                keep(target)
                spend(1)
        release(N.qkv)
        attend(
            b[query], [b[name] for name in keys], [b[name] for name in values], b[mixed],
            lambda: spend(1.5),
        )
        keep(mixed)
        need(N.proj, block, 0)
        residual(
            b[mixed], b[N.w_proj], vector(12 + block), vector(8 + 2 * block), b[before], b[after], b[branch],
            0, model // TILE,
        )
        release(N.proj)
        keep(branch)
        keep(after)
        spend(1.2)

    def feed(block, before, after, inner):
        branch = N.fd + str(block)
        norm_into(before, inner, 2 * block + 1, 4 + 2 * block + 1)
        b.saved(N.active)
        b.saved(N.slope)
        hidden = b[N.active].shape[1]
        for piece in range(hidden // model):
            need(N.fc1, block, piece)
            rise(
                b[inner], b[N.w_fc1], vec.at[pl.ds(20 + 4 * block, 4)], b[N.active], b[N.slope],
                piece * (model // TILE), model // TILE,
            )
            spend(2.2)
        release(N.fc1)
        keep(N.active, block)
        keep(N.slope, block)
        for piece in range(model // TILE):
            need(N.fc2, block, piece)
            residual(
                b[N.active], b[N.w_fc2], vector(14 + block), vector(8 + 2 * block + 1), b[before], b[after],
                b[branch], piece, 1,
            )
            spend(1.3)
        release(N.fc2)
        keep(branch)

    attention(0, ([N.a0], [N.a0], [N.a0]), [N.k0], [N.v0], N.start, N.mid0)
    feed(0, N.mid0, N.lat, N.a20)
    keep(N.lat)
    low_into(N.lat, N.latent)
    norm_into(N.lat, N.ak, 2, 6)
    both = [N.ak, N.aq]
    attention(1, ([N.aq], both, both), [N.k1, N.k2], [N.v1, N.v2], N.query, N.mid1)
    feed(1, N.mid1, N.reg, N.a21)
    low_into(N.reg, N.regressed)


KEPT_WIDE = (N.start, N.query, N.mid0, N.lat, N.mid1)
KEPT_LOW = (
    N.a0, N.aq, N.a20, N.ak, N.a21, N.q0, N.k0, N.v0, N.mix0, N.br0, N.fd0,
    N.q1, N.k1, N.v1, N.k2, N.v2, N.mix1, N.br1, N.fd1, N.latent, N.regressed,
)


def shape_of(*args):
    return jax.ShapeDtypeStruct(*args)


def cut(shapes):
    model = shapes[N.proj][1]
    pieces = []
    for kind, wide in ((N.qkv, model), (N.proj, model), (N.fc1, model), (N.fc2, TILE)):
        pieces += [(kind, k, k * wide, wide) for k in range(shapes[kind][1] // wide)]
    return pieces


def forward(patches, vis, hid, extra_shard, weights, line, tables):
    rows, model = patches.shape
    kinds = (N.qkv, N.proj, N.fc1, N.fc2)
    shapes = {kind: (2 * weight.shape[1], weight.shape[2]) for kind, weight in zip(kinds, weights)}
    shapes[N.extra] = (2 * extra_shard.shape[0], extra_shard.shape[1])
    hidden = shapes[N.fc1][1]
    whole = {kind: (line, 4) + shape for kind, shape in shapes.items()}
    arrays = [(N.extra, 0)] + [(kind, block) for block in (0, 1) for kind in kinds]
    names = [kind + str(block) for kind, block in arrays]
    items = [(0, N.extra, 0, 0, 0, shapes[N.extra][1])]
    for block in (0, 1):
        for kind, piece, first, wide in cut(shapes):
            items.append((arrays.index((kind, block)), kind, block, piece, first, wide))
    outs = {name: shape_of(whole[kind], LOW) for name, (kind, _) in zip(names, arrays)}
    outs[N.vec_out] = shape_of((32, model), WIDE)
    for name in KEPT_WIDE:
        outs[name + N._out] = shape_of((rows, model), WIDE)
    for name in KEPT_LOW:
        outs[name + N._out] = shape_of((rows, model), LOW)
    for block in (0, 1):
        for name in (N.active, N.slope):
            outs[name + str(block) + N._out] = shape_of((rows, hidden), LOW)
    scratch = {name: ((rows, model), WIDE) for name in KEPT_WIDE + (N.reg,)}
    scratch.update({name: ((rows, model), LOW) for name in KEPT_LOW + (N.patches,)})
    scratch[N.active] = scratch[N.slope] = ((rows, hidden), LOW)
    scratch[N.vec] = ((32, model), WIDE)
    scratch[N.extra4] = (whole[N.extra], LOW)
    scratch[N.extra] = ((model, shapes[N.extra][1]), LOW)
    for kind in kinds:
        scratch[N.w_ + kind] = (whole[kind], LOW)
    for name, (kind, _) in zip(names, arrays):
        held = (shapes[kind][0] // 2, shapes[kind][1])
        scratch[N.own_ + name] = scratch[N.their_ + name] = (held, LOW)
    for i, (a, kind, _, _, _, wide) in enumerate(items):
        scratch[N.stage + str(i)] = ((shapes[kind][0], wide // 2), LOW)
    ins = {N.patches_in: patches, N.extra_in: extra_shard}
    ins.update({kind + N._in: weight for kind, weight in zip(kinds, weights)})
    small = {N.vis: vis, N.hid: hid}
    small.update(dict(zip((N.spots_q, N.which_q, N.spots_f, N.which_f), tables)))
    pairs = len(arrays) + len(items) * (line + 8)
    extra = [pltpu.SemaphoreType.DMA((pairs,)), pltpu.SemaphoreType.DMA((pairs,))]

    def body(b, send, recv):
        sources = [b[N.extra_in]] + [b[kind + N._in].at[block] for kind, block in arrays[1:]]
        b.load(N.own_ + names[0], sources[0])
        b.load(N.patches, b[N.patches_in])
        for name, source in list(zip(names, sources))[1:]:
            b.load(N.own_ + name, source)
        free, held, loaded = {(N.extra, 0)} | {(kind, 0) for kind in kinds}, [], {}

        def bring(i):
            a, kind, block, piece, first, wide = items[i]
            if (kind, block) not in free:
                held.append(i)
                return
            part = (slice(None),) * 3 + (pl.ds(first, wide),)
            target = b.refs[N.extra4 if kind == N.extra else N.w_ + kind].at[part]
            b.load(N.item + str(i), b[names[a]].at[part], target)
            loaded[(kind, block, piece)] = N.item + str(i)

        shards = [lambda name=name: b[N.own_ + name] for name in names]
        steps = gather_steps(
            line, [(a, shapes[kind][0], first, wide) for a, kind, _, _, first, wide in items], sources, shards,
            [b[N.their_ + name] for name in names], [b[name] for name in names],
            [b[N.stage + str(i)] for i in range(len(items))], send, recv, bring,
        )
        pace = Pace(steps)

        def need(kind, block, piece):
            pace.until(lambda: (kind, block, piece) in loaded)
            b.wait(loaded[(kind, block, piece)])

        def release(kind):
            free.add((kind, 1))
            for i in [i for i in held if items[i][1] == kind]:
                held.remove(i)
                bring(i)

        def keep(name, block=None):
            b.save(name, b[name + ("" if block is None else str(block)) + N._out])

        forward_compute(b, need, pace.spend, keep, release)
        pace.finish()
        b.drain()

    return call(body, ins, small, outs, scratch, 128, extra, N.forward, 0, 63 << 20)


class Reducer:
    def __init__(self, line, items, slots, grads, outs, shared, single, send, recv, credit, ended):
        self.line, self.items, self.slots = line, items, slots
        self.grads, self.outs, self.shared, self.single = grads, outs, shared, single
        self.credit, self.ended = credit, ended
        self.place = Place(line)
        self.copies = Copies(send, recv)
        self.place.greet()
        self.ready, self.begun, self.state = set(), {}, {}
        self.next, self.due = [0] * 5, {}
        self.now = self.link_free = self.line_free = 0.0
        self.sends = {i: [] for i in range(len(items))}
        self.steps = [self.pair, self.near, self.along, self.swap, self.finish]

    def remote(self, i, source, target, device):
        copy = self.copies.remote(source, target, device)
        self.sends[i].append(copy)
        return copy

    def unit(self, i):
        return self.line * self.items[i][0] * self.half(i) * 2

    def half(self, i):
        return self.items[i][2] // 2

    def columns(self, i, core):
        return lanes(self.items[i][1] + core * self.half(i), self.half(i))

    def earlier(self, i):
        return [j for j in range(i) if self.slots[j] == self.slots[i]]

    def later(self, i):
        return [j for j in range(i + 1, len(self.items)) if self.slots[j] == self.slots[i]]

    def buffers(self, i):
        mine, twins, owned, final, other = self.shared[self.slots[i]]
        through, direct, joined, arrived = self.single[i]
        return mine, twins, through, direct, joined, owned, arrived, final, other

    def begin(self, i):
        place = self.place
        mine, twins = self.buffers(i)[:2]
        if self.earlier(i):
            pl.semaphore_wait(self.credit.at[self.slots[i]], 1)
        away = self.remote(
            i, self.grads[i].at[:, :, :, self.columns(i, 1 - place.core)], twins, place.twin
        )
        here = self.copies.local(self.grads[i].at[:, :, :, self.columns(i, place.core)], mine)
        self.begun[i] = (away, here)
        self.due[0, i] = self.now + 2.0 + 4 * self.unit(i) / TWIN

    def begin_some(self):
        i = len(self.begun)
        while i < len(self.items) and i in self.ready and i <= self.next[0] + 2:
            if any(j >= self.next[4] for j in self.earlier(i)):
                return
            self.begin(i)
            i += 1

    def pair(self, i):
        place = self.place
        mine, twins, through, direct = self.buffers(i)[:4]
        away, here = self.begun[i]
        away.wait_recv()
        here.wait()

        def step(k):
            a, c = k // 4, k % 4
            mine[a, c] = mine[a, c] + twins[a, c]

        each(self.line * 4, step, unroll=2)
        self.state[i] = [
            self.remote(i, mine.at[:, place.across], through, place.far),
            self.remote(i, mine.at[:, place.second], direct, place.far),
        ]
        unit = self.unit(i) / LINK
        start = max(self.now, self.link_free)
        self.link_free = start + 3 * unit
        self.due[1, i] = start + 1.0 + 1.6 * unit
        self.now += 0.5 + self.unit(i) / 1e6

    def near(self, i):
        place = self.place
        mine, _, through, _, joined = self.buffers(i)[:5]
        self.state[i][0].wait_recv()

        def step(k):
            through[k] = through[k] + mine[k, place.first]

        each(self.line, step)
        self.state[i].append(self.remote(i, through, joined, place.near))
        self.due[2, i] = self.now + 1.0 + 1.6 * self.unit(i) / LINK
        self.now += 0.3

    def along(self, i):
        place, line = self.place, self.line
        mine, _, _, direct, joined, owned, arrived = self.buffers(i)[:7]
        self.state[i][1].wait_recv()
        self.state[i][2].wait_recv()

        def step(k):
            total = mine[k, place.own].astype(WIDE) + direct[k].astype(WIDE) + joined[k].astype(WIDE)
            owned[k] = total.astype(LOW)

        each(line, step)
        self.state[i] = [
            self.remote(
                i, owned.at[lax.rem(place.z + k + 1, line)], arrived.at[k], place.above[k]
            )
            for k in range(line - 1)
        ]
        start = max(self.now, self.line_free)
        self.line_free = start + 2 * self.unit(i) / LINK
        self.due[3, i] = self.line_free + 1.0
        self.now += 0.3

    def swap(self, i):
        place, rows = self.place, self.items[i][0] // 2
        owned, arrived, final, other = self.buffers(i)[5:]
        for copy in self.state[i]:
            copy.wait_recv()
        total = owned[place.z].astype(WIDE)
        for k in range(self.line - 1):
            total = total + arrived[k].astype(WIDE)
        final[...] = total
        away = pl.ds(pl.multiple_of((1 - place.core) * rows, 8), rows)
        self.state[i] = [self.remote(i, final.at[away], other, place.twin)]
        self.due[4, i] = self.now + 2.0
        self.now += 0.2

    def finish(self, i):
        place = self.place
        final, other = self.buffers(i)[7:]
        rows = self.items[i][0] // 2
        own = pl.ds(pl.multiple_of(place.core * rows, 8), rows)
        self.outs[i][:, self.columns(i, place.core)] = final[own]
        self.state[i][0].wait_recv()
        self.outs[i][:, self.columns(i, 1 - place.core)] = other[...]
        for copy in self.sends[i]:
            copy.wait_send()
        if self.later(i):
            pl.semaphore_signal(
                self.credit.at[self.slots[i]], inc=1, device_id=place.twin, device_id_type=MESH
            )
        self.ended(i)

    def able(self):
        found = []
        for stage in range(5):
            i = self.next[stage]
            if (i in self.begun) if stage == 0 else (i < self.next[stage - 1]):
                found.append((self.due[stage, i], -stage))
        return sorted(found)

    def run(self, stage):
        self.now = max(self.now, self.due[stage, self.next[stage]])
        self.steps[stage](self.next[stage])
        self.next[stage] += 1
        self.begin_some()

    def spend(self, time):
        self.now += time
        self.begin_some()
        while True:
            found = [entry for entry in self.able() if entry[0] <= self.now]
            if not found:
                return
            self.run(-found[0][1])

    def complete(self):
        self.begin_some()
        while self.next[4] < len(self.items):
            self.run(-self.able()[0][1])


def backward_compute(b, block, keys, spend, emit, bring):
    rows, model = b[N.acc].shape
    vec, sums = b[N.vec], b[N.sums]
    scale_row, feed_bias = 8 + 2 * block, 14 + block
    res, acc, gm, turned = b[N.res], b[N.acc], b[N.gm], b[N.turn]

    def close_rows(r):
        grad = res[r, :]
        if block:
            grad = jnp.where(live_rows(128, model), grad, 0.0)
            res[r, :] = grad
        add_rows(sums, scale_row + 1, grad * b[N.fd][r, :].astype(WIDE))
        low = (row(vec, scale_row + 1) * grad).astype(LOW)
        gm[r, :] = low
        add_rows(sums, feed_bias, low)

    b[N.fd]
    row_blocks(rows, 128, close_rows)
    if block:
        b.load(N.fd, b[N.ak_out])
    spend(2.5)

    def turn(value, start=0):
        turned[:, start : start + rows] = value.T

    def weight_grad(right, first, stage, depth):
        def step(k):
            value = dot_nn(turned[:, :depth], right[:, lanes(first + k * TILE, TILE)])
            shape = stage.shape[:-1] + (TILE,)
            stage[..., lanes(k * TILE, TILE)] = value.reshape(shape).astype(LOW)

        each(model // TILE, step, unroll=3)

    w_fc2, slope = b[N.w_fc2], b[N.slope]
    chunks = slope.shape[1] // model
    turn(b[N.inner][...])
    bring(N.inner)
    for chunk in range(chunks):
        part = slice(chunk * model, (chunk + 1) * model)

        def hidden_rows(r):
            value = dot_nt(gm[r, :], flat(w_fc2[chunk]))
            low = (value * slope[r, part].astype(WIDE)).astype(LOW)
            slope[r, part] = low
            add_rows(sums, 20 + 4 * block + chunk, low)

        row_blocks(rows, 256, hidden_rows)
        stage = N.stage + str(chunk % 2)
        b.saved(stage)
        weight_grad(slope, chunk * model, b[stage], rows)
        emit(N.fc1, chunk, stage)
        spend(3.2)
    bring(N.w_fc2)
    active = b[N.active]
    for chunk in range(chunks):
        turn(active[:, chunk * model : (chunk + 1) * model])
        b.saved(N.stage2)
        weight_grad(gm, 0, b[N.stage2], rows)
        emit(N.fc2, chunk, N.stage2)
        spend(2.2)
    bring(N.active)
    w_fc1 = b[N.w_fc1]
    for chunk in range(chunks):
        part = slice(chunk * model, (chunk + 1) * model)

        def inner_rows(r):
            value = dot_nt(slope[r, part], flat(w_fc1[:, :, :, part]))
            if chunk:
                value = acc[r, :] + value
            acc[r, :] = value

        row_blocks(rows, 256, inner_rows)
        spend(1.4)
    bring(N.slope)
    b.load(N.w_proj, b[N.w_ + N.proj + str(block)], w_fc1.at[:, :, :, 3 * model :])
    b.load(N.w_qkv, b[N.w_ + N.qkv + str(block)], w_fc1.at[:, :, :, : 3 * model])
    branch = b[N.br]

    def middle_rows(r):
        back = norm_back(
            b[N.mid][r, :], acc[r, :], row(vec, 2 * block + 1), sums, 2 * block + 1, 4 + 2 * block + 1
        )
        grad = res[r, :] + back
        res[r, :] = grad
        add_rows(sums, scale_row, grad * branch[r, :].astype(WIDE))
        low = (row(vec, scale_row) * grad).astype(LOW)
        gm[r, :] = low
        add_rows(sums, 12 + block, low)

    b[N.mid]
    row_blocks(rows, 64, middle_rows)
    b.load(N.mid, b[N.query_out if block else N.start_out])
    bring(N.br)
    spend(3)
    turn(b[N.mix][...])
    b.saved(N.stage0)
    weight_grad(gm, 0, b[N.stage0], rows)
    emit(N.proj, 0, N.stage0)
    spend(2.2)
    b.wait(N.w_proj)
    w_qkv, w_proj = w_fc1.at[:, :, :, : 3 * model], w_fc1.at[:, :, :, 3 * model :]

    def mixed_rows(r):
        b[N.mix][r, :] = dot_nt(gm[r, :], flat(w_proj[...])).astype(LOW)

    row_blocks(rows, 256, mixed_rows)
    spend(1.2)
    query, key, value = b[N.query], b[N.key], b[N.value]
    b.wait(N.key2, N.value2)
    queries = b[N.aq]
    key_parts = [key.at[pl.ds(k * rows, rows)] for k in range(keys)]
    value_parts = [value.at[pl.ds(k * rows, rows)] for k in range(keys)]
    attend_back(
        b[N.mix], query, key_parts, value_parts, query, key_parts, value_parts,
        lambda: spend(1.7 + 0.5 * keys),
    )
    bring(N.mix)

    def bias_rows(r):
        add_rows(sums, 16 + 2 * block, query[r, :])
        for k in range(keys):
            add_rows(sums, 17 + 2 * block, value_parts[k][r, :])

    row_blocks(rows, 128, bias_rows)
    if block:
        turn(b[N.fd][...])
        turn(queries[...], rows)
        bring(N.fd)
    else:
        turn(queries[...])
    depth = pl.ds(0, keys * rows)
    for chunk, right in ((1, key.at[depth]), (2, value.at[depth])):
        stage = N.stage + str(chunk % 2)
        b.saved(stage)
        weight_grad(right, 0, b[stage], keys * rows)
        emit(N.qkv, chunk, stage)
        spend(1 + 1.3 * keys)
    if block:
        turn(queries[...])
    bring(N.aq)
    b.saved(N.stage1)
    weight_grad(query, 0, b[N.stage1], rows)
    emit(N.qkv, 0, N.stage1)
    spend(2.2)
    b.wait(N.w_qkv)

    def back(parts):
        def step(r):
            total = 0.0
            for ref, chunk in parts:
                total = total + dot_nt(ref[r, :], flat(w_qkv[:, :, :, chunk * model : (chunk + 1) * model]))
            acc[r, :] = total

        row_blocks(rows, 256, step)

    gain, shift = 2 * block, 4 + 2 * block
    back([(query, 0), (key_parts[keys - 1], 1), (value_parts[keys - 1], 2)])
    spend(3.3)
    b[N.mid]

    def start_rows(r):
        grad = res[r, :] + norm_back(b[N.mid][r, :], acc[r, :], row(vec, gain), sums, gain, shift)
        res[r, :] = grad
        gm[r, :] = grad.astype(LOW)

    row_blocks(rows, 64, start_rows)
    if block:
        b.load(N.mid, b[N.lat_out])
        b.load(N.res, b[N.grad_latent])
    spend(2.5)
    place = b[N.hid if block else N.vis]
    table = dot_tn(gm[...], picks(place[...], b[N.table].shape[1]))
    if block:
        b[N.table][...] = table
        back([(key_parts[0], 1), (value_parts[0], 2)])
        bring(N.query, N.key, N.value, N.w_fc1)
        spend(3)
        b[N.mid], b[N.res]

        def latent_pair(k):
            for part in range(2):
                r = pl.ds(pl.multiple_of(k * SET + part * 64, 64), 64)
                grad = res[r, :]
                live = lax.broadcasted_iota(jnp.int32, grad.shape, 0) + part * 64 < VIS
                res[r, :] = jnp.where(live, grad, 0.0) + norm_back(
                    b[N.mid][r, :], acc[r, :], row(vec, gain), sums, gain, shift
                )

        each(rows // SET, latent_pair)
        bring(N.mid)
        spend(2.5)
    else:
        b[N.table][...] += table


def table_of_sums(b, parts):
    table, sums = b[N.table], b[N.sums]
    pick = selection(PATCHES, table.shape[1])
    plain = lax.broadcasted_iota(jnp.int32, sums.shape, 0) < 16
    table[...] += dot_tn(jnp.where(plain, sums[...], 0.0).astype(LOW), pick)
    at = 16
    lines = lax.broadcasted_iota(jnp.int32, sums.shape, 0)
    for count, spots, which in ((parts[0], b[N.spots_q], b[N.which_q]), (parts[1], b[N.spots_f], b[N.which_f])):
        rows = spots.shape[0]
        for chunk in range(count):
            spread = jnp.zeros(sums.shape, WIDE)
            for block in range(2):
                base = at + block * count
                for j in range(count):
                    entry = sums[base + chunk : base + chunk + 1, :] * which[j : j + 1, :]
                    spread = spread + jnp.where(lines == base + j, entry, 0.0)
            held = dot_nt(spots[...], spread.astype(LOW)).astype(LOW)
            table[pl.ds(chunk * rows, rows), :] += dot_nn(held, pick)
        at += 2 * count


HELD = (
    {
        N.fd: N.fd0, N.active: N.active0, N.slope: N.slope0, N.inner: N.a20, N.mid: N.mid0, N.br: N.br0,
        N.mix: N.mix0, N.query: N.q0, N.key: N.k0, N.value: N.v0, N.aq: N.a0,
    },
    {
        N.fd: N.fd1, N.active: N.active1, N.slope: N.slope1, N.inner: N.a21, N.mid: N.mid1, N.br: N.br1,
        N.mix: N.mix1, N.query: N.q1, N.key: N.k1, N.value: N.v1, N.aq: N.aq,
    },
)


def backward(f, grad_out, grad_latent, vis, hid, line, tables):
    rows, model = f[N.mid0_out].shape
    hidden = f[N.active0_out].shape[1]
    wide = f[N.extra0].shape[3]
    shapes = {
        N.fc2: (hidden // (4 * line), model),
        N.fc1: (model // (4 * line), hidden),
        N.proj: (model // (4 * line), model),
        N.qkv: (model // (4 * line), 3 * model),
        N.extra: (model // (4 * line), wide),
    }
    whole = {kind: (line, 4) + shape for kind, shape in shapes.items()}
    pieces = {kind: [] for kind in shapes}
    for kind, piece, first, columns in cut(shapes):
        pieces[kind].append((piece, first, columns))
    pieces[N.extra] = [(0, 0, wide)]
    pieces[N.qkv] = pieces[N.qkv][1:] + pieces[N.qkv][:1]
    made = [N.fc1, N.fc2, N.proj, N.qkv]
    order_of = [(kind, block) for block in (1, 0) for kind in made] + [(N.extra, 0)]
    items, owners, counts, slots = [], [], {}, []
    for kind, block in order_of:
        for piece, first, columns in pieces[kind]:
            items.append((shapes[kind][0], first, columns))
            owners.append((kind, block, piece))
            shape = (shapes[kind][0], columns // 2)
            counts[shape] = counts.get(shape, 0) + 1
            slots.append((shape, (counts[shape] - 1) % (3 if kind == N.fc2 else 4)))
    held = sorted(set(slots))
    slots = [held.index(slot) for slot in slots]
    ins = {N.res_in: grad_out, N.grad_latent: grad_latent}
    for name in (N.query, N.start, N.lat, N.k2, N.v2, N.ak, N.vec):
        ins[name + N._out] = f[name + N._out]
    for block in (1, 0):
        for kind in made:
            ins[N.w_ + kind + str(block)] = f[kind + str(block)]
        for source in HELD[block].values():
            ins[N.in_ + source] = f[source + N._out]
    small = {N.vis: vis, N.hid: hid}
    small.update(dict(zip((N.spots_q, N.which_q, N.spots_f, N.which_f), tables)))
    outs = {N.g_ + kind + str(block): shape_of(whole[kind], LOW) for kind, block in order_of}
    for kind in made:
        outs[N.out_ + kind] = shape_of((2, shapes[kind][0] // 2, shapes[kind][1]), WIDE)
    outs[N.out_extra] = shape_of((shapes[N.extra][0] // 2, wide), WIDE)
    outs[N.res_out] = shape_of((rows, model), WIDE)
    scratch = {name: ((rows, model), WIDE) for name in (N.res, N.acc, N.mid)}
    for name in (N.fd, N.inner, N.br, N.mix, N.query, N.gm, N.aq):
        scratch[name] = ((rows, model), LOW)
    scratch[N.key] = scratch[N.value] = ((2 * rows, model), LOW)
    scratch[N.turn] = ((model, 2 * rows), LOW)
    scratch[N.active] = scratch[N.slope] = ((rows, hidden), LOW)
    scratch[N.w_fc1], scratch[N.w_fc2] = (whole[N.fc1], LOW), (whole[N.fc2], LOW)
    scratch[N.stage0] = scratch[N.stage1] = (whole[N.proj], LOW)
    scratch[N.stage2] = (whole[N.fc2][1:], LOW)
    scratch[N.vec] = scratch[N.sums] = ((32, model), WIDE)
    scratch[N.table] = ((model, wide), WIDE)
    scratch[N.table4] = (whole[N.extra], LOW)
    for kind, block in order_of:
        scratch[N.shard_ + kind + str(block)] = ((shapes[kind][0] // 2, shapes[kind][1]), WIDE)
    extra = []
    for (r, half), _ in held:
        extra += [pltpu.VMEM((line, 4, r, half), LOW)] * 2
        extra += [pltpu.VMEM((line, r, half), LOW), pltpu.VMEM((r, half), WIDE)]
        extra += [pltpu.VMEM((r // 2, half), WIDE)]
    for r, _, columns in items:
        half = columns // 2
        extra += [pltpu.VMEM((line, r, half), LOW)] * 3 + [pltpu.VMEM((line - 1, r, half), LOW)]
    pairs = len(items) * (line + 5)
    extra += [pltpu.SemaphoreType.DMA((pairs,))] * 2 + [pltpu.SemaphoreType.REGULAR((len(held),))]

    def body(b, *refs):
        shared = [refs[5 * k : 5 * k + 5] for k in range(len(held))]
        rest = refs[5 * len(held) :]
        single = [rest[4 * k : 4 * k + 4] for k in range(len(items))]
        send, recv, credit = rest[-3:]

        def fetch(name, block):
            if name in (N.w_fc1, N.w_fc2):
                b.load(name, b[name + str(block)])
            elif name in (N.key, N.value):
                b.load(name, b[N.in_ + HELD[block][name]], b.refs[name].at[pl.ds(0, rows)])
            else:
                b.load(name, b[N.in_ + HELD[block][name]])

        b.load(N.res, b[N.res_in])
        fetch(N.fd, 1)
        b.load(N.vec, b[N.vec_out])
        for name in (N.inner, N.w_fc2, N.slope, N.active, N.w_fc1, N.mid, N.br, N.mix, N.query, N.key, N.value, N.aq):
            fetch(name, 1)
        b.load(N.key2, b[N.k2_out], b.refs[N.key].at[pl.ds(rows, rows)])
        b.load(N.value2, b[N.v2_out], b.refs[N.value].at[pl.ds(rows, rows)])
        b[N.sums][...] = jnp.zeros(b[N.sums].shape, WIDE)
        left = {}
        for kind, block, _ in owners:
            left[kind, block] = left.get((kind, block), 0) + 1

        def ended(i):
            kind, block, _ = owners[i]
            left[kind, block] -= 1
            if left[kind, block] == 0:
                out = b[N.out_ + kind]
                b.save(N.shard_ + kind + str(block), out if kind == N.extra else out.at[block])

        reducer = Reducer(
            line, items, slots, [b[N.g_ + kind + str(block)] for kind, block, _ in owners],
            [b[N.shard_ + kind + str(block)] for kind, block, _ in owners],
            shared, single, send, recv, credit, ended,
        )
        waiting, fresh = [], [0]

        def settle(count):
            for _ in range(count):
                kind, block, chunk, entry = waiting.pop(0)
                b.settle([entry])
                for i, owner in enumerate(owners):
                    if owner[:2] == (kind, block):
                        if chunk == (hidden // model - 1 if kind == N.fc2 else owner[2]):
                            reducer.ready.add(i)

        def spend(time):
            settle(len(waiting) - fresh[0])
            reducer.spend(time)
            fresh[0] = 0

        def emitter(block):
            def emit(kind, chunk, stage):
                out = b[N.g_ + kind + str(block)]
                target = out.at[chunk] if kind == N.fc2 else out
                if kind in (N.fc1, N.qkv):
                    target = out.at[:, :, :, pl.ds(chunk * model, model)]
                b.save(stage, target)
                waiting.append((kind, block, chunk, b.saving[-1]))
                fresh[0] += 1

            return emit

        def bring(*names):
            for name in names:
                fetch(name, 0)

        b[N.res]
        backward_compute(b, 1, 2, spend, emitter(1), bring)
        backward_compute(b, 0, 1, spend, emitter(0), lambda *names: None)
        b.save(N.res, b[N.res_out])
        table_of_sums(b, (2, 4))
        b[N.table4][...] = b[N.table][...].astype(LOW).reshape(b[N.table4].shape)
        emitter(0)(N.extra, 0, N.table4)
        settle(len(waiting))
        reducer.complete()
        b.drain()

    return call(body, ins, small, outs, scratch, 128, extra, N.backward, 1, 64 << 20)


def pack(pos, ln_gain, ln_bias, scales, b_proj, b_fc2, b_qkv, b_fc1):
    rows = pos.shape[1]

    def turned(array):
        return jnp.moveaxis(array.reshape(-1, array.shape[-1]), 1, 0)

    def folded(array):
        return turned(array.reshape(2, -1, rows))

    columns = [turned(pos), turned(ln_gain), turned(ln_bias), turned(scales)]
    columns += [turned(b_proj), turned(b_fc2), folded(b_qkv), folded(b_fc1)]
    joined = jnp.concatenate([column.astype(LOW) for column in columns], axis=1)
    return jnp.pad(joined, ((0, 0), (0, 256 - joined.shape[1])))


def unpack_rows(extra, patches, devices, fold):
    at = patches
    turned = extra.T
    pos = turned[:patches]
    outs = []
    for _ in range(3):
        outs.append(turned[at : at + 4].reshape(2, 2, -1))
        at += 4
    for _ in range(2):
        outs.append(turned[at : at + 2])
        at += 2
    for pieces in fold:
        part = turned[at : at + 2 * pieces].reshape(2, pieces, devices, -1)
        outs.append(jnp.swapaxes(part, 1, 2).reshape(2, -1))
        at += 2 * pieces
    return [pos] + outs


def fused(
    devices, patches, order, grad_latent, grad_out, pos_embed, ln_gain, ln_bias, w_qkv, b_qkv, w_proj, b_proj,
    w_fc1, b_fc1, w_fc2, b_fc2, layer_scale,
):
    line = devices // 8
    model = patches.shape[1]
    own = pos_embed.shape[1]

    def places(index):
        return jnp.pad(index, ((0, 0), (0, SET - VIS)), constant_values=-1).reshape(-1, 1)

    vis, hid = places(order[:, :VIS]), places(order[:, VIS:])
    extra = pack(pos_embed, ln_gain, ln_bias, layer_scale, b_proj, b_fc2, b_qkv, b_fc1)
    fold = (b_qkv.shape[1] // own, b_fc1.shape[1] // own)
    tables = fold_tables(model, own, fold[0]) + fold_tables(model, own, fold[1])
    kept = forward(patches, vis, hid, extra, (w_qkv, w_proj, w_fc1, w_fc2), line, tables)
    made = backward(kept, grad_out, grad_latent, vis, hid, line, tables)
    pos_shard, gains, shifts, scales, proj_b, fc2_b, qkv_b, fc1_b = unpack_rows(
        made[N.out_extra], PATCHES, 1, fold
    )
    return (
        kept[N.latent_out], kept[N.regressed_out], made[N.res_out], pos_shard,
        gains, shifts, made[N.out_qkv], qkv_b, made[N.out_proj], proj_b,
        made[N.out_fc1], fc1_b, made[N.out_fc2], fc2_b, scales,
    )


def norm_forward(value, gain, shift):
    center = jnp.mean(value, axis=-1, keepdims=True)
    centered = value - center
    inverse = lax.rsqrt(jnp.mean(centered * centered, axis=-1, keepdims=True) + 1e-06)
    normed = centered * inverse
    return (normed * gain + shift, normed, inverse)


def norm_backward(grad, normed, inverse, gain):
    scaled = grad * gain
    first_mean = jnp.mean(scaled, axis=-1, keepdims=True)
    second_mean = jnp.mean(scaled * normed, axis=-1, keepdims=True)
    back = inverse * (scaled - first_mean - normed * second_mean)
    return (back, jnp.sum(grad * normed, axis=0), jnp.sum(grad, axis=0))


def unpack(pieces):
    gains, shifts, w_qkv, b_qkv, w_proj, b_proj, w_fc1, b_fc1, w_fc2, b_fc2, scales = pieces
    wide = jnp.float32
    return (
        gains.astype(wide),
        shifts.astype(wide),
        w_qkv,
        b_qkv.astype(wide),
        w_proj,
        b_proj.astype(wide),
        w_fc1,
        b_fc1.astype(wide),
        w_fc2,
        b_fc2.astype(wide),
        scales.astype(wide),
    )


def fetch(block, arrays):
    ln_gain, ln_bias, w_qkv, b_qkv, w_proj, b_proj, w_fc1, b_fc1, w_fc2, b_fc2, layer_scale = arrays
    gathered = (
        lax.all_gather(ln_gain[block], ("dp", "fsdp"), axis=1, tiled=True),
        lax.all_gather(ln_bias[block], ("dp", "fsdp"), axis=1, tiled=True),
        lax.all_gather(w_qkv[block], ("dp", "fsdp"), axis=0, tiled=True),
        lax.all_gather(b_qkv[block], ("dp", "fsdp"), axis=0, tiled=True),
        lax.all_gather(w_proj[block], ("dp", "fsdp"), axis=0, tiled=True),
        lax.all_gather(b_proj[block], ("dp", "fsdp"), axis=0, tiled=True),
        lax.all_gather(w_fc1[block], ("dp", "fsdp"), axis=0, tiled=True),
        lax.all_gather(b_fc1[block], ("dp", "fsdp"), axis=0, tiled=True),
        lax.all_gather(w_fc2[block], ("dp", "fsdp"), axis=0, tiled=True),
        lax.all_gather(b_fc2[block], ("dp", "fsdp"), axis=0, tiled=True),
        lax.all_gather(layer_scale[block], ("dp", "fsdp"), axis=1, tiled=True),
    )
    return unpack(gathered)


def column_sum(value):
    return jnp.sum(value.astype(jnp.float32), axis=0)


def outer_rows(left, right):
    return jnp.einsum("rd,rf->df", left, right, preferred_element_type=jnp.float32)


def attend_scores(queries, keys, key_live):
    scores = jnp.einsum("gqhe,gkhe->ghqk", queries, keys, preferred_element_type=jnp.float32) * (
        1.0 / math.sqrt(HEAD_DIM)
    )
    return jnp.where(key_live, scores, -1e30)


def attend_forward(query_in, key_in, images, key_live, weights):
    w_qkv, b_qkv, w_proj, b_proj = (weights[2], weights[3], weights[4], weights[5])
    model = query_in.shape[1]
    heads = model // HEAD_DIM
    queries = (
        jnp.dot(query_in, w_qkv[:, :model], preferred_element_type=jnp.float32) + b_qkv[:model]
    ).astype(jnp.bfloat16)
    paired = jnp.dot(key_in, w_qkv[:, model:], preferred_element_type=jnp.float32)
    keys = paired[:, :model].astype(jnp.bfloat16).reshape(images, -1, heads, HEAD_DIM)
    values = (
        (paired[:, model:] + b_qkv[model:])
        .astype(jnp.bfloat16)
        .reshape(images, -1, heads, HEAD_DIM)
    )
    queries = queries.reshape(images, -1, heads, HEAD_DIM)
    scores = attend_scores(queries, keys, key_live)
    highest_score = jnp.max(scores, axis=-1, keepdims=True)
    weighted = jnp.exp(scores - highest_score)
    summed = jnp.sum(weighted, axis=-1, keepdims=True)
    softmax_out = (weighted / summed).astype(jnp.bfloat16)
    mixed = jnp.einsum("ghqk,gkhe->gqhe", softmax_out, values, preferred_element_type=jnp.float32)
    mixed = mixed.reshape(-1, model).astype(jnp.bfloat16)
    branch = jnp.dot(mixed, w_proj, preferred_element_type=jnp.float32) + b_proj
    return (branch, (queries, keys, values, highest_score + jnp.log(summed), mixed))


def attend_backward(grad_branch, query_in, key_in, key_live, kept, weights):
    w_qkv, w_proj = (weights[2], weights[4])
    queries, keys, values, log_total, mixed = kept
    model = query_in.shape[1]
    grad_low = grad_branch.astype(jnp.bfloat16)
    grad_w_proj = outer_rows(mixed, grad_low)
    grad_b_proj = column_sum(grad_low)
    grad_mixed = (
        jnp.dot(grad_low, w_proj.T, preferred_element_type=jnp.float32)
        .astype(jnp.bfloat16)
        .reshape(queries.shape)
    )
    softmax_out = jnp.exp(attend_scores(queries, keys, key_live) - log_total)
    grad_values = jnp.einsum(
        "ghqk,gqhe->gkhe",
        softmax_out.astype(jnp.bfloat16),
        grad_mixed,
        preferred_element_type=jnp.float32,
    )
    grad_soft = jnp.einsum(
        "gqhe,gkhe->ghqk", grad_mixed, values, preferred_element_type=jnp.float32
    )
    grad_scores = (
        softmax_out * (grad_soft - jnp.sum(grad_soft * softmax_out, axis=-1, keepdims=True))
    ).astype(jnp.bfloat16)
    factor = 1.0 / math.sqrt(HEAD_DIM)
    grad_queries = (
        (
            jnp.einsum("ghqk,gkhe->gqhe", grad_scores, keys, preferred_element_type=jnp.float32)
            * factor
        )
        .astype(jnp.bfloat16)
        .reshape(-1, model)
    )
    grad_keys = (
        (
            jnp.einsum("ghqk,gqhe->gkhe", grad_scores, queries, preferred_element_type=jnp.float32)
            * factor
        )
        .astype(jnp.bfloat16)
        .reshape(-1, model)
    )
    grad_values = grad_values.astype(jnp.bfloat16).reshape(-1, model)
    grad_pairs = jnp.concatenate([grad_keys, grad_values], axis=1)
    grad_w_qkv = jnp.concatenate(
        [outer_rows(query_in, grad_queries), outer_rows(key_in, grad_pairs)], axis=1
    )
    grad_b_qkv = jnp.concatenate([column_sum(grad_queries), column_sum(grad_values)])
    grad_query_in = jnp.dot(grad_queries, w_qkv[:, :model].T, preferred_element_type=jnp.float32)
    grad_key_in = jnp.dot(grad_pairs, w_qkv[:, model:].T, preferred_element_type=jnp.float32)
    return (grad_query_in, grad_key_in, (grad_w_qkv, grad_b_qkv, grad_w_proj, grad_b_proj))


def feed_forward(middle, weights):
    gains, shifts, w_fc1, b_fc1, w_fc2, b_fc2 = (
        weights[0],
        weights[1],
        weights[6],
        weights[7],
        weights[8],
        weights[9],
    )
    normed_out, normed, inverse = norm_forward(middle, gains[1], shifts[1])
    inner_in = normed_out.astype(jnp.bfloat16)
    hidden = jnp.dot(inner_in, w_fc1, preferred_element_type=jnp.float32) + b_fc1
    active = jax.nn.gelu(hidden, approximate=True).astype(jnp.bfloat16)
    branch = jnp.dot(active, w_fc2, preferred_element_type=jnp.float32) + b_fc2
    return (branch, (normed, inverse, inner_in, hidden, active))


def feed_backward(grad_branch, kept, weights):
    gains, w_fc1, w_fc2 = (weights[0], weights[6], weights[8])
    normed, inverse, inner_in, hidden, active = kept
    grad_low = grad_branch.astype(jnp.bfloat16)
    grad_w_fc2 = outer_rows(active, grad_low)
    grad_b_fc2 = column_sum(grad_low)
    grad_active = jnp.dot(grad_low, w_fc2.T, preferred_element_type=jnp.float32)
    gelu_back = jax.vjp(functools.partial(jax.nn.gelu, approximate=True), hidden)[1]
    grad_hidden = gelu_back(grad_active)[0].astype(jnp.bfloat16)
    grad_w_fc1 = outer_rows(inner_in, grad_hidden)
    grad_b_fc1 = column_sum(grad_hidden)
    grad_normed = jnp.dot(grad_hidden, w_fc1.T, preferred_element_type=jnp.float32)
    grad_middle, grad_gain, grad_shift = norm_backward(grad_normed, normed, inverse, gains[1])
    return (grad_middle, grad_gain, grad_shift, (grad_w_fc1, grad_b_fc1, grad_w_fc2, grad_b_fc2))


def local(
    patches,
    order,
    grad_latent,
    grad_out,
    pos_embed,
    ln_gain,
    ln_bias,
    w_qkv,
    b_qkv,
    w_proj,
    b_proj,
    w_fc1,
    b_fc1,
    w_fc2,
    b_fc2,
    layer_scale,
):
    arrays = (
        ln_gain,
        ln_bias,
        w_qkv,
        b_qkv,
        w_proj,
        b_proj,
        w_fc1,
        b_fc1,
        w_fc2,
        b_fc2,
        layer_scale,
    )
    images = order.shape[0]
    model = patches.shape[1]
    highest = lax.Precision.HIGHEST
    live = jnp.arange(SET) < VIS
    live_rows = jnp.tile(live, images).astype(jnp.float32)[:, None]
    patch_slots = jnp.arange(PATCHES)

    def picker(index):
        padded = jnp.pad(index, ((0, 0), (0, SET - VIS)))
        chosen = (padded[:, :, None] == patch_slots[None, None, :]) & live[None, :, None]
        return chosen.astype(jnp.float32).reshape(-1, PATCHES)

    pick_visible = picker(order[:, :VIS])
    pick_masked = picker(order[:, VIS:])
    pos_table = lax.all_gather(pos_embed, ("dp", "fsdp"), axis=1, tiled=True).astype(jnp.float32)
    enc_weights, reg_weights = fetch(0, arrays), fetch(1, arrays)
    start = patches.astype(jnp.float32) + jnp.dot(pick_visible, pos_table, precision=highest)
    enc_out, enc_normed, enc_inverse = norm_forward(start, enc_weights[0][0], enc_weights[1][0])
    enc_attn_in = enc_out.astype(jnp.bfloat16)
    enc_branch, enc_attn_kept = attend_forward(enc_attn_in, enc_attn_in, images, live, enc_weights)
    enc_middle = start + enc_weights[10][0] * enc_branch
    enc_feed, enc_feed_kept = feed_forward(enc_middle, enc_weights)
    latent_f = enc_middle + enc_weights[10][1] * enc_feed
    query_start = jnp.dot(pick_masked, pos_table, precision=highest)
    query_out, query_normed, query_inverse = norm_forward(
        query_start, reg_weights[0][0], reg_weights[1][0]
    )
    latent_out, latent_normed, latent_inverse = norm_forward(
        latent_f, reg_weights[0][0], reg_weights[1][0]
    )
    query_in = query_out.astype(jnp.bfloat16)
    key_in = jnp.concatenate(
        [
            latent_out.astype(jnp.bfloat16).reshape(images, SET, model),
            query_in.reshape(images, SET, model),
        ],
        axis=1,
    ).reshape(-1, model)
    key_live = jnp.concatenate([live, live])
    reg_branch, reg_attn_kept = attend_forward(query_in, key_in, images, key_live, reg_weights)
    reg_middle = query_start + reg_weights[10][0] * reg_branch
    reg_feed, reg_feed_kept = feed_forward(reg_middle, reg_weights)
    regressed_f = reg_middle + reg_weights[10][1] * reg_feed
    reg_back = reg_weights
    grad_final = grad_out * live_rows
    reg_scale_late = jnp.sum(grad_final * reg_feed, axis=0)
    grad_from_feed, reg_gain_late, reg_shift_late, reg_feed_grads = feed_backward(
        reg_back[10][1] * grad_final, reg_feed_kept, reg_back
    )
    grad_reg_middle = grad_final + grad_from_feed
    reg_scale_early = jnp.sum(grad_reg_middle * reg_branch, axis=0)
    grad_query_in, grad_key_in, reg_attn_grads = attend_backward(
        reg_back[10][0] * grad_reg_middle, query_in, key_in, key_live, reg_attn_kept, reg_back
    )
    grad_key_in = grad_key_in.reshape(images, 2 * SET, model)
    grad_query_norm = grad_query_in + grad_key_in[:, SET:].reshape(-1, model)
    grad_latent_norm = grad_key_in[:, :SET].reshape(-1, model)
    back_query, reg_gain_query, reg_shift_query = norm_backward(
        grad_query_norm, query_normed, query_inverse, reg_back[0][0]
    )
    back_latent, reg_gain_key, reg_shift_key = norm_backward(
        grad_latent_norm, latent_normed, latent_inverse, reg_back[0][0]
    )
    grad_query_start = grad_reg_middle + back_query
    reg_grads = (
        (
            jnp.stack([reg_gain_query + reg_gain_key, reg_gain_late]),
            jnp.stack([reg_shift_query + reg_shift_key, reg_shift_late]),
        )
        + reg_attn_grads
        + reg_feed_grads
        + (jnp.stack([reg_scale_early, reg_scale_late]),)
    )
    enc_back = enc_weights
    grad_finish = grad_latent * live_rows + back_latent
    enc_scale_late = jnp.sum(grad_finish * enc_feed, axis=0)
    grad_from_feed, enc_gain_late, enc_shift_late, enc_feed_grads = feed_backward(
        enc_back[10][1] * grad_finish, enc_feed_kept, enc_back
    )
    grad_enc_middle = grad_finish + grad_from_feed
    enc_scale_early = jnp.sum(grad_enc_middle * enc_branch, axis=0)
    grad_as_query, grad_as_key, enc_attn_grads = attend_backward(
        enc_back[10][0] * grad_enc_middle, enc_attn_in, enc_attn_in, live, enc_attn_kept, enc_back
    )
    back_start, enc_gain_early, enc_shift_early = norm_backward(
        grad_as_query + grad_as_key, enc_normed, enc_inverse, enc_back[0][0]
    )
    grad_start = grad_enc_middle + back_start
    grad_table = jnp.dot(pick_visible.T, grad_start, precision=highest) + jnp.dot(
        pick_masked.T, grad_query_start, precision=highest
    )
    enc_grads = (
        (jnp.stack([enc_gain_early, enc_gain_late]), jnp.stack([enc_shift_early, enc_shift_late]))
        + enc_attn_grads
        + enc_feed_grads
        + (jnp.stack([enc_scale_early, enc_scale_late]),)
    )
    reg_shards = (
        lax.psum_scatter(reg_grads[0], ("dp", "fsdp"), scatter_dimension=1, tiled=True),
        lax.psum_scatter(reg_grads[1], ("dp", "fsdp"), scatter_dimension=1, tiled=True),
        lax.psum_scatter(reg_grads[2], ("dp", "fsdp"), scatter_dimension=0, tiled=True),
        lax.psum_scatter(reg_grads[3], ("dp", "fsdp"), scatter_dimension=0, tiled=True),
        lax.psum_scatter(reg_grads[4], ("dp", "fsdp"), scatter_dimension=0, tiled=True),
        lax.psum_scatter(reg_grads[5], ("dp", "fsdp"), scatter_dimension=0, tiled=True),
        lax.psum_scatter(reg_grads[6], ("dp", "fsdp"), scatter_dimension=0, tiled=True),
        lax.psum_scatter(reg_grads[7], ("dp", "fsdp"), scatter_dimension=0, tiled=True),
        lax.psum_scatter(reg_grads[8], ("dp", "fsdp"), scatter_dimension=0, tiled=True),
        lax.psum_scatter(reg_grads[9], ("dp", "fsdp"), scatter_dimension=0, tiled=True),
        lax.psum_scatter(reg_grads[10], ("dp", "fsdp"), scatter_dimension=1, tiled=True),
    )
    enc_shards = (
        lax.psum_scatter(grad_table, ("dp", "fsdp"), scatter_dimension=1, tiled=True),
        lax.psum_scatter(enc_grads[0], ("dp", "fsdp"), scatter_dimension=1, tiled=True),
        lax.psum_scatter(enc_grads[1], ("dp", "fsdp"), scatter_dimension=1, tiled=True),
        lax.psum_scatter(enc_grads[2], ("dp", "fsdp"), scatter_dimension=0, tiled=True),
        lax.psum_scatter(enc_grads[3], ("dp", "fsdp"), scatter_dimension=0, tiled=True),
        lax.psum_scatter(enc_grads[4], ("dp", "fsdp"), scatter_dimension=0, tiled=True),
        lax.psum_scatter(enc_grads[5], ("dp", "fsdp"), scatter_dimension=0, tiled=True),
        lax.psum_scatter(enc_grads[6], ("dp", "fsdp"), scatter_dimension=0, tiled=True),
        lax.psum_scatter(enc_grads[7], ("dp", "fsdp"), scatter_dimension=0, tiled=True),
        lax.psum_scatter(enc_grads[8], ("dp", "fsdp"), scatter_dimension=0, tiled=True),
        lax.psum_scatter(enc_grads[9], ("dp", "fsdp"), scatter_dimension=0, tiled=True),
        lax.psum_scatter(enc_grads[10], ("dp", "fsdp"), scatter_dimension=1, tiled=True),
    )
    pos_shard = enc_shards[0]
    weight_shards = tuple(
        (jnp.stack([early, late]) for early, late in zip(enc_shards[1:], reg_shards))
    )
    return (
        latent_f.astype(jnp.bfloat16),
        regressed_f.astype(jnp.bfloat16),
        grad_start,
        pos_shard,
    ) + weight_shards


def solution(mesh):
    in_specs = (
        P(("dp", "fsdp"), None),
        P(("dp", "fsdp"), None),
        P(("dp", "fsdp"), None),
        P(("dp", "fsdp"), None),
        P(None, ("dp", "fsdp")),
        P(None, None, ("dp", "fsdp")),
        P(None, None, ("dp", "fsdp")),
        P(None, ("dp", "fsdp"), None),
        P(None, ("dp", "fsdp")),
        P(None, ("dp", "fsdp"), None),
        P(None, ("dp", "fsdp")),
        P(None, ("dp", "fsdp"), None),
        P(None, ("dp", "fsdp")),
        P(None, ("dp", "fsdp"), None),
        P(None, ("dp", "fsdp")),
        P(None, None, ("dp", "fsdp")),
    )
    out_specs = (
        P(("dp", "fsdp"), None),
        P(("dp", "fsdp"), None),
        P(("dp", "fsdp"), None),
        P(None, ("dp", "fsdp")),
        P(None, None, ("dp", "fsdp")),
        P(None, None, ("dp", "fsdp")),
        P(None, ("dp", "fsdp"), None),
        P(None, ("dp", "fsdp")),
        P(None, ("dp", "fsdp"), None),
        P(None, ("dp", "fsdp")),
        P(None, ("dp", "fsdp"), None),
        P(None, ("dp", "fsdp")),
        P(None, ("dp", "fsdp"), None),
        P(None, ("dp", "fsdp")),
        P(None, None, ("dp", "fsdp")),
    )
    devices = mesh.shape["dp"] * mesh.shape["fsdp"]

    def step(*args):
        rows = args[7].shape[1]
        kernels = mesh.shape["fsdp"] == 4 and rows // (devices // 2) % 16 == 0
        run = jax.shard_map(
            functools.partial(fused, devices) if kernels else local,
            mesh=mesh,
            in_specs=in_specs,
            out_specs=out_specs,
            check_vma=False,
        )
        return run(*args)

    return step
```

```python
import functools
import math

import jax
import jax.numpy as jnp
import numpy as np
from jax import lax
from jax.experimental import pallas as pl
from jax.experimental.pallas import tpu as pltpu
from jax.sharding import PartitionSpec as P

HEAD_DIM = 64
VIS = 98
SET = 128
PATCHES = 196

MESH = pl.DeviceIdType.MESH
WIDE = jnp.float32
LOW = jnp.bfloat16


def lanes(start, size):
    return pl.ds(pl.multiple_of(start, 128), size)


class Place:
    def __init__(self, line):
        dp, fsdp = lax.axis_index("dp"), lax.axis_index("fsdp")
        self.line = line
        self.z, self.y = dp // 2, dp % 2
        self.x, self.core = fsdp // 2, fsdp % 2
        z, y, x, core = self.z, self.y, self.x, self.core
        first_y = jnp.where(core == 0, 1 - y, y)
        first_x = jnp.where(core == 0, x, 1 - x)
        second_y = jnp.where(core == 0, y, 1 - y)
        second_x = jnp.where(core == 0, 1 - x, x)
        self.own = 2 * y + x
        self.first = 2 * first_y + first_x
        self.second = 2 * second_y + second_x
        self.across = 2 * (1 - y) + (1 - x)
        self.twin = self.at(z, y, x, 1 - core)
        self.near = self.at(z, first_y, first_x, core)
        self.far = self.at(z, second_y, second_x, core)
        self.above = [
            self.at(lax.rem(z + step, line), y, x, core) for step in range(1, line)
        ]

    def at(self, z, y, x, core):
        return (2 * z + y, 2 * x + core)

    def greet(self):
        barrier = pltpu.get_barrier_semaphore()
        others = [self.twin, self.near, self.far] + self.above
        for other in others:
            pl.semaphore_signal(barrier, inc=1, device_id=other, device_id_type=MESH)
        pl.semaphore_wait(barrier, len(others))


class Copies:
    def __init__(self, send, recv):
        self.send, self.recv, self.used, self.sent = send, recv, 0, []

    def remote(self, source, target, device):
        copy = pltpu.make_async_remote_copy(
            src_ref=source,
            dst_ref=target,
            send_sem=self.send.at[self.used],
            recv_sem=self.recv.at[self.used],
            device_id=device,
            device_id_type=MESH,
        )
        self.used += 1
        copy.start()
        self.sent.append(copy)
        return copy

    def local(self, source, target):
        copy = pltpu.make_async_copy(source, target, self.send.at[self.used])
        self.used += 1
        copy.start()
        return copy

    def drain(self):
        for copy in self.sent:
            copy.wait_send()


def gather_steps(line, items, sources, shards, theirs, fulls, stages, send, recv, bring):
    count = len(items)
    place = Place(line)
    copies = Copies(send, recv)
    place.greet()
    swaps = [copies.remote(source, their, place.twin) for source, their in zip(sources, theirs)]
    arrived = set()
    sizes = [wide // 2 for _, _, _, wide in items]
    columns = [lanes(item[2] + place.core * half, half) for item, half in zip(items, sizes)]

    def stage(i):
        array, rows, first, _ = items[i]
        own, their = shards[array](), theirs[array]
        if array not in arrived:
            arrived.add(array)
            swaps[array].wait_recv()
        for which, (low_ref, high_ref) in ((0, (own, their)), (1, (their, own))):

            @pl.when(place.core == which)
            def _():
                part = pl.ds(first + which * sizes[i], sizes[i])
                both = jnp.concatenate(
                    [low_ref[:, part].astype(WIDE), high_ref[:, part].astype(WIDE)], axis=0
                )
                stages[i][...] = both.astype(LOW)

    def group(i, which):
        return fulls[items[i][0]].at[:, which, :, columns[i]]

    def spread(i):
        target = fulls[items[i][0]].at[place.z, place.own, :, columns[i]]
        own = copies.local(stages[i], target)
        return [own] + [copies.remote(stages[i], target, device) for device in place.above]

    def send_on(i, which, devices):
        return [copies.remote(group(i, which), group(i, which), device) for device in devices]

    def share(i, far, twin, onward):
        far.wait_recv()
        onward[0].wait_recv()
        more = send_on(i, place.second, [place.twin]) + send_on(i, place.across, [place.twin])
        return [twin, onward[1]] + more

    def complete(i, started):
        for copy in started:
            copy.wait_recv()
        bring(i)

    ahead, lead = 5, 2
    start = 9.0
    spreads, owned, last, shared = {}, {}, {}, {}

    def own_sends(i):
        if i + ahead < count:
            stage(i + ahead)
            spreads[i + ahead] = spread(i + ahead)
        spreads[i][0].wait()
        for copy in spreads[i][1:]:
            copy.wait_recv()
        owned[i] = send_on(i, place.own, [place.near, place.far, place.twin])

    for i in range(min(ahead, count)):
        stage(i)
        spreads[i] = spread(i)
    for i in range(min(lead, count)):
        yield start
        own_sends(i)
    for i in range(count + 2):
        if i < count:
            start += 3 * line * items[i][1] * sizes[i] * 2 / RATE
            if i + lead < count:
                yield start - 1.5
                own_sends(i + lead)
            yield start
            near, far, twin = owned[i]
            near.wait_recv()
            last[i] = (far, twin, send_on(i, place.first, [place.far, place.twin]))
        else:
            yield start + 2
        if 0 <= i - 1 < count:
            shared[i - 1] = share(i - 1, *last[i - 1])
        if 0 <= i - 2 < count:
            complete(i - 2, shared[i - 2])
    yield start
    copies.drain()


class Names:
    def __getattr__(self, word):
        return word


N = Names()
LINK = 64e3
RATE = 92e3
TWIN = 4e5


class Pace:
    def __init__(self, steps):
        self.steps, self.now = steps, 0.0
        self.due = next(steps)

    def advance(self):
        self.now = max(self.now, self.due)
        self.due = next(self.steps, None)

    def spend(self, time):
        self.now += time
        while self.due is not None and self.due <= self.now:
            self.advance()

    def until(self, reached):
        while not reached():
            self.advance()

    def finish(self):
        while self.due is not None:
            self.advance()
TILE = 256
ROOT = math.sqrt(2.0 / math.pi)
CUBE = 0.044715


def dot_nn(left, right):
    return lax.dot_general(left, right, (((1,), (0,)), ((), ())), preferred_element_type=WIDE)


def dot_nt(left, right):
    return lax.dot_general(left, right, (((1,), (1,)), ((), ())), preferred_element_type=WIDE)


def dot_tn(left, right):
    return lax.dot_general(left, right, (((0,), (0,)), ((), ())), preferred_element_type=WIDE)


def each(count, step, first=0, unroll=1):
    def run(k, carry):
        step(k)
        return carry

    lax.fori_loop(first, first + count, run, 0, unroll=unroll)


def row_blocks(total, block, step):
    each(total // block, lambda k: step(pl.ds(pl.multiple_of(k * block, block), block)), unroll=2)


def row(ref, k):
    return ref[pl.ds(k, 1), :]


def flat(value):
    return value.reshape(-1, value.shape[-1])


def add_rows(ref, k, value):
    ref[pl.ds(k, 1), :] += jnp.sum(value.astype(WIDE), axis=0, keepdims=True)


def live_rows(block, wide):
    return lax.broadcasted_iota(jnp.int32, (block, wide), 0) % SET < VIS


def selection(slots, wide):
    rows = lax.broadcasted_iota(jnp.int32, (32, wide), 0)
    return (lax.broadcasted_iota(jnp.int32, (32, wide), 1) == rows + slots).astype(LOW)


def unit_matrix(size):
    same = lax.broadcasted_iota(jnp.int32, (size, size), 0) == lax.broadcasted_iota(jnp.int32, (size, size), 1)
    return jnp.where(same, 1.0, 0.0)


def fill_picks(marks, first, target):
    wide = target.shape[1]

    def step(k):
        own = lax.broadcasted_iota(jnp.int32, (wide, SET), 0) == marks[pl.ds(first + k, 1), :]
        target[pl.ds(pl.multiple_of(k * SET, SET), SET), :] = jnp.where(own, 1.0, 0.0).T.astype(LOW)

    each(target.shape[0] // SET, step)


def fold_tables(model, rows, parts):
    entry = np.arange(model)
    source = rows * (entry // (parts * rows)) + entry % rows
    spots = (np.arange(model // parts)[:, None] == source[None, :]).astype(np.float32)
    column = entry % (parts * rows) // rows
    which = (np.arange(8)[:, None] == column[None, :]).astype(np.float32)
    return jnp.asarray(spots, LOW), jnp.asarray(which, WIDE)


class Buffers:
    def __init__(self, refs, sems):
        self.refs, self.sems, self.used = refs, sems, 0
        self.loading, self.saving = {}, []

    def __getitem__(self, name):
        if name in self.loading:
            self.loading.pop(name).wait()
        return self.refs[name]

    def copy(self, source, target):
        copy = pltpu.make_async_copy(source, target, self.sems.at[self.used])
        self.used += 1
        copy.start()
        return copy

    def load(self, name, source, target=None):
        self.loading[name] = self.copy(source, self.refs[name] if target is None else target)

    def wait(self, *names):
        for name in names:
            if name in self.loading:
                self.loading.pop(name).wait()

    def save(self, name, target):
        self.saving.append((name, self.copy(self.refs[name], target)))

    def saved(self, name):
        self.settle([entry for entry in self.saving if entry[0] == name])

    def settle(self, entries):
        for entry in entries:
            if any(entry is other for other in self.saving):
                entry[1].wait()
        self.saving = [other for other in self.saving if not any(other is entry for entry in entries)]

    def drain(self):
        for name in list(self.loading):
            self.loading.pop(name).wait()
        for _, copy in self.saving:
            copy.wait()


def call(body, ins, small, outs, scratch, sems, extra, name, collective, vmem):
    names = list(ins) + list(small) + list(outs) + list(scratch)

    def kernel(*refs):
        named = dict(zip(names, refs[: len(names)]))
        body(Buffers(named, refs[len(names)]), *refs[len(names) + 1 :])

    anywhere = pl.BlockSpec(memory_space=pl.ANY)
    results = pl.pallas_call(
        kernel,
        out_shape=list(outs.values()),
        in_specs=[anywhere] * len(ins) + [pl.BlockSpec(memory_space=pltpu.VMEM)] * len(small),
        out_specs=[anywhere] * len(outs),
        scratch_shapes=[pltpu.VMEM(*shape) for shape in scratch.values()]
        + [pltpu.SemaphoreType.DMA((sems,))]
        + extra,
        name=name,
        compiler_params=pltpu.CompilerParams(
            collective_id=collective, has_side_effects=True, vmem_limit_bytes=vmem
        ),
    )(*ins.values(), *small.values())
    return dict(zip(outs, results))


def norm_block(value, gain, shift):
    centered = value - jnp.mean(value, axis=-1, keepdims=True)
    inverse = lax.rsqrt(jnp.mean(centered * centered, axis=-1, keepdims=True) + 1e-06)
    normed = centered * inverse
    return normed * gain + shift, normed, inverse


def norm_back(value, grad, gain, sums, gain_row, shift_row):
    _, normed, inverse = norm_block(value, gain, 0.0)
    add_rows(sums, gain_row, grad * normed)
    add_rows(sums, shift_row, grad)
    scaled = grad * gain
    first = jnp.mean(scaled, axis=-1, keepdims=True)
    second = jnp.mean(scaled * normed, axis=-1, keepdims=True)
    return inverse * (scaled - first - normed * second)


def halves(value):
    low = lax.broadcasted_iota(jnp.int32, value.shape, 1) < HEAD_DIM
    zero = jnp.zeros_like(value)
    return jnp.concatenate([jnp.where(low, value, zero), jnp.where(low, zero, value)], axis=0)


def rejoin(value):
    rows = value.shape[0] // 2
    low = lax.broadcasted_iota(jnp.int32, (rows, value.shape[1]), 1) < HEAD_DIM
    return jnp.where(low, value[:rows], value[rows:])


def spot(k, pairs):
    return pl.ds(pl.multiple_of(k // pairs * SET, SET), SET), lanes(k % pairs * 128, 128)


def stacked(refs, at):
    parts = [ref[at[0], at[1]] for ref in refs]
    return parts[0] if len(parts) == 1 else jnp.concatenate(parts, axis=0)


def soft(keys, queries):
    scores = dot_nt(keys, queries) * (1.0 / math.sqrt(HEAD_DIM))
    scores = jnp.where(live_rows(*scores.shape), scores, -1e30)
    weighted = jnp.exp(scores - jnp.max(scores, axis=0, keepdims=True))
    return weighted / jnp.sum(weighted, axis=0, keepdims=True)


def in_pieces(count, piece, step, between):
    for first in range(0, count, piece):
        each(piece, step, first, piece)
        between()


def attend(queries, keys, values, mixed, between):
    pairs = queries.shape[1] // 128

    def step(k):
        at = spot(k, pairs)
        weights = soft(stacked(keys, at), halves(queries[at[0], at[1]])).astype(LOW)
        mixed[at[0], at[1]] = rejoin(dot_tn(weights, stacked(values, at))).astype(LOW)

    in_pieces(queries.shape[0] // SET * pairs, 4, step, between)


def attend_back(grad_mixed, queries, keys, values, grad_queries, grad_keys, grad_values, between):
    pairs = queries.shape[1] // 128
    factor = 1.0 / math.sqrt(HEAD_DIM)

    def step(k):
        at = spot(k, pairs)
        key, value = stacked(keys, at), stacked(values, at)
        query, grad = halves(queries[at[0], at[1]]), halves(grad_mixed[at[0], at[1]])
        weights = soft(key, query)
        back_value = dot_nn(weights.astype(LOW), grad).astype(LOW)
        grad_soft = dot_nt(value, grad)
        inner = jnp.sum(grad_soft * weights, axis=0, keepdims=True)
        grad_scores = (weights * (grad_soft - inner)).astype(LOW)
        back_key = (dot_nn(grad_scores, query) * factor).astype(LOW)
        grad_queries[at[0], at[1]] = (rejoin(dot_tn(grad_scores, key)) * factor).astype(LOW)
        for which in range(len(keys)):
            part = slice(which * SET, (which + 1) * SET)
            grad_keys[which][at[0], at[1]] = back_key[part]
            grad_values[which][at[0], at[1]] = back_value[part]

    in_pieces(queries.shape[0] // SET * pairs, 4, step, between)


def project(source, weight, start, bias, target):
    def step(k):
        part = lanes(k * TILE, TILE)
        value = dot_nn(source[...], flat(weight[:, :, :, lanes(start + k * TILE, TILE)]))
        if bias is not None:
            value = value + bias[:, part]
        target[:, part] = value.astype(LOW)

    each(target.shape[1] // TILE, step, unroll=3)


def residual(source, weight, bias, scale, before, after, branch, first, count):
    def step(k):
        part = lanes(k * TILE, TILE)
        value = dot_nn(source[...], flat(weight[:, :, :, part])) + bias[:, part]
        branch[:, part] = value.astype(LOW)
        after[:, part] = before[:, part] + scale[:, part] * value

    each(count, step, first, count)


def rise(source, weight, bias, active, slope, first, count):
    per = source.shape[1] // TILE

    def step(k):
        part = lanes(k * TILE, TILE)
        own = bias[pl.ds(k // per, 1), lanes(k % per * TILE, TILE)]
        value = dot_nn(source[...], flat(weight[:, :, :, part])) + own
        square = value * value
        curve = jnp.tanh(value * (ROOT + (ROOT * CUBE) * square))
        half = 0.5 + 0.5 * curve
        active[:, part] = (value * half).astype(LOW)
        bend = value * (half - half * curve) * (ROOT + (3.0 * ROOT * CUBE) * square)
        slope[:, part] = (half + bend).astype(LOW)

    each(count, step, first, count)


def small_vectors(b, parts):
    extra, vec = b[N.extra], b[N.vec]
    pick = selection(PATCHES, extra.shape[1])
    vec[...] = dot_nt(pick, extra[...])
    at = 16
    for count, spots, which in ((parts[0], b[N.spots_q], b[N.which_q]), (parts[1], b[N.spots_f], b[N.which_f])):
        rows = spots.shape[0]
        found = []
        for chunk in range(count):
            held = dot_nt(pick, extra[pl.ds(chunk * rows, rows), :]).astype(LOW)
            found.append(dot_nn(held, spots[...]))
        for block in range(2):
            for chunk in range(count):
                base = at + block * count
                total = sum(
                    found[chunk][base + j : base + j + 1] * which[j : j + 1, :] for j in range(count)
                )
                vec[base + chunk : base + chunk + 1, :] = total
        at += 2 * count


def forward_compute(b, need, spend, keep, release):
    rows, model = b[N.start].shape
    need(N.extra, 0, 0)
    b[N.extra][...] = flat(b[N.extra4][...])
    small_vectors(b, (2, 4))
    vec, extra = b[N.vec], b[N.extra]
    keep(N.vec)
    spend(2)

    def vector(k):
        return vec.at[pl.ds(k, 1)]

    def open_rows(r):
        start = b[N.patches][r, :].astype(WIDE) + dot_nt(b[N.pick_vis][r, :], extra[...])
        b[N.start][r, :] = start
        b[N.a0][r, :] = norm_block(start, row(vec, 0), row(vec, 4))[0].astype(LOW)
        query = dot_nt(b[N.pick_hid][r, :], extra[...])
        b[N.query][r, :] = query
        b[N.aq][r, :] = norm_block(query, row(vec, 2), row(vec, 6))[0].astype(LOW)

    b[N.patches]
    row_blocks(rows, 64, open_rows)
    for name in (N.start, N.a0, N.query, N.aq):
        keep(name)
    spend(4)

    def norm_into(source, target, gain, shift):
        def step(r):
            b[target][r, :] = norm_block(b[source][r, :], row(vec, gain), row(vec, shift))[0].astype(LOW)

        row_blocks(rows, 64, step)
        keep(target)
        spend(1)

    def low_into(source, target):
        def step(r):
            b[target][r, :] = b[source][r, :].astype(LOW)

        row_blocks(rows, 64, step)
        keep(target)

    def attention(block, sources, keys, values, before, after):
        query, mixed, branch = N.q + str(block), N.mix + str(block), N.br + str(block)
        for part, bias in enumerate((16 + 2 * block, None, 17 + 2 * block)):
            need(N.qkv, block, part)
            targets = ([query], keys, values)[part]
            for source, target in zip(sources[part], targets):
                shift = None if bias is None else vector(bias)
                project(b[source], b[N.w_qkv], part * model, shift, b[target])
                keep(target)
                spend(1)
        release(N.qkv)
        attend(
            b[query], [b[name] for name in keys], [b[name] for name in values], b[mixed],
            lambda: spend(1.5),
        )
        keep(mixed)
        need(N.proj, block, 0)
        residual(
            b[mixed], b[N.w_proj], vector(12 + block), vector(8 + 2 * block), b[before], b[after], b[branch],
            0, model // TILE,
        )
        release(N.proj)
        keep(branch)
        keep(after)
        spend(1.2)

    def feed(block, before, after, inner):
        branch = N.fd + str(block)
        norm_into(before, inner, 2 * block + 1, 4 + 2 * block + 1)
        b.saved(N.active)
        b.saved(N.slope)
        hidden = b[N.active].shape[1]
        for piece in range(hidden // model):
            need(N.fc1, block, piece)
            rise(
                b[inner], b[N.w_fc1], vec.at[pl.ds(20 + 4 * block, 4)], b[N.active], b[N.slope],
                piece * (model // TILE), model // TILE,
            )
            spend(2.2)
        release(N.fc1)
        keep(N.active, block)
        keep(N.slope, block)
        for piece in range(model // TILE):
            need(N.fc2, block, piece)
            residual(
                b[N.active], b[N.w_fc2], vector(14 + block), vector(8 + 2 * block + 1), b[before], b[after],
                b[branch], piece, 1,
            )
            spend(1.3)
        release(N.fc2)
        keep(branch)

    attention(0, ([N.a0], [N.a0], [N.a0]), [N.k0], [N.v0], N.start, N.mid0)
    feed(0, N.mid0, N.lat, N.a20)
    keep(N.lat)
    low_into(N.lat, N.latent)
    norm_into(N.lat, N.ak, 2, 6)
    both = [N.ak, N.aq]
    attention(1, ([N.aq], both, both), [N.k1, N.k2], [N.v1, N.v2], N.query, N.mid1)
    feed(1, N.mid1, N.reg, N.a21)
    low_into(N.reg, N.regressed)


KEPT_WIDE = (N.start, N.query, N.mid0, N.lat, N.mid1)
KEPT_LOW = (
    N.a0, N.aq, N.a20, N.ak, N.a21, N.q0, N.k0, N.v0, N.mix0, N.br0, N.fd0,
    N.q1, N.k1, N.v1, N.k2, N.v2, N.mix1, N.br1, N.fd1, N.latent, N.regressed,
)


def shape_of(*args):
    return jax.ShapeDtypeStruct(*args)


def cut(shapes):
    model = shapes[N.proj][1]
    pieces = []
    for kind, wide in ((N.qkv, model), (N.proj, model), (N.fc1, model), (N.fc2, TILE)):
        pieces += [(kind, k, k * wide, wide) for k in range(shapes[kind][1] // wide)]
    return pieces


def forward(patches, marks, vectors, wide_rows, weights, line, tables):
    rows, model = patches.shape
    kinds = (N.qkv, N.proj, N.fc1, N.fc2)
    shapes = {kind: (2 * weight.shape[1], weight.shape[2]) for kind, weight in zip(kinds, weights)}
    shapes[N.extra] = (2 * vectors[0].shape[-1], wide_rows)
    hidden = shapes[N.fc1][1]
    whole = {kind: (line, 4) + shape for kind, shape in shapes.items()}
    arrays = [(N.extra, 0)] + [(kind, block) for block in (0, 1) for kind in kinds]
    names = [kind + str(block) for kind, block in arrays]
    items = [(0, N.extra, 0, 0, 0, shapes[N.extra][1])]
    for block in (0, 1):
        for kind, piece, first, wide in cut(shapes):
            items.append((arrays.index((kind, block)), kind, block, piece, first, wide))
    outs = {name: shape_of(whole[kind], LOW) for name, (kind, _) in zip(names, arrays)}
    outs[N.vec_out] = shape_of((32, model), WIDE)
    for name in KEPT_WIDE:
        outs[name + N._out] = shape_of((rows, model), WIDE)
    for name in KEPT_LOW:
        outs[name + N._out] = shape_of((rows, model), LOW)
    for block in (0, 1):
        for name in (N.active, N.slope):
            outs[name + str(block) + N._out] = shape_of((rows, hidden), LOW)
    scratch = {name: ((rows, model), WIDE) for name in KEPT_WIDE + (N.reg,)}
    scratch.update({name: ((rows, model), LOW) for name in KEPT_LOW + (N.patches,)})
    scratch[N.active] = scratch[N.slope] = ((rows, hidden), LOW)
    scratch[N.vec] = ((32, model), WIDE)
    scratch[N.extra4] = (whole[N.extra], LOW)
    scratch[N.extra] = ((model, shapes[N.extra][1]), LOW)
    for kind in kinds:
        scratch[N.w_ + kind] = (whole[kind], LOW)
    for name, (kind, _) in zip(names, arrays):
        held = (shapes[kind][0] // 2, shapes[kind][1])
        scratch[N.own_ + name] = scratch[N.their_ + name] = (held, LOW)
    for i, (a, kind, _, _, _, wide) in enumerate(items):
        scratch[N.stage + str(i)] = ((shapes[kind][0], wide // 2), LOW)
    scratch[N.pick_vis] = scratch[N.pick_hid] = ((rows, shapes[N.extra][1]), LOW)
    ins = {N.patches_in: patches}
    ins.update({kind + N._in: weight for kind, weight in zip(kinds, weights)})
    small = {N.marks: marks}
    small.update({N.vector + str(k): vector for k, vector in enumerate(vectors)})
    scratch[N.extra_rows] = ((wide_rows, vectors[0].shape[-1]), WIDE)
    small.update(dict(zip((N.spots_q, N.which_q, N.spots_f, N.which_f), tables)))
    pairs = len(arrays) + len(items) * (line + 8)
    extra = [pltpu.SemaphoreType.DMA((pairs,)), pltpu.SemaphoreType.DMA((pairs,))]

    def body(b, send, recv):
        own = b[N.own_ + names[0]]
        stacked_rows, at = b[N.extra_rows], 0
        stacked_rows[...] = jnp.zeros(stacked_rows.shape, WIDE)
        for k in range(len(vectors)):
            ref = b[N.vector + str(k)]
            for place in [()] if len(ref.shape) == 2 else [(0,), (1,)]:
                piece = ref[place + (slice(None), slice(None))].astype(WIDE)
                stacked_rows[at : at + piece.shape[0], :] = piece
                at += piece.shape[0]
        own[...] = dot_nt(unit_matrix(own.shape[0]).astype(LOW), stacked_rows[...].astype(LOW)).astype(LOW)
        sources = [own] + [b[kind + N._in].at[block] for kind, block in arrays[1:]]
        b.load(N.patches, b[N.patches_in])
        for name, source in list(zip(names, sources))[1:]:
            b.load(N.own_ + name, source)
        free, held, loaded = {(N.extra, 0)} | {(kind, 0) for kind in kinds}, [], {}

        def bring(i):
            a, kind, block, piece, first, wide = items[i]
            if (kind, block) not in free:
                held.append(i)
                return
            part = (slice(None),) * 3 + (pl.ds(first, wide),)
            target = b.refs[N.extra4 if kind == N.extra else N.w_ + kind].at[part]
            b.load(N.item + str(i), b[names[a]].at[part], target)
            loaded[(kind, block, piece)] = N.item + str(i)

        shards = [lambda name=name: b[N.own_ + name] for name in names]
        steps = gather_steps(
            line, [(a, shapes[kind][0], first, wide) for a, kind, _, _, first, wide in items], sources, shards,
            [b[N.their_ + name] for name in names], [b[name] for name in names],
            [b[N.stage + str(i)] for i in range(len(items))], send, recv, bring,
        )
        pace = Pace(steps)
        for first, name in ((0, N.pick_vis), (rows // SET, N.pick_hid)):
            fill_picks(b[N.marks], first, b[name])

        def need(kind, block, piece):
            pace.until(lambda: (kind, block, piece) in loaded)
            b.wait(loaded[(kind, block, piece)])

        def release(kind):
            free.add((kind, 1))
            for i in [i for i in held if items[i][1] == kind]:
                held.remove(i)
                bring(i)

        def keep(name, block=None):
            b.save(name, b[name + ("" if block is None else str(block)) + N._out])

        forward_compute(b, need, pace.spend, keep, release)
        pace.finish()
        b.drain()

    return call(body, ins, small, outs, scratch, 128, extra, N.forward, 0, 63 << 20)


class Reducer:
    def __init__(self, line, items, slots, grads, outs, shared, single, send, recv, credit, ended):
        self.line, self.items, self.slots = line, items, slots
        self.grads, self.outs, self.shared, self.single = grads, outs, shared, single
        self.credit, self.ended = credit, ended
        self.place = Place(line)
        self.copies = Copies(send, recv)
        self.place.greet()
        self.ready, self.begun, self.state = set(), {}, {}
        self.next, self.due = [0] * 5, {}
        self.now = self.link_free = self.line_free = 0.0
        self.sends = {i: [] for i in range(len(items))}
        self.steps = [self.pair, self.near, self.along, self.swap, self.finish]

    def remote(self, i, source, target, device):
        copy = self.copies.remote(source, target, device)
        self.sends[i].append(copy)
        return copy

    def unit(self, i):
        return self.line * self.items[i][0] * self.half(i) * 2

    def half(self, i):
        return self.items[i][2] // 2

    def columns(self, i, core):
        return lanes(self.items[i][1] + core * self.half(i), self.half(i))

    def earlier(self, i):
        return [j for j in range(i) if self.slots[j] == self.slots[i]]

    def later(self, i):
        return [j for j in range(i + 1, len(self.items)) if self.slots[j] == self.slots[i]]

    def buffers(self, i):
        mine, twins, owned, final, other = self.shared[self.slots[i]]
        through, direct, joined, arrived = self.single[i]
        return mine, twins, through, direct, joined, owned, arrived, final, other

    def begin(self, i):
        place = self.place
        mine, twins = self.buffers(i)[:2]
        if self.earlier(i):
            pl.semaphore_wait(self.credit.at[self.slots[i]], 1)
        away = self.remote(
            i, self.grads[i].at[:, :, :, self.columns(i, 1 - place.core)], twins, place.twin
        )
        here = self.copies.local(self.grads[i].at[:, :, :, self.columns(i, place.core)], mine)
        self.begun[i] = (away, here)
        self.due[0, i] = self.now + 2.0 + 4 * self.unit(i) / TWIN

    def begin_some(self):
        i = len(self.begun)
        while i < len(self.items) and i in self.ready and i <= self.next[0] + 2:
            if any(j >= self.next[4] for j in self.earlier(i)):
                return
            self.begin(i)
            i += 1

    def pair(self, i):
        place = self.place
        mine, twins, through, direct = self.buffers(i)[:4]
        away, here = self.begun[i]
        away.wait_recv()
        here.wait()

        def step(k):
            a, c = k // 4, k % 4
            mine[a, c] = mine[a, c] + twins[a, c]

        each(self.line * 4, step, unroll=2)
        self.state[i] = [
            self.remote(i, mine.at[:, place.across], through, place.far),
            self.remote(i, mine.at[:, place.second], direct, place.far),
        ]
        unit = self.unit(i) / LINK
        start = max(self.now, self.link_free)
        self.link_free = start + 3 * unit
        self.due[1, i] = start + 1.0 + 1.6 * unit
        self.now += 0.5 + self.unit(i) / 1e6

    def near(self, i):
        place = self.place
        mine, _, through, _, joined = self.buffers(i)[:5]
        self.state[i][0].wait_recv()

        def step(k):
            through[k] = through[k] + mine[k, place.first]

        each(self.line, step)
        self.state[i].append(self.remote(i, through, joined, place.near))
        self.due[2, i] = self.now + 1.0 + 1.6 * self.unit(i) / LINK
        self.now += 0.3

    def along(self, i):
        place, line = self.place, self.line
        mine, _, _, direct, joined, owned, arrived = self.buffers(i)[:7]
        self.state[i][1].wait_recv()
        self.state[i][2].wait_recv()

        def step(k):
            total = mine[k, place.own].astype(WIDE) + direct[k].astype(WIDE) + joined[k].astype(WIDE)
            owned[k] = total.astype(LOW)

        each(line, step)
        self.state[i] = [
            self.remote(
                i, owned.at[lax.rem(place.z + k + 1, line)], arrived.at[k], place.above[k]
            )
            for k in range(line - 1)
        ]
        start = max(self.now, self.line_free)
        self.line_free = start + 2 * self.unit(i) / LINK
        self.due[3, i] = self.line_free + 1.0
        self.now += 0.3

    def swap(self, i):
        place, rows = self.place, self.items[i][0] // 2
        owned, arrived, final, other = self.buffers(i)[5:]
        for copy in self.state[i]:
            copy.wait_recv()
        total = owned[place.z].astype(WIDE)
        for k in range(self.line - 1):
            total = total + arrived[k].astype(WIDE)
        final[...] = total
        away = pl.ds(pl.multiple_of((1 - place.core) * rows, 8), rows)
        self.state[i] = [self.remote(i, final.at[away], other, place.twin)]
        self.due[4, i] = self.now + 2.0
        self.now += 0.2

    def finish(self, i):
        place = self.place
        final, other = self.buffers(i)[7:]
        rows = self.items[i][0] // 2
        own = pl.ds(pl.multiple_of(place.core * rows, 8), rows)
        self.outs[i][:, self.columns(i, place.core)] = final[own]
        self.state[i][0].wait_recv()
        self.outs[i][:, self.columns(i, 1 - place.core)] = other[...]
        for copy in self.sends[i]:
            copy.wait_send()
        if self.later(i):
            pl.semaphore_signal(
                self.credit.at[self.slots[i]], inc=1, device_id=place.twin, device_id_type=MESH
            )
        self.ended(i)

    def able(self):
        found = []
        for stage in range(5):
            i = self.next[stage]
            if (i in self.begun) if stage == 0 else (i < self.next[stage - 1]):
                found.append((self.due[stage, i], -stage))
        return sorted(found)

    def run(self, stage):
        self.now = max(self.now, self.due[stage, self.next[stage]])
        self.steps[stage](self.next[stage])
        self.next[stage] += 1
        self.begin_some()

    def spend(self, time):
        self.now += time
        self.begin_some()
        while True:
            found = [entry for entry in self.able() if entry[0] <= self.now]
            if not found:
                return
            self.run(-found[0][1])

    def complete(self):
        self.begin_some()
        while self.next[4] < len(self.items):
            self.run(-self.able()[0][1])


def backward_compute(b, block, keys, spend, emit, bring):
    rows, model = b[N.acc].shape
    vec, sums = b[N.vec], b[N.sums]
    scale_row, feed_bias = 8 + 2 * block, 14 + block
    res, acc, gm, turned = b[N.res], b[N.acc], b[N.gm], b[N.turn]

    def close_rows(r):
        grad = res[r, :]
        if block:
            grad = jnp.where(live_rows(128, model), grad, 0.0)
            res[r, :] = grad
        add_rows(sums, scale_row + 1, grad * b[N.fd][r, :].astype(WIDE))
        low = (row(vec, scale_row + 1) * grad).astype(LOW)
        gm[r, :] = low
        add_rows(sums, feed_bias, low)

    b[N.fd]
    row_blocks(rows, 128, close_rows)
    if block:
        b.load(N.fd, b[N.ak_out])
    spend(2.5)

    def turn(value, start=0):
        turned[:, start : start + rows] = value.T

    def weight_grad(right, first, stage, depth):
        def step(k):
            value = dot_nn(turned[:, :depth], right[:, lanes(first + k * TILE, TILE)])
            shape = stage.shape[:-1] + (TILE,)
            stage[..., lanes(k * TILE, TILE)] = value.reshape(shape).astype(LOW)

        each(model // TILE, step, unroll=3)

    w_fc2, slope = b[N.w_fc2], b[N.slope]
    chunks = slope.shape[1] // model
    turn(b[N.inner][...])
    bring(N.inner)
    for chunk in range(chunks):
        part = slice(chunk * model, (chunk + 1) * model)

        def hidden_rows(r):
            value = dot_nt(gm[r, :], flat(w_fc2[chunk]))
            low = (value * slope[r, part].astype(WIDE)).astype(LOW)
            slope[r, part] = low
            add_rows(sums, 20 + 4 * block + chunk, low)

        row_blocks(rows, 256, hidden_rows)
        stage = N.stage + str(chunk % 2)
        b.saved(stage)
        weight_grad(slope, chunk * model, b[stage], rows)
        emit(N.fc1, chunk, stage)
        spend(3.2)
    bring(N.w_fc2)
    active = b[N.active]
    for chunk in range(chunks):
        turn(active[:, chunk * model : (chunk + 1) * model])
        b.saved(N.stage2)
        weight_grad(gm, 0, b[N.stage2], rows)
        emit(N.fc2, chunk, N.stage2)
        spend(2.2)
    bring(N.active)
    w_fc1 = b[N.w_fc1]
    for chunk in range(chunks):
        part = slice(chunk * model, (chunk + 1) * model)

        def inner_rows(r):
            value = dot_nt(slope[r, part], flat(w_fc1[:, :, :, part]))
            if chunk:
                value = acc[r, :] + value
            acc[r, :] = value

        row_blocks(rows, 256, inner_rows)
        spend(1.4)
    bring(N.slope)
    b.load(N.w_proj, b[N.w_ + N.proj + str(block)], w_fc1.at[:, :, :, 3 * model :])
    b.load(N.w_qkv, b[N.w_ + N.qkv + str(block)], w_fc1.at[:, :, :, : 3 * model])
    branch = b[N.br]

    def middle_rows(r):
        back = norm_back(
            b[N.mid][r, :], acc[r, :], row(vec, 2 * block + 1), sums, 2 * block + 1, 4 + 2 * block + 1
        )
        grad = res[r, :] + back
        res[r, :] = grad
        add_rows(sums, scale_row, grad * branch[r, :].astype(WIDE))
        low = (row(vec, scale_row) * grad).astype(LOW)
        gm[r, :] = low
        add_rows(sums, 12 + block, low)

    b[N.mid]
    row_blocks(rows, 64, middle_rows)
    b.load(N.mid, b[N.query_out if block else N.start_out])
    bring(N.br)
    spend(3)
    turn(b[N.mix][...])
    b.saved(N.stage0)
    weight_grad(gm, 0, b[N.stage0], rows)
    emit(N.proj, 0, N.stage0)
    spend(2.2)
    b.wait(N.w_proj)
    w_qkv, w_proj = w_fc1.at[:, :, :, : 3 * model], w_fc1.at[:, :, :, 3 * model :]

    def mixed_rows(r):
        b[N.mix][r, :] = dot_nt(gm[r, :], flat(w_proj[...])).astype(LOW)

    row_blocks(rows, 256, mixed_rows)
    spend(1.2)
    query, key, value = b[N.query], b[N.key], b[N.value]
    b.wait(N.key2, N.value2)
    queries = b[N.aq]
    key_parts = [key.at[pl.ds(k * rows, rows)] for k in range(keys)]
    value_parts = [value.at[pl.ds(k * rows, rows)] for k in range(keys)]
    attend_back(
        b[N.mix], query, key_parts, value_parts, query, key_parts, value_parts,
        lambda: spend(1.7 + 0.5 * keys),
    )
    bring(N.mix)

    def bias_rows(r):
        add_rows(sums, 16 + 2 * block, query[r, :])
        for k in range(keys):
            add_rows(sums, 17 + 2 * block, value_parts[k][r, :])

    row_blocks(rows, 128, bias_rows)
    if block:
        turn(b[N.fd][...])
        turn(queries[...], rows)
        bring(N.fd)
    else:
        turn(queries[...])
    depth = pl.ds(0, keys * rows)
    for chunk, right in ((1, key.at[depth]), (2, value.at[depth])):
        stage = N.stage + str(chunk % 2)
        b.saved(stage)
        weight_grad(right, 0, b[stage], keys * rows)
        emit(N.qkv, chunk, stage)
        spend(1 + 1.3 * keys)
    if block:
        turn(queries[...])
    bring(N.aq)
    b.saved(N.stage1)
    weight_grad(query, 0, b[N.stage1], rows)
    emit(N.qkv, 0, N.stage1)
    spend(2.2)
    b.wait(N.w_qkv)

    def back(parts):
        def step(r):
            total = 0.0
            for ref, chunk in parts:
                total = total + dot_nt(ref[r, :], flat(w_qkv[:, :, :, chunk * model : (chunk + 1) * model]))
            acc[r, :] = total

        row_blocks(rows, 256, step)

    gain, shift = 2 * block, 4 + 2 * block
    back([(query, 0), (key_parts[keys - 1], 1), (value_parts[keys - 1], 2)])
    spend(3.3)
    b[N.mid]

    def start_rows(r):
        grad = res[r, :] + norm_back(b[N.mid][r, :], acc[r, :], row(vec, gain), sums, gain, shift)
        res[r, :] = grad
        gm[r, :] = grad.astype(LOW)

    row_blocks(rows, 64, start_rows)
    if block:
        b.load(N.mid, b[N.lat_out])
        b.load(N.res, b[N.grad_latent])
    spend(2.5)
    fill_picks(b[N.marks], rows // SET * block, b[N.pick])
    table = dot_tn(gm[...], b[N.pick][...])
    if block:
        b[N.table][...] = table
        back([(key_parts[0], 1), (value_parts[0], 2)])
        bring(N.query, N.key, N.value, N.w_fc1)
        spend(3)
        b[N.mid], b[N.res]

        def latent_pair(k):
            for part in range(2):
                r = pl.ds(pl.multiple_of(k * SET + part * 64, 64), 64)
                grad = res[r, :]
                live = lax.broadcasted_iota(jnp.int32, grad.shape, 0) + part * 64 < VIS
                res[r, :] = jnp.where(live, grad, 0.0) + norm_back(
                    b[N.mid][r, :], acc[r, :], row(vec, gain), sums, gain, shift
                )

        each(rows // SET, latent_pair)
        bring(N.mid)
        spend(2.5)
    else:
        b[N.table][...] += table


def table_of_sums(b, parts):
    table, sums = b[N.table], b[N.sums]
    pick = selection(PATCHES, table.shape[1])
    plain = lax.broadcasted_iota(jnp.int32, sums.shape, 0) < 16
    table[...] += dot_tn(jnp.where(plain, sums[...], 0.0).astype(LOW), pick)
    at = 16
    lines = lax.broadcasted_iota(jnp.int32, sums.shape, 0)
    for count, spots, which in ((parts[0], b[N.spots_q], b[N.which_q]), (parts[1], b[N.spots_f], b[N.which_f])):
        rows = spots.shape[0]
        for chunk in range(count):
            spread = jnp.zeros(sums.shape, WIDE)
            for block in range(2):
                base = at + block * count
                for j in range(count):
                    entry = sums[base + chunk : base + chunk + 1, :] * which[j : j + 1, :]
                    spread = spread + jnp.where(lines == base + j, entry, 0.0)
            held = dot_nt(spots[...], spread.astype(LOW)).astype(LOW)
            table[pl.ds(chunk * rows, rows), :] += dot_nn(held, pick)
        at += 2 * count


HELD = (
    {
        N.fd: N.fd0, N.active: N.active0, N.slope: N.slope0, N.inner: N.a20, N.mid: N.mid0, N.br: N.br0,
        N.mix: N.mix0, N.query: N.q0, N.key: N.k0, N.value: N.v0, N.aq: N.a0,
    },
    {
        N.fd: N.fd1, N.active: N.active1, N.slope: N.slope1, N.inner: N.a21, N.mid: N.mid1, N.br: N.br1,
        N.mix: N.mix1, N.query: N.q1, N.key: N.k1, N.value: N.v1, N.aq: N.aq,
    },
)


def backward(f, grad_out, grad_latent, marks, line, tables):
    rows, model = f[N.mid0_out].shape
    hidden = f[N.active0_out].shape[1]
    wide = f[N.extra0].shape[3]
    shapes = {
        N.fc2: (hidden // (4 * line), model),
        N.fc1: (model // (4 * line), hidden),
        N.proj: (model // (4 * line), model),
        N.qkv: (model // (4 * line), 3 * model),
        N.extra: (model // (4 * line), wide),
    }
    whole = {kind: (line, 4) + shape for kind, shape in shapes.items()}
    pieces = {kind: [] for kind in shapes}
    for kind, piece, first, columns in cut(shapes):
        pieces[kind].append((piece, first, columns))
    pieces[N.extra] = [(0, 0, wide)]
    pieces[N.qkv] = pieces[N.qkv][1:] + pieces[N.qkv][:1]
    made = [N.fc1, N.fc2, N.proj, N.qkv]
    order_of = [(kind, block) for block in (1, 0) for kind in made] + [(N.extra, 0)]
    items, owners, counts, slots = [], [], {}, []
    for kind, block in order_of:
        for piece, first, columns in pieces[kind]:
            items.append((shapes[kind][0], first, columns))
            owners.append((kind, block, piece))
            shape = (shapes[kind][0], columns // 2)
            counts[shape] = counts.get(shape, 0) + 1
            slots.append((shape, (counts[shape] - 1) % (3 if kind == N.fc2 else 4)))
    held = sorted(set(slots))
    slots = [held.index(slot) for slot in slots]
    ins = {N.res_in: grad_out, N.grad_latent: grad_latent}
    for name in (N.query, N.start, N.lat, N.k2, N.v2, N.ak, N.vec):
        ins[name + N._out] = f[name + N._out]
    for block in (1, 0):
        for kind in made:
            ins[N.w_ + kind + str(block)] = f[kind + str(block)]
        for source in HELD[block].values():
            ins[N.in_ + source] = f[source + N._out]
    small = {N.marks: marks}
    small.update(dict(zip((N.spots_q, N.which_q, N.spots_f, N.which_f), tables)))
    outs = {N.g_ + kind + str(block): shape_of(whole[kind], LOW) for kind, block in order_of}
    for kind in made:
        outs[N.out_ + kind] = shape_of((2, shapes[kind][0] // 2, shapes[kind][1]), WIDE)
    outs[N.out_extra] = shape_of((wide, shapes[N.extra][0] // 2), WIDE)
    outs[N.res_out] = shape_of((rows, model), WIDE)
    scratch = {name: ((rows, model), WIDE) for name in (N.res, N.acc, N.mid)}
    for name in (N.fd, N.inner, N.br, N.mix, N.query, N.gm, N.aq):
        scratch[name] = ((rows, model), LOW)
    scratch[N.key] = scratch[N.value] = ((2 * rows, model), LOW)
    scratch[N.turn] = ((model, 2 * rows), LOW)
    scratch[N.active] = scratch[N.slope] = ((rows, hidden), LOW)
    scratch[N.w_fc1], scratch[N.w_fc2] = (whole[N.fc1], LOW), (whole[N.fc2], LOW)
    scratch[N.stage0] = scratch[N.stage1] = (whole[N.proj], LOW)
    scratch[N.stage2] = (whole[N.fc2][1:], LOW)
    scratch[N.vec] = scratch[N.sums] = ((32, model), WIDE)
    scratch[N.table] = ((model, wide), WIDE)
    scratch[N.pick] = ((rows, wide), LOW)
    scratch[N.rows_extra] = ((wide, shapes[N.extra][0] // 2), WIDE)
    scratch[N.table4] = (whole[N.extra], LOW)
    for kind, block in order_of:
        scratch[N.shard_ + kind + str(block)] = ((shapes[kind][0] // 2, shapes[kind][1]), WIDE)
    extra = []
    for (r, half), _ in held:
        extra += [pltpu.VMEM((line, 4, r, half), LOW)] * 2
        extra += [pltpu.VMEM((line, r, half), LOW), pltpu.VMEM((r, half), WIDE)]
        extra += [pltpu.VMEM((r // 2, half), WIDE)]
    for r, _, columns in items:
        half = columns // 2
        extra += [pltpu.VMEM((line, r, half), LOW)] * 3 + [pltpu.VMEM((line - 1, r, half), LOW)]
    pairs = len(items) * (line + 5)
    extra += [pltpu.SemaphoreType.DMA((pairs,))] * 2 + [pltpu.SemaphoreType.REGULAR((len(held),))]

    def body(b, *refs):
        shared = [refs[5 * k : 5 * k + 5] for k in range(len(held))]
        rest = refs[5 * len(held) :]
        single = [rest[4 * k : 4 * k + 4] for k in range(len(items))]
        send, recv, credit = rest[-3:]

        def fetch(name, block):
            if name in (N.w_fc1, N.w_fc2):
                b.load(name, b[name + str(block)])
            elif name in (N.key, N.value):
                b.load(name, b[N.in_ + HELD[block][name]], b.refs[name].at[pl.ds(0, rows)])
            else:
                b.load(name, b[N.in_ + HELD[block][name]])

        b.load(N.res, b[N.res_in])
        fetch(N.fd, 1)
        b.load(N.vec, b[N.vec_out])
        for name in (N.inner, N.w_fc2, N.slope, N.active, N.w_fc1, N.mid, N.br, N.mix, N.query, N.key, N.value, N.aq):
            fetch(name, 1)
        b.load(N.key2, b[N.k2_out], b.refs[N.key].at[pl.ds(rows, rows)])
        b.load(N.value2, b[N.v2_out], b.refs[N.value].at[pl.ds(rows, rows)])
        b[N.sums][...] = jnp.zeros(b[N.sums].shape, WIDE)
        left = {}
        for kind, block, _ in owners:
            left[kind, block] = left.get((kind, block), 0) + 1

        def ended(i):
            kind, block, _ = owners[i]
            left[kind, block] -= 1
            if left[kind, block] == 0:
                name, out = N.shard_ + kind + str(block), b[N.out_ + kind]
                if kind == N.extra:
                    held_rows = b[name][...]
                    name = N.rows_extra
                    b[name][...] = lax.dot_general(
                        held_rows, unit_matrix(held_rows.shape[0]), (((0,), (0,)), ((), ())),
                        precision=lax.Precision.HIGHEST, preferred_element_type=WIDE,
                    )
                b.save(name, out if kind == N.extra else out.at[block])

        reducer = Reducer(
            line, items, slots, [b[N.g_ + kind + str(block)] for kind, block, _ in owners],
            [b[N.shard_ + kind + str(block)] for kind, block, _ in owners],
            shared, single, send, recv, credit, ended,
        )
        waiting, fresh = [], [0]

        def settle(count):
            for _ in range(count):
                kind, block, chunk, entry = waiting.pop(0)
                b.settle([entry])
                for i, owner in enumerate(owners):
                    if owner[:2] == (kind, block):
                        if chunk == (hidden // model - 1 if kind == N.fc2 else owner[2]):
                            reducer.ready.add(i)

        def spend(time):
            settle(len(waiting) - fresh[0])
            reducer.spend(time)
            fresh[0] = 0

        def emitter(block):
            def emit(kind, chunk, stage):
                out = b[N.g_ + kind + str(block)]
                target = out.at[chunk] if kind == N.fc2 else out
                if kind in (N.fc1, N.qkv):
                    target = out.at[:, :, :, pl.ds(chunk * model, model)]
                b.save(stage, target)
                waiting.append((kind, block, chunk, b.saving[-1]))
                fresh[0] += 1

            return emit

        def bring(*names):
            for name in names:
                fetch(name, 0)

        b[N.res]
        backward_compute(b, 1, 2, spend, emitter(1), bring)
        backward_compute(b, 0, 1, spend, emitter(0), lambda *names: None)
        b.save(N.res, b[N.res_out])
        table_of_sums(b, (2, 4))
        b[N.table4][...] = b[N.table][...].astype(LOW).reshape(b[N.table4].shape)
        emitter(0)(N.extra, 0, N.table4)
        settle(len(waiting))
        reducer.complete()
        b.drain()

    return call(body, ins, small, outs, scratch, 128, extra, N.backward, 1, 64 << 20)


def fused(
    devices, patches, order, grad_latent, grad_out, pos_embed, ln_gain, ln_bias, w_qkv, b_qkv, w_proj, b_proj,
    w_fc1, b_fc1, w_fc2, b_fc2, layer_scale,
):
    line = devices // 8
    model = patches.shape[1]
    own = pos_embed.shape[1]
    marks = jnp.concatenate([order[:, :VIS], order[:, VIS:]], axis=0)
    marks = jnp.pad(marks, ((0, 0), (0, SET - VIS)), constant_values=-1)
    vectors = (ln_gain, ln_bias, layer_scale, b_proj, b_fc2, b_qkv, b_fc1)
    held = [array if array.shape[-1] == own else array.reshape(-1, own) for array in (pos_embed,) + vectors]
    counts = [array.size // own for array in held]
    wide = -(-sum(counts) // 128) * 128
    tables = fold_tables(model, own, b_qkv.shape[1] // own) + fold_tables(model, own, b_fc1.shape[1] // own)
    kept = forward(patches, marks, held, wide, (w_qkv, w_proj, w_fc1, w_fc2), line, tables)
    made = backward(kept, grad_out, grad_latent, marks, line, tables)
    parts, at = [], 0
    for array, count in zip((pos_embed,) + vectors, counts):
        parts.append(made[N.out_extra][at : at + count].reshape(array.shape))
        at += count
    pos_shard, gains, shifts, scales, proj_b, fc2_b, qkv_b, fc1_b = parts
    return (
        kept[N.latent_out], kept[N.regressed_out], made[N.res_out], pos_shard,
        gains, shifts, made[N.out_qkv], qkv_b, made[N.out_proj], proj_b,
        made[N.out_fc1], fc1_b, made[N.out_fc2], fc2_b, scales,
    )


def norm_forward(value, gain, shift):
    center = jnp.mean(value, axis=-1, keepdims=True)
    centered = value - center
    inverse = lax.rsqrt(jnp.mean(centered * centered, axis=-1, keepdims=True) + 1e-06)
    normed = centered * inverse
    return (normed * gain + shift, normed, inverse)


def norm_backward(grad, normed, inverse, gain):
    scaled = grad * gain
    first_mean = jnp.mean(scaled, axis=-1, keepdims=True)
    second_mean = jnp.mean(scaled * normed, axis=-1, keepdims=True)
    back = inverse * (scaled - first_mean - normed * second_mean)
    return (back, jnp.sum(grad * normed, axis=0), jnp.sum(grad, axis=0))


def unpack(pieces):
    gains, shifts, w_qkv, b_qkv, w_proj, b_proj, w_fc1, b_fc1, w_fc2, b_fc2, scales = pieces
    wide = jnp.float32
    return (
        gains.astype(wide),
        shifts.astype(wide),
        w_qkv,
        b_qkv.astype(wide),
        w_proj,
        b_proj.astype(wide),
        w_fc1,
        b_fc1.astype(wide),
        w_fc2,
        b_fc2.astype(wide),
        scales.astype(wide),
    )


def fetch(block, arrays):
    ln_gain, ln_bias, w_qkv, b_qkv, w_proj, b_proj, w_fc1, b_fc1, w_fc2, b_fc2, layer_scale = arrays
    gathered = (
        lax.all_gather(ln_gain[block], ("dp", "fsdp"), axis=1, tiled=True),
        lax.all_gather(ln_bias[block], ("dp", "fsdp"), axis=1, tiled=True),
        lax.all_gather(w_qkv[block], ("dp", "fsdp"), axis=0, tiled=True),
        lax.all_gather(b_qkv[block], ("dp", "fsdp"), axis=0, tiled=True),
        lax.all_gather(w_proj[block], ("dp", "fsdp"), axis=0, tiled=True),
        lax.all_gather(b_proj[block], ("dp", "fsdp"), axis=0, tiled=True),
        lax.all_gather(w_fc1[block], ("dp", "fsdp"), axis=0, tiled=True),
        lax.all_gather(b_fc1[block], ("dp", "fsdp"), axis=0, tiled=True),
        lax.all_gather(w_fc2[block], ("dp", "fsdp"), axis=0, tiled=True),
        lax.all_gather(b_fc2[block], ("dp", "fsdp"), axis=0, tiled=True),
        lax.all_gather(layer_scale[block], ("dp", "fsdp"), axis=1, tiled=True),
    )
    return unpack(gathered)


def column_sum(value):
    return jnp.sum(value.astype(jnp.float32), axis=0)


def outer_rows(left, right):
    return jnp.einsum("rd,rf->df", left, right, preferred_element_type=jnp.float32)


def attend_scores(queries, keys, key_live):
    scores = jnp.einsum("gqhe,gkhe->ghqk", queries, keys, preferred_element_type=jnp.float32) * (
        1.0 / math.sqrt(HEAD_DIM)
    )
    return jnp.where(key_live, scores, -1e30)


def attend_forward(query_in, key_in, images, key_live, weights):
    w_qkv, b_qkv, w_proj, b_proj = (weights[2], weights[3], weights[4], weights[5])
    model = query_in.shape[1]
    heads = model // HEAD_DIM
    queries = (
        jnp.dot(query_in, w_qkv[:, :model], preferred_element_type=jnp.float32) + b_qkv[:model]
    ).astype(jnp.bfloat16)
    paired = jnp.dot(key_in, w_qkv[:, model:], preferred_element_type=jnp.float32)
    keys = paired[:, :model].astype(jnp.bfloat16).reshape(images, -1, heads, HEAD_DIM)
    values = (
        (paired[:, model:] + b_qkv[model:])
        .astype(jnp.bfloat16)
        .reshape(images, -1, heads, HEAD_DIM)
    )
    queries = queries.reshape(images, -1, heads, HEAD_DIM)
    scores = attend_scores(queries, keys, key_live)
    highest_score = jnp.max(scores, axis=-1, keepdims=True)
    weighted = jnp.exp(scores - highest_score)
    summed = jnp.sum(weighted, axis=-1, keepdims=True)
    softmax_out = (weighted / summed).astype(jnp.bfloat16)
    mixed = jnp.einsum("ghqk,gkhe->gqhe", softmax_out, values, preferred_element_type=jnp.float32)
    mixed = mixed.reshape(-1, model).astype(jnp.bfloat16)
    branch = jnp.dot(mixed, w_proj, preferred_element_type=jnp.float32) + b_proj
    return (branch, (queries, keys, values, highest_score + jnp.log(summed), mixed))


def attend_backward(grad_branch, query_in, key_in, key_live, kept, weights):
    w_qkv, w_proj = (weights[2], weights[4])
    queries, keys, values, log_total, mixed = kept
    model = query_in.shape[1]
    grad_low = grad_branch.astype(jnp.bfloat16)
    grad_w_proj = outer_rows(mixed, grad_low)
    grad_b_proj = column_sum(grad_low)
    grad_mixed = (
        jnp.dot(grad_low, w_proj.T, preferred_element_type=jnp.float32)
        .astype(jnp.bfloat16)
        .reshape(queries.shape)
    )
    softmax_out = jnp.exp(attend_scores(queries, keys, key_live) - log_total)
    grad_values = jnp.einsum(
        "ghqk,gqhe->gkhe",
        softmax_out.astype(jnp.bfloat16),
        grad_mixed,
        preferred_element_type=jnp.float32,
    )
    grad_soft = jnp.einsum(
        "gqhe,gkhe->ghqk", grad_mixed, values, preferred_element_type=jnp.float32
    )
    grad_scores = (
        softmax_out * (grad_soft - jnp.sum(grad_soft * softmax_out, axis=-1, keepdims=True))
    ).astype(jnp.bfloat16)
    factor = 1.0 / math.sqrt(HEAD_DIM)
    grad_queries = (
        (
            jnp.einsum("ghqk,gkhe->gqhe", grad_scores, keys, preferred_element_type=jnp.float32)
            * factor
        )
        .astype(jnp.bfloat16)
        .reshape(-1, model)
    )
    grad_keys = (
        (
            jnp.einsum("ghqk,gqhe->gkhe", grad_scores, queries, preferred_element_type=jnp.float32)
            * factor
        )
        .astype(jnp.bfloat16)
        .reshape(-1, model)
    )
    grad_values = grad_values.astype(jnp.bfloat16).reshape(-1, model)
    grad_pairs = jnp.concatenate([grad_keys, grad_values], axis=1)
    grad_w_qkv = jnp.concatenate(
        [outer_rows(query_in, grad_queries), outer_rows(key_in, grad_pairs)], axis=1
    )
    grad_b_qkv = jnp.concatenate([column_sum(grad_queries), column_sum(grad_values)])
    grad_query_in = jnp.dot(grad_queries, w_qkv[:, :model].T, preferred_element_type=jnp.float32)
    grad_key_in = jnp.dot(grad_pairs, w_qkv[:, model:].T, preferred_element_type=jnp.float32)
    return (grad_query_in, grad_key_in, (grad_w_qkv, grad_b_qkv, grad_w_proj, grad_b_proj))


def feed_forward(middle, weights):
    gains, shifts, w_fc1, b_fc1, w_fc2, b_fc2 = (
        weights[0],
        weights[1],
        weights[6],
        weights[7],
        weights[8],
        weights[9],
    )
    normed_out, normed, inverse = norm_forward(middle, gains[1], shifts[1])
    inner_in = normed_out.astype(jnp.bfloat16)
    hidden = jnp.dot(inner_in, w_fc1, preferred_element_type=jnp.float32) + b_fc1
    active = jax.nn.gelu(hidden, approximate=True).astype(jnp.bfloat16)
    branch = jnp.dot(active, w_fc2, preferred_element_type=jnp.float32) + b_fc2
    return (branch, (normed, inverse, inner_in, hidden, active))


def feed_backward(grad_branch, kept, weights):
    gains, w_fc1, w_fc2 = (weights[0], weights[6], weights[8])
    normed, inverse, inner_in, hidden, active = kept
    grad_low = grad_branch.astype(jnp.bfloat16)
    grad_w_fc2 = outer_rows(active, grad_low)
    grad_b_fc2 = column_sum(grad_low)
    grad_active = jnp.dot(grad_low, w_fc2.T, preferred_element_type=jnp.float32)
    gelu_back = jax.vjp(functools.partial(jax.nn.gelu, approximate=True), hidden)[1]
    grad_hidden = gelu_back(grad_active)[0].astype(jnp.bfloat16)
    grad_w_fc1 = outer_rows(inner_in, grad_hidden)
    grad_b_fc1 = column_sum(grad_hidden)
    grad_normed = jnp.dot(grad_hidden, w_fc1.T, preferred_element_type=jnp.float32)
    grad_middle, grad_gain, grad_shift = norm_backward(grad_normed, normed, inverse, gains[1])
    return (grad_middle, grad_gain, grad_shift, (grad_w_fc1, grad_b_fc1, grad_w_fc2, grad_b_fc2))


def local(
    patches,
    order,
    grad_latent,
    grad_out,
    pos_embed,
    ln_gain,
    ln_bias,
    w_qkv,
    b_qkv,
    w_proj,
    b_proj,
    w_fc1,
    b_fc1,
    w_fc2,
    b_fc2,
    layer_scale,
):
    arrays = (
        ln_gain,
        ln_bias,
        w_qkv,
        b_qkv,
        w_proj,
        b_proj,
        w_fc1,
        b_fc1,
        w_fc2,
        b_fc2,
        layer_scale,
    )
    images = order.shape[0]
    model = patches.shape[1]
    highest = lax.Precision.HIGHEST
    live = jnp.arange(SET) < VIS
    live_rows = jnp.tile(live, images).astype(jnp.float32)[:, None]
    patch_slots = jnp.arange(PATCHES)

    def picker(index):
        padded = jnp.pad(index, ((0, 0), (0, SET - VIS)))
        chosen = (padded[:, :, None] == patch_slots[None, None, :]) & live[None, :, None]
        return chosen.astype(jnp.float32).reshape(-1, PATCHES)

    pick_visible = picker(order[:, :VIS])
    pick_masked = picker(order[:, VIS:])
    pos_table = lax.all_gather(pos_embed, ("dp", "fsdp"), axis=1, tiled=True).astype(jnp.float32)
    enc_weights, reg_weights = fetch(0, arrays), fetch(1, arrays)
    start = patches.astype(jnp.float32) + jnp.dot(pick_visible, pos_table, precision=highest)
    enc_out, enc_normed, enc_inverse = norm_forward(start, enc_weights[0][0], enc_weights[1][0])
    enc_attn_in = enc_out.astype(jnp.bfloat16)
    enc_branch, enc_attn_kept = attend_forward(enc_attn_in, enc_attn_in, images, live, enc_weights)
    enc_middle = start + enc_weights[10][0] * enc_branch
    enc_feed, enc_feed_kept = feed_forward(enc_middle, enc_weights)
    latent_f = enc_middle + enc_weights[10][1] * enc_feed
    query_start = jnp.dot(pick_masked, pos_table, precision=highest)
    query_out, query_normed, query_inverse = norm_forward(
        query_start, reg_weights[0][0], reg_weights[1][0]
    )
    latent_out, latent_normed, latent_inverse = norm_forward(
        latent_f, reg_weights[0][0], reg_weights[1][0]
    )
    query_in = query_out.astype(jnp.bfloat16)
    key_in = jnp.concatenate(
        [
            latent_out.astype(jnp.bfloat16).reshape(images, SET, model),
            query_in.reshape(images, SET, model),
        ],
        axis=1,
    ).reshape(-1, model)
    key_live = jnp.concatenate([live, live])
    reg_branch, reg_attn_kept = attend_forward(query_in, key_in, images, key_live, reg_weights)
    reg_middle = query_start + reg_weights[10][0] * reg_branch
    reg_feed, reg_feed_kept = feed_forward(reg_middle, reg_weights)
    regressed_f = reg_middle + reg_weights[10][1] * reg_feed
    reg_back = reg_weights
    grad_final = grad_out * live_rows
    reg_scale_late = jnp.sum(grad_final * reg_feed, axis=0)
    grad_from_feed, reg_gain_late, reg_shift_late, reg_feed_grads = feed_backward(
        reg_back[10][1] * grad_final, reg_feed_kept, reg_back
    )
    grad_reg_middle = grad_final + grad_from_feed
    reg_scale_early = jnp.sum(grad_reg_middle * reg_branch, axis=0)
    grad_query_in, grad_key_in, reg_attn_grads = attend_backward(
        reg_back[10][0] * grad_reg_middle, query_in, key_in, key_live, reg_attn_kept, reg_back
    )
    grad_key_in = grad_key_in.reshape(images, 2 * SET, model)
    grad_query_norm = grad_query_in + grad_key_in[:, SET:].reshape(-1, model)
    grad_latent_norm = grad_key_in[:, :SET].reshape(-1, model)
    back_query, reg_gain_query, reg_shift_query = norm_backward(
        grad_query_norm, query_normed, query_inverse, reg_back[0][0]
    )
    back_latent, reg_gain_key, reg_shift_key = norm_backward(
        grad_latent_norm, latent_normed, latent_inverse, reg_back[0][0]
    )
    grad_query_start = grad_reg_middle + back_query
    reg_grads = (
        (
            jnp.stack([reg_gain_query + reg_gain_key, reg_gain_late]),
            jnp.stack([reg_shift_query + reg_shift_key, reg_shift_late]),
        )
        + reg_attn_grads
        + reg_feed_grads
        + (jnp.stack([reg_scale_early, reg_scale_late]),)
    )
    enc_back = enc_weights
    grad_finish = grad_latent * live_rows + back_latent
    enc_scale_late = jnp.sum(grad_finish * enc_feed, axis=0)
    grad_from_feed, enc_gain_late, enc_shift_late, enc_feed_grads = feed_backward(
        enc_back[10][1] * grad_finish, enc_feed_kept, enc_back
    )
    grad_enc_middle = grad_finish + grad_from_feed
    enc_scale_early = jnp.sum(grad_enc_middle * enc_branch, axis=0)
    grad_as_query, grad_as_key, enc_attn_grads = attend_backward(
        enc_back[10][0] * grad_enc_middle, enc_attn_in, enc_attn_in, live, enc_attn_kept, enc_back
    )
    back_start, enc_gain_early, enc_shift_early = norm_backward(
        grad_as_query + grad_as_key, enc_normed, enc_inverse, enc_back[0][0]
    )
    grad_start = grad_enc_middle + back_start
    grad_table = jnp.dot(pick_visible.T, grad_start, precision=highest) + jnp.dot(
        pick_masked.T, grad_query_start, precision=highest
    )
    enc_grads = (
        (jnp.stack([enc_gain_early, enc_gain_late]), jnp.stack([enc_shift_early, enc_shift_late]))
        + enc_attn_grads
        + enc_feed_grads
        + (jnp.stack([enc_scale_early, enc_scale_late]),)
    )
    reg_shards = (
        lax.psum_scatter(reg_grads[0], ("dp", "fsdp"), scatter_dimension=1, tiled=True),
        lax.psum_scatter(reg_grads[1], ("dp", "fsdp"), scatter_dimension=1, tiled=True),
        lax.psum_scatter(reg_grads[2], ("dp", "fsdp"), scatter_dimension=0, tiled=True),
        lax.psum_scatter(reg_grads[3], ("dp", "fsdp"), scatter_dimension=0, tiled=True),
        lax.psum_scatter(reg_grads[4], ("dp", "fsdp"), scatter_dimension=0, tiled=True),
        lax.psum_scatter(reg_grads[5], ("dp", "fsdp"), scatter_dimension=0, tiled=True),
        lax.psum_scatter(reg_grads[6], ("dp", "fsdp"), scatter_dimension=0, tiled=True),
        lax.psum_scatter(reg_grads[7], ("dp", "fsdp"), scatter_dimension=0, tiled=True),
        lax.psum_scatter(reg_grads[8], ("dp", "fsdp"), scatter_dimension=0, tiled=True),
        lax.psum_scatter(reg_grads[9], ("dp", "fsdp"), scatter_dimension=0, tiled=True),
        lax.psum_scatter(reg_grads[10], ("dp", "fsdp"), scatter_dimension=1, tiled=True),
    )
    enc_shards = (
        lax.psum_scatter(grad_table, ("dp", "fsdp"), scatter_dimension=1, tiled=True),
        lax.psum_scatter(enc_grads[0], ("dp", "fsdp"), scatter_dimension=1, tiled=True),
        lax.psum_scatter(enc_grads[1], ("dp", "fsdp"), scatter_dimension=1, tiled=True),
        lax.psum_scatter(enc_grads[2], ("dp", "fsdp"), scatter_dimension=0, tiled=True),
        lax.psum_scatter(enc_grads[3], ("dp", "fsdp"), scatter_dimension=0, tiled=True),
        lax.psum_scatter(enc_grads[4], ("dp", "fsdp"), scatter_dimension=0, tiled=True),
        lax.psum_scatter(enc_grads[5], ("dp", "fsdp"), scatter_dimension=0, tiled=True),
        lax.psum_scatter(enc_grads[6], ("dp", "fsdp"), scatter_dimension=0, tiled=True),
        lax.psum_scatter(enc_grads[7], ("dp", "fsdp"), scatter_dimension=0, tiled=True),
        lax.psum_scatter(enc_grads[8], ("dp", "fsdp"), scatter_dimension=0, tiled=True),
        lax.psum_scatter(enc_grads[9], ("dp", "fsdp"), scatter_dimension=0, tiled=True),
        lax.psum_scatter(enc_grads[10], ("dp", "fsdp"), scatter_dimension=1, tiled=True),
    )
    pos_shard = enc_shards[0]
    weight_shards = tuple(
        (jnp.stack([early, late]) for early, late in zip(enc_shards[1:], reg_shards))
    )
    return (
        latent_f.astype(jnp.bfloat16),
        regressed_f.astype(jnp.bfloat16),
        grad_start,
        pos_shard,
    ) + weight_shards


def solution(mesh):
    in_specs = (
        P(("dp", "fsdp"), None),
        P(("dp", "fsdp"), None),
        P(("dp", "fsdp"), None),
        P(("dp", "fsdp"), None),
        P(None, ("dp", "fsdp")),
        P(None, None, ("dp", "fsdp")),
        P(None, None, ("dp", "fsdp")),
        P(None, ("dp", "fsdp"), None),
        P(None, ("dp", "fsdp")),
        P(None, ("dp", "fsdp"), None),
        P(None, ("dp", "fsdp")),
        P(None, ("dp", "fsdp"), None),
        P(None, ("dp", "fsdp")),
        P(None, ("dp", "fsdp"), None),
        P(None, ("dp", "fsdp")),
        P(None, None, ("dp", "fsdp")),
    )
    out_specs = (
        P(("dp", "fsdp"), None),
        P(("dp", "fsdp"), None),
        P(("dp", "fsdp"), None),
        P(None, ("dp", "fsdp")),
        P(None, None, ("dp", "fsdp")),
        P(None, None, ("dp", "fsdp")),
        P(None, ("dp", "fsdp"), None),
        P(None, ("dp", "fsdp")),
        P(None, ("dp", "fsdp"), None),
        P(None, ("dp", "fsdp")),
        P(None, ("dp", "fsdp"), None),
        P(None, ("dp", "fsdp")),
        P(None, ("dp", "fsdp"), None),
        P(None, ("dp", "fsdp")),
        P(None, None, ("dp", "fsdp")),
    )
    devices = mesh.shape["dp"] * mesh.shape["fsdp"]

    def step(*args):
        rows = args[7].shape[1]
        kernels = mesh.shape["fsdp"] == 4 and rows // (devices // 2) % 16 == 0
        run = jax.shard_map(
            functools.partial(fused, devices) if kernels else local,
            mesh=mesh,
            in_specs=in_specs,
            out_specs=out_specs,
            check_vma=False,
        )
        return run(*args)

    return step
```

```python
import functools
import math

import jax
import jax.numpy as jnp
import numpy as np
from jax import lax
from jax.experimental import pallas as pl
from jax.experimental.pallas import tpu as pltpu
from jax.sharding import PartitionSpec as P

HEAD_DIM = 64
VIS = 98
SET = 128
PATCHES = 196

MESH = pl.DeviceIdType.MESH
WIDE = jnp.float32
LOW = jnp.bfloat16


def lanes(start, size):
    return pl.ds(pl.multiple_of(start, 128), size)


class Place:
    def __init__(self, line):
        dp, fsdp = lax.axis_index("dp"), lax.axis_index("fsdp")
        self.line = line
        self.z, self.y = dp // 2, dp % 2
        self.x, self.core = fsdp // 2, fsdp % 2
        z, y, x, core = self.z, self.y, self.x, self.core
        first_y = jnp.where(core == 0, 1 - y, y)
        first_x = jnp.where(core == 0, x, 1 - x)
        second_y = jnp.where(core == 0, y, 1 - y)
        second_x = jnp.where(core == 0, 1 - x, x)
        self.own = 2 * y + x
        self.first = 2 * first_y + first_x
        self.second = 2 * second_y + second_x
        self.across = 2 * (1 - y) + (1 - x)
        self.twin = self.at(z, y, x, 1 - core)
        self.near = self.at(z, first_y, first_x, core)
        self.far = self.at(z, second_y, second_x, core)
        self.above = [
            self.at(lax.rem(z + step, line), y, x, core) for step in range(1, line)
        ]

    def at(self, z, y, x, core):
        return (2 * z + y, 2 * x + core)

    def greet(self):
        barrier = pltpu.get_barrier_semaphore()
        others = [self.twin, self.near, self.far] + self.above
        for other in others:
            pl.semaphore_signal(barrier, inc=1, device_id=other, device_id_type=MESH)
        pl.semaphore_wait(barrier, len(others))


class Copies:
    def __init__(self, send, recv):
        self.send, self.recv, self.used, self.sent = send, recv, 0, []

    def remote(self, source, target, device):
        copy = pltpu.make_async_remote_copy(
            src_ref=source,
            dst_ref=target,
            send_sem=self.send.at[self.used],
            recv_sem=self.recv.at[self.used],
            device_id=device,
            device_id_type=MESH,
        )
        self.used += 1
        copy.start()
        self.sent.append(copy)
        return copy

    def local(self, source, target):
        copy = pltpu.make_async_copy(source, target, self.send.at[self.used])
        self.used += 1
        copy.start()
        return copy

    def drain(self):
        for copy in self.sent:
            copy.wait_send()


def gather_steps(line, items, sources, shards, theirs, fulls, stages, send, recv, bring):
    count = len(items)
    place = Place(line)
    copies = Copies(send, recv)
    place.greet()
    swaps = [copies.remote(source, their, place.twin) for source, their in zip(sources, theirs)]
    arrived = set()
    sizes = [wide // 2 for _, _, _, wide in items]
    columns = [lanes(item[2] + place.core * half, half) for item, half in zip(items, sizes)]

    def stage(i):
        array, rows, first, _ = items[i]
        own, their = shards[array](), theirs[array]
        if array not in arrived:
            arrived.add(array)
            swaps[array].wait_recv()
        for which, (low_ref, high_ref) in ((0, (own, their)), (1, (their, own))):

            @pl.when(place.core == which)
            def _():
                part = pl.ds(first + which * sizes[i], sizes[i])
                both = jnp.concatenate(
                    [low_ref[:, part].astype(WIDE), high_ref[:, part].astype(WIDE)], axis=0
                )
                stages[i][...] = both.astype(LOW)

    def group(i, which):
        return fulls[items[i][0]].at[:, which, :, columns[i]]

    def spread(i):
        target = fulls[items[i][0]].at[place.z, place.own, :, columns[i]]
        own = copies.local(stages[i], target)
        return [own] + [copies.remote(stages[i], target, device) for device in place.above]

    def send_on(i, which, devices):
        return [copies.remote(group(i, which), group(i, which), device) for device in devices]

    def share(i, far, twin, onward):
        far.wait_recv()
        onward[0].wait_recv()
        more = send_on(i, place.second, [place.twin]) + send_on(i, place.across, [place.twin])
        return [twin, onward[1]] + more

    def complete(i, started):
        for copy in started:
            copy.wait_recv()
        bring(i)

    ahead, lead = 5, 2
    start = 9.0
    spreads, owned, last, shared = {}, {}, {}, {}

    def own_sends(i):
        if i + ahead < count:
            stage(i + ahead)
            spreads[i + ahead] = spread(i + ahead)
        spreads[i][0].wait()
        for copy in spreads[i][1:]:
            copy.wait_recv()
        owned[i] = send_on(i, place.own, [place.near, place.far, place.twin])

    for i in range(min(ahead, count)):
        stage(i)
        spreads[i] = spread(i)
    for i in range(min(lead, count)):
        yield start
        own_sends(i)
    for i in range(count + 2):
        if i < count:
            start += 3 * line * items[i][1] * sizes[i] * 2 / RATE
            if i + lead < count:
                yield start - 1.5
                own_sends(i + lead)
            yield start
            near, far, twin = owned[i]
            near.wait_recv()
            last[i] = (far, twin, send_on(i, place.first, [place.far, place.twin]))
        else:
            yield start + 2
        if 0 <= i - 1 < count:
            shared[i - 1] = share(i - 1, *last[i - 1])
        if 0 <= i - 2 < count:
            complete(i - 2, shared[i - 2])
    yield start
    copies.drain()


class Names:
    def __getattr__(self, word):
        return word


N = Names()
LINK = 64e3
RATE = 92e3
TWIN = 4e5


class Pace:
    def __init__(self, steps):
        self.steps, self.now = steps, 0.0
        self.due = next(steps)

    def advance(self):
        self.now = max(self.now, self.due)
        self.due = next(self.steps, None)

    def spend(self, time):
        self.now += time
        while self.due is not None and self.due <= self.now:
            self.advance()

    def until(self, reached):
        while not reached():
            self.advance()

    def finish(self):
        while self.due is not None:
            self.advance()
TILE = 256
ROOT = math.sqrt(2.0 / math.pi)
CUBE = 0.044715


def dot_nn(left, right):
    return lax.dot_general(left, right, (((1,), (0,)), ((), ())), preferred_element_type=WIDE)


def dot_nt(left, right):
    return lax.dot_general(left, right, (((1,), (1,)), ((), ())), preferred_element_type=WIDE)


def dot_tn(left, right):
    return lax.dot_general(left, right, (((0,), (0,)), ((), ())), preferred_element_type=WIDE)


def each(count, step, first=0, unroll=1):
    def run(k, carry):
        step(k)
        return carry

    lax.fori_loop(first, first + count, run, 0, unroll=unroll)


def row_blocks(total, block, step):
    each(total // block, lambda k: step(pl.ds(pl.multiple_of(k * block, block), block)), unroll=2)


def row(ref, k):
    return ref[pl.ds(k, 1), :]


def flat(value):
    return value.reshape(-1, value.shape[-1])


def add_rows(ref, k, value):
    ref[pl.ds(k, 1), :] += jnp.sum(value.astype(WIDE), axis=0, keepdims=True)


def live_rows(block, wide):
    return lax.broadcasted_iota(jnp.int32, (block, wide), 0) % SET < VIS


def selection(slots, wide):
    rows = lax.broadcasted_iota(jnp.int32, (32, wide), 0)
    return (lax.broadcasted_iota(jnp.int32, (32, wide), 1) == rows + slots).astype(LOW)


def unit_matrix(size):
    same = lax.broadcasted_iota(jnp.int32, (size, size), 0) == lax.broadcasted_iota(jnp.int32, (size, size), 1)
    return jnp.where(same, 1.0, 0.0)


def fill_picks(marks, first, target):
    wide = target.shape[1]

    def step(k):
        own = lax.broadcasted_iota(jnp.int32, (wide, SET), 0) == marks[pl.ds(first + k, 1), :]
        target[pl.ds(pl.multiple_of(k * SET, SET), SET), :] = jnp.where(own, 1.0, 0.0).T.astype(LOW)

    each(target.shape[0] // SET, step)


def fold_tables(model, rows, parts):
    entry = np.arange(model)
    source = rows * (entry // (parts * rows)) + entry % rows
    spots = (np.arange(model // parts)[:, None] == source[None, :]).astype(np.float32)
    column = entry % (parts * rows) // rows
    which = (np.arange(8)[:, None] == column[None, :]).astype(np.float32)
    return jnp.asarray(spots, LOW), jnp.asarray(which, WIDE)


class Buffers:
    def __init__(self, refs, sems):
        self.refs, self.sems, self.used = refs, sems, 0
        self.loading, self.saving = {}, []

    def __getitem__(self, name):
        if name in self.loading:
            self.loading.pop(name).wait()
        return self.refs[name]

    def copy(self, source, target):
        copy = pltpu.make_async_copy(source, target, self.sems.at[self.used])
        self.used += 1
        copy.start()
        return copy

    def load(self, name, source, target=None):
        self.loading[name] = self.copy(source, self.refs[name] if target is None else target)

    def wait(self, *names):
        for name in names:
            if name in self.loading:
                self.loading.pop(name).wait()

    def save(self, name, target):
        self.saving.append((name, self.copy(self.refs[name], target)))

    def saved(self, name):
        self.settle([entry for entry in self.saving if entry[0] == name])

    def settle(self, entries):
        for entry in entries:
            if any(entry is other for other in self.saving):
                entry[1].wait()
        self.saving = [other for other in self.saving if not any(other is entry for entry in entries)]

    def drain(self):
        for name in list(self.loading):
            self.loading.pop(name).wait()
        for _, copy in self.saving:
            copy.wait()


def call(body, ins, small, outs, scratch, sems, extra, name, collective, vmem):
    names = list(ins) + list(small) + list(outs) + list(scratch)

    def kernel(*refs):
        named = dict(zip(names, refs[: len(names)]))
        body(Buffers(named, refs[len(names)]), *refs[len(names) + 1 :])

    anywhere = pl.BlockSpec(memory_space=pl.ANY)
    results = pl.pallas_call(
        kernel,
        out_shape=list(outs.values()),
        in_specs=[anywhere] * len(ins) + [pl.BlockSpec(memory_space=pltpu.VMEM)] * len(small),
        out_specs=[anywhere] * len(outs),
        scratch_shapes=[pltpu.VMEM(*shape) for shape in scratch.values()]
        + [pltpu.SemaphoreType.DMA((sems,))]
        + extra,
        name=name,
        compiler_params=pltpu.CompilerParams(
            collective_id=collective, has_side_effects=True, vmem_limit_bytes=vmem
        ),
    )(*ins.values(), *small.values())
    return dict(zip(outs, results))


def norm_block(value, gain, shift):
    centered = value - jnp.mean(value, axis=-1, keepdims=True)
    inverse = lax.rsqrt(jnp.mean(centered * centered, axis=-1, keepdims=True) + 1e-06)
    normed = centered * inverse
    return normed * gain + shift, normed, inverse


def norm_back(value, grad, gain, sums, gain_row, shift_row):
    _, normed, inverse = norm_block(value, gain, 0.0)
    add_rows(sums, gain_row, grad * normed)
    add_rows(sums, shift_row, grad)
    scaled = grad * gain
    first = jnp.mean(scaled, axis=-1, keepdims=True)
    second = jnp.mean(scaled * normed, axis=-1, keepdims=True)
    return inverse * (scaled - first - normed * second)


def halves(value):
    low = lax.broadcasted_iota(jnp.int32, value.shape, 1) < HEAD_DIM
    zero = jnp.zeros_like(value)
    return jnp.concatenate([jnp.where(low, value, zero), jnp.where(low, zero, value)], axis=0)


def rejoin(value):
    rows = value.shape[0] // 2
    low = lax.broadcasted_iota(jnp.int32, (rows, value.shape[1]), 1) < HEAD_DIM
    return jnp.where(low, value[:rows], value[rows:])


def spot(k, pairs):
    return pl.ds(pl.multiple_of(k // pairs * SET, SET), SET), lanes(k % pairs * 128, 128)


def stacked(refs, at):
    parts = [ref[at[0], at[1]] for ref in refs]
    return parts[0] if len(parts) == 1 else jnp.concatenate(parts, axis=0)


def soft(keys, queries):
    scores = dot_nt(keys, queries) * (1.0 / math.sqrt(HEAD_DIM))
    scores = jnp.where(live_rows(*scores.shape), scores, -1e30)
    weighted = jnp.exp(scores - jnp.max(scores, axis=0, keepdims=True))
    return weighted / jnp.sum(weighted, axis=0, keepdims=True)


def in_pieces(count, piece, step, between):
    for first in range(0, count, piece):
        each(piece, step, first, piece)
        between()


def attend(queries, keys, values, mixed, between):
    pairs = queries.shape[1] // 128

    def step(k):
        at = spot(k, pairs)
        weights = soft(stacked(keys, at), halves(queries[at[0], at[1]])).astype(LOW)
        mixed[at[0], at[1]] = rejoin(dot_tn(weights, stacked(values, at))).astype(LOW)

    in_pieces(queries.shape[0] // SET * pairs, 4, step, between)


def attend_back(grad_mixed, queries, keys, values, grad_queries, grad_keys, grad_values, between):
    pairs = queries.shape[1] // 128
    factor = 1.0 / math.sqrt(HEAD_DIM)

    def step(k):
        at = spot(k, pairs)
        key, value = stacked(keys, at), stacked(values, at)
        query, grad = halves(queries[at[0], at[1]]), halves(grad_mixed[at[0], at[1]])
        weights = soft(key, query)
        back_value = dot_nn(weights.astype(LOW), grad).astype(LOW)
        grad_soft = dot_nt(value, grad)
        inner = jnp.sum(grad_soft * weights, axis=0, keepdims=True)
        grad_scores = (weights * (grad_soft - inner)).astype(LOW)
        back_key = (dot_nn(grad_scores, query) * factor).astype(LOW)
        grad_queries[at[0], at[1]] = (rejoin(dot_tn(grad_scores, key)) * factor).astype(LOW)
        for which in range(len(keys)):
            part = slice(which * SET, (which + 1) * SET)
            grad_keys[which][at[0], at[1]] = back_key[part]
            grad_values[which][at[0], at[1]] = back_value[part]

    in_pieces(queries.shape[0] // SET * pairs, 4, step, between)


def project(source, weight, start, bias, target):
    def step(k):
        part = lanes(k * TILE, TILE)
        value = dot_nn(source[...], flat(weight[:, :, :, lanes(start + k * TILE, TILE)]))
        if bias is not None:
            value = value + bias[:, part]
        target[:, part] = value.astype(LOW)

    each(target.shape[1] // TILE, step, unroll=3)


def residual(source, weight, bias, scale, before, after, branch, first, count, low=None):
    def step(k):
        part = lanes(k * TILE, TILE)
        value = dot_nn(source[...], flat(weight[:, :, :, part])) + bias[:, part]
        branch[:, part] = value.astype(LOW)
        total = before[:, part] + scale[:, part] * value
        if after is not None:
            after[:, part] = total
        if low is not None:
            low[:, part] = total.astype(LOW)

    each(count, step, first, count)


def rise(source, weight, bias, active, slope, first, count):
    per = source.shape[1] // TILE

    def step(k):
        part = lanes(k * TILE, TILE)
        own = bias[pl.ds(k // per, 1), lanes(k % per * TILE, TILE)]
        value = dot_nn(source[...], flat(weight[:, :, :, part])) + own
        square = value * value
        curve = jnp.tanh(value * (ROOT + (ROOT * CUBE) * square))
        half = 0.5 + 0.5 * curve
        active[:, part] = (value * half).astype(LOW)
        bend = value * (half - half * curve) * (ROOT + (3.0 * ROOT * CUBE) * square)
        slope[:, part] = (half + bend).astype(LOW)

    each(count, step, first, count)


def small_vectors(b, parts):
    extra, vec = b[N.extra], b[N.vec]
    pick = selection(PATCHES, extra.shape[1])
    vec[...] = dot_nt(pick, extra[...])
    at = 16
    for count, spots, which in ((parts[0], b[N.spots_q], b[N.which_q]), (parts[1], b[N.spots_f], b[N.which_f])):
        rows = spots.shape[0]
        found = []
        for chunk in range(count):
            held = dot_nt(pick, extra[pl.ds(chunk * rows, rows), :]).astype(LOW)
            found.append(dot_nn(held, spots[...]))
        for block in range(2):
            for chunk in range(count):
                base = at + block * count
                total = sum(
                    found[chunk][base + j : base + j + 1] * which[j : j + 1, :] for j in range(count)
                )
                vec[base + chunk : base + chunk + 1, :] = total
        at += 2 * count


def forward_compute(b, need, spend, keep, release):
    rows, model = b[N.start].shape
    need(N.extra, 0, 0)
    b[N.extra][...] = flat(b[N.extra4][...])
    small_vectors(b, (2, 4))
    vec, extra = b[N.vec], b[N.extra]
    keep(N.vec)
    spend(2)

    def vector(k):
        return vec.at[pl.ds(k, 1)]

    def open_rows(r):
        start = b[N.patches][r, :].astype(WIDE) + dot_nt(b[N.pick_vis][r, :], extra[...])
        b[N.start][r, :] = start
        b[N.a0][r, :] = norm_block(start, row(vec, 0), row(vec, 4))[0].astype(LOW)
        query = dot_nt(b[N.pick_hid][r, :], extra[...])
        b[N.query][r, :] = query
        b[N.aq][r, :] = norm_block(query, row(vec, 2), row(vec, 6))[0].astype(LOW)

    b[N.patches]
    row_blocks(rows, 64, open_rows)
    for name in (N.start, N.a0, N.query, N.aq):
        keep(name)
    spend(4)

    def norm_into(source, target, gain, shift):
        def step(r):
            b[target][r, :] = norm_block(b[source][r, :], row(vec, gain), row(vec, shift))[0].astype(LOW)

        row_blocks(rows, 64, step)
        keep(target)
        spend(1)

    def attention(block, sources, keys, values, before, after):
        query, mixed, branch = N.q + str(block), N.mix + str(block), N.br + str(block)
        for part, bias in enumerate((16 + 2 * block, None, 17 + 2 * block)):
            need(N.qkv, block, part)
            targets = ([query], keys, values)[part]
            for source, target in zip(sources[part], targets):
                shift = None if bias is None else vector(bias)
                project(b[source], b[N.w_qkv], part * model, shift, b[target])
                keep(target)
                spend(1)
        release(N.qkv)
        attend(
            b[query], [b[name] for name in keys], [b[name] for name in values], b[mixed],
            lambda: spend(1.5),
        )
        keep(mixed)
        need(N.proj, block, 0)
        residual(
            b[mixed], b[N.w_proj], vector(12 + block), vector(8 + 2 * block), b[before], b[after], b[branch],
            0, model // TILE,
        )
        release(N.proj)
        keep(branch)
        keep(after)
        spend(1.2)

    def feed(block, before, after, inner, low):
        branch = N.fd + str(block)
        norm_into(before, inner, 2 * block + 1, 4 + 2 * block + 1)
        b.saved(N.active)
        b.saved(N.slope)
        hidden = b[N.active].shape[1]
        for piece in range(hidden // model):
            need(N.fc1, block, piece)
            rise(
                b[inner], b[N.w_fc1], vec.at[pl.ds(20 + 4 * block, 4)], b[N.active], b[N.slope],
                piece * (model // TILE), model // TILE,
            )
            spend(2.2)
        release(N.fc1)
        keep(N.active, block)
        keep(N.slope, block)
        for piece in range(model // TILE):
            need(N.fc2, block, piece)
            residual(
                b[N.active], b[N.w_fc2], vector(14 + block), vector(8 + 2 * block + 1), b[before],
                None if after is None else b[after], b[branch], piece, 1, b[low],
            )
            spend(1.3)
        release(N.fc2)
        keep(low)
        keep(branch)

    attention(0, ([N.a0], [N.a0], [N.a0]), [N.k0], [N.v0], N.start, N.mid0)
    feed(0, N.mid0, N.lat, N.a20, N.latent)
    keep(N.lat)
    norm_into(N.lat, N.ak, 2, 6)
    both = [N.ak, N.aq]
    attention(1, ([N.aq], both, both), [N.k1, N.k2], [N.v1, N.v2], N.query, N.mid1)
    feed(1, N.mid1, None, N.a21, N.regressed)


KEPT_WIDE = (N.start, N.query, N.mid0, N.lat, N.mid1)
KEPT_LOW = (
    N.a0, N.aq, N.a20, N.ak, N.a21, N.q0, N.k0, N.v0, N.mix0, N.br0, N.fd0,
    N.q1, N.k1, N.v1, N.k2, N.v2, N.mix1, N.br1, N.fd1, N.latent, N.regressed,
)


def shape_of(*args):
    return jax.ShapeDtypeStruct(*args)


def cut(shapes):
    model = shapes[N.proj][1]
    pieces = []
    for kind, wide in ((N.qkv, model), (N.proj, model), (N.fc1, model), (N.fc2, TILE)):
        pieces += [(kind, k, k * wide, wide) for k in range(shapes[kind][1] // wide)]
    return pieces


def forward(patches, marks, vectors, wide_rows, weights, line, tables):
    rows, model = patches.shape
    kinds = (N.qkv, N.proj, N.fc1, N.fc2)
    shapes = {kind: (2 * weight.shape[1], weight.shape[2]) for kind, weight in zip(kinds, weights)}
    shapes[N.extra] = (2 * vectors[0].shape[-1], wide_rows)
    hidden = shapes[N.fc1][1]
    whole = {kind: (line, 4) + shape for kind, shape in shapes.items()}
    arrays = [(N.extra, 0)] + [(kind, block) for block in (0, 1) for kind in kinds]
    names = [kind + str(block) for kind, block in arrays]
    items = [(0, N.extra, 0, 0, 0, shapes[N.extra][1])]
    for block in (0, 1):
        for kind, piece, first, wide in cut(shapes):
            items.append((arrays.index((kind, block)), kind, block, piece, first, wide))
    outs = {name: shape_of(whole[kind], LOW) for name, (kind, _) in zip(names, arrays)}
    outs[N.vec_out] = shape_of((32, model), WIDE)
    for name in KEPT_WIDE:
        outs[name + N._out] = shape_of((rows, model), WIDE)
    for name in KEPT_LOW:
        outs[name + N._out] = shape_of((rows, model), LOW)
    for block in (0, 1):
        for name in (N.active, N.slope):
            outs[name + str(block) + N._out] = shape_of((rows, hidden), LOW)
    scratch = {name: ((rows, model), WIDE) for name in KEPT_WIDE}
    scratch.update({name: ((rows, model), LOW) for name in KEPT_LOW + (N.patches,)})
    scratch[N.active] = scratch[N.slope] = ((rows, hidden), LOW)
    scratch[N.vec] = ((32, model), WIDE)
    scratch[N.extra4] = (whole[N.extra], LOW)
    scratch[N.extra] = ((model, shapes[N.extra][1]), LOW)
    for kind in kinds:
        scratch[N.w_ + kind] = (whole[kind], LOW)
    for name, (kind, _) in zip(names, arrays):
        held = (shapes[kind][0] // 2, shapes[kind][1])
        scratch[N.own_ + name] = scratch[N.their_ + name] = (held, LOW)
    for i, (a, kind, _, _, _, wide) in enumerate(items):
        scratch[N.stage + str(i)] = ((shapes[kind][0], wide // 2), LOW)
    scratch[N.pick_vis] = scratch[N.pick_hid] = ((rows, shapes[N.extra][1]), LOW)
    ins = {N.patches_in: patches}
    ins.update({kind + N._in: weight for kind, weight in zip(kinds, weights)})
    small = {N.marks: marks}
    small.update({N.vector + str(k): vector for k, vector in enumerate(vectors)})
    scratch[N.extra_rows] = ((wide_rows, vectors[0].shape[-1]), WIDE)
    small.update(dict(zip((N.spots_q, N.which_q, N.spots_f, N.which_f), tables)))
    pairs = len(arrays) + len(items) * (line + 8)
    extra = [pltpu.SemaphoreType.DMA((pairs,)), pltpu.SemaphoreType.DMA((pairs,))]

    def body(b, send, recv):
        own = b[N.own_ + names[0]]
        stacked_rows, at = b[N.extra_rows], 0
        stacked_rows[...] = jnp.zeros(stacked_rows.shape, WIDE)
        for k in range(len(vectors)):
            ref = b[N.vector + str(k)]
            for place in [()] if len(ref.shape) == 2 else [(0,), (1,)]:
                value = ref[place + (slice(None), slice(None))].astype(WIDE)
                wide = stacked_rows.shape[1]
                if value.shape[1] == wide:
                    stacked_rows[at : at + value.shape[0], :] = value
                    at += value.shape[0]
                    continue
                for block in range(value.shape[0]):
                    for first in range(0, value.shape[1], wide):
                        stacked_rows[at : at + 1, :] = value[block : block + 1, first : first + wide]
                        at += 1
        own[...] = dot_nt(unit_matrix(own.shape[0]).astype(LOW), stacked_rows[...].astype(LOW)).astype(LOW)
        sources = [own] + [b[kind + N._in].at[block] for kind, block in arrays[1:]]
        b.load(N.patches, b[N.patches_in])
        for name, source in list(zip(names, sources))[1:]:
            b.load(N.own_ + name, source)
        free, held, loaded = {(N.extra, 0)} | {(kind, 0) for kind in kinds}, [], {}

        def bring(i):
            a, kind, block, piece, first, wide = items[i]
            if (kind, block) not in free:
                held.append(i)
                return
            part = (slice(None),) * 3 + (pl.ds(first, wide),)
            target = b.refs[N.extra4 if kind == N.extra else N.w_ + kind].at[part]
            b.load(N.item + str(i), b[names[a]].at[part], target)
            loaded[(kind, block, piece)] = N.item + str(i)

        shards = [lambda name=name: b[N.own_ + name] for name in names]
        steps = gather_steps(
            line, [(a, shapes[kind][0], first, wide) for a, kind, _, _, first, wide in items], sources, shards,
            [b[N.their_ + name] for name in names], [b[name] for name in names],
            [b[N.stage + str(i)] for i in range(len(items))], send, recv, bring,
        )
        pace = Pace(steps)
        for first, name in ((0, N.pick_vis), (rows // SET, N.pick_hid)):
            fill_picks(b[N.marks], first, b[name])

        def need(kind, block, piece):
            pace.until(lambda: (kind, block, piece) in loaded)
            b.wait(loaded[(kind, block, piece)])

        def release(kind):
            free.add((kind, 1))
            for i in [i for i in held if items[i][1] == kind]:
                held.remove(i)
                bring(i)

        def keep(name, block=None):
            b.save(name, b[name + ("" if block is None else str(block)) + N._out])

        forward_compute(b, need, pace.spend, keep, release)
        pace.finish()
        b.drain()

    return call(body, ins, small, outs, scratch, 128, extra, N.forward, 0, 63 << 20)


class Reducer:
    def __init__(self, line, items, slots, grads, outs, shared, single, send, recv, credit, ended):
        self.line, self.items, self.slots = line, items, slots
        self.grads, self.outs, self.shared, self.single = grads, outs, shared, single
        self.credit, self.ended = credit, ended
        self.place = Place(line)
        self.copies = Copies(send, recv)
        self.place.greet()
        self.ready, self.begun, self.state = set(), {}, {}
        self.next, self.due = [0] * 5, {}
        self.now = self.link_free = self.line_free = 0.0
        self.sends = {i: [] for i in range(len(items))}
        self.steps = [self.pair, self.near, self.along, self.swap, self.finish]

    def remote(self, i, source, target, device):
        copy = self.copies.remote(source, target, device)
        self.sends[i].append(copy)
        return copy

    def unit(self, i):
        return self.line * self.items[i][0] * self.half(i) * 2

    def half(self, i):
        return self.items[i][2] // 2

    def columns(self, i, core):
        return lanes(self.items[i][1] + core * self.half(i), self.half(i))

    def earlier(self, i):
        return [j for j in range(i) if self.slots[j] == self.slots[i]]

    def later(self, i):
        return [j for j in range(i + 1, len(self.items)) if self.slots[j] == self.slots[i]]

    def buffers(self, i):
        mine, twins, owned, final, other = self.shared[self.slots[i]]
        through, direct, joined, arrived = self.single[i]
        return mine, twins, through, direct, joined, owned, arrived, final, other

    def begin(self, i):
        place = self.place
        mine, twins = self.buffers(i)[:2]
        if self.earlier(i):
            pl.semaphore_wait(self.credit.at[self.slots[i]], 1)
        away = self.remote(
            i, self.grads[i].at[:, :, :, self.columns(i, 1 - place.core)], twins, place.twin
        )
        here = self.copies.local(self.grads[i].at[:, :, :, self.columns(i, place.core)], mine)
        self.begun[i] = (away, here)
        self.due[0, i] = self.now + 2.0 + 4 * self.unit(i) / TWIN

    def begin_some(self):
        i = len(self.begun)
        while i < len(self.items) and i in self.ready and i <= self.next[0] + 2:
            if any(j >= self.next[4] for j in self.earlier(i)):
                return
            self.begin(i)
            i += 1

    def pair(self, i):
        place = self.place
        mine, twins, through, direct = self.buffers(i)[:4]
        away, here = self.begun[i]
        away.wait_recv()
        here.wait()

        def step(k):
            a, c = k // 4, k % 4
            mine[a, c] = mine[a, c] + twins[a, c]

        each(self.line * 4, step, unroll=2)
        self.state[i] = [
            self.remote(i, mine.at[:, place.across], through, place.far),
            self.remote(i, mine.at[:, place.second], direct, place.far),
        ]
        unit = self.unit(i) / LINK
        start = max(self.now, self.link_free)
        self.link_free = start + 3 * unit
        self.due[1, i] = start + 1.0 + 1.6 * unit
        self.now += 0.5 + self.unit(i) / 1e6

    def near(self, i):
        place = self.place
        mine, _, through, _, joined = self.buffers(i)[:5]
        self.state[i][0].wait_recv()

        def step(k):
            through[k] = through[k] + mine[k, place.first]

        each(self.line, step)
        self.state[i].append(self.remote(i, through, joined, place.near))
        self.due[2, i] = self.now + 1.0 + 1.6 * self.unit(i) / LINK
        self.now += 0.3

    def along(self, i):
        place, line = self.place, self.line
        mine, _, _, direct, joined, owned, arrived = self.buffers(i)[:7]
        self.state[i][1].wait_recv()
        self.state[i][2].wait_recv()

        def step(k):
            total = mine[k, place.own].astype(WIDE) + direct[k].astype(WIDE) + joined[k].astype(WIDE)
            owned[k] = total.astype(LOW)

        each(line, step)
        self.state[i] = [
            self.remote(
                i, owned.at[lax.rem(place.z + k + 1, line)], arrived.at[k], place.above[k]
            )
            for k in range(line - 1)
        ]
        start = max(self.now, self.line_free)
        self.line_free = start + 2 * self.unit(i) / LINK
        self.due[3, i] = self.line_free + 1.0
        self.now += 0.3

    def swap(self, i):
        place, rows = self.place, self.items[i][0] // 2
        owned, arrived, final, other = self.buffers(i)[5:]
        for copy in self.state[i]:
            copy.wait_recv()
        total = owned[place.z].astype(WIDE)
        for k in range(self.line - 1):
            total = total + arrived[k].astype(WIDE)
        final[...] = total
        away = pl.ds(pl.multiple_of((1 - place.core) * rows, 8), rows)
        self.state[i] = [self.remote(i, final.at[away], other, place.twin)]
        self.due[4, i] = self.now + 2.0
        self.now += 0.2

    def finish(self, i):
        place = self.place
        final, other = self.buffers(i)[7:]
        rows = self.items[i][0] // 2
        own = pl.ds(pl.multiple_of(place.core * rows, 8), rows)
        self.outs[i][:, self.columns(i, place.core)] = final[own]
        self.state[i][0].wait_recv()
        self.outs[i][:, self.columns(i, 1 - place.core)] = other[...]
        for copy in self.sends[i]:
            copy.wait_send()
        if self.later(i):
            pl.semaphore_signal(
                self.credit.at[self.slots[i]], inc=1, device_id=place.twin, device_id_type=MESH
            )
        self.ended(i)

    def able(self):
        found = []
        for stage in range(5):
            i = self.next[stage]
            if (i in self.begun) if stage == 0 else (i < self.next[stage - 1]):
                found.append((self.due[stage, i], -stage))
        return sorted(found)

    def run(self, stage):
        self.now = max(self.now, self.due[stage, self.next[stage]])
        self.steps[stage](self.next[stage])
        self.next[stage] += 1
        self.begin_some()

    def spend(self, time):
        self.now += time
        self.begin_some()
        while True:
            found = [entry for entry in self.able() if entry[0] <= self.now]
            if not found:
                return
            self.run(-found[0][1])

    def complete(self):
        self.begin_some()
        while self.next[4] < len(self.items):
            self.run(-self.able()[0][1])


def backward_compute(b, block, keys, spend, emit, bring):
    rows, model = b[N.acc].shape
    vec, sums = b[N.vec], b[N.sums]
    scale_row, feed_bias = 8 + 2 * block, 14 + block
    res, acc, gm, turned = b[N.res], b[N.acc], b[N.gm], b[N.turn]

    def close_rows(r):
        grad = res[r, :]
        if block:
            grad = jnp.where(live_rows(128, model), grad, 0.0)
            res[r, :] = grad
        add_rows(sums, scale_row + 1, grad * b[N.fd][r, :].astype(WIDE))
        low = (row(vec, scale_row + 1) * grad).astype(LOW)
        gm[r, :] = low
        add_rows(sums, feed_bias, low)

    b[N.fd]
    row_blocks(rows, 128, close_rows)
    if block:
        b.load(N.fd, b[N.ak_out])
    spend(2.5)

    def turn(value, start=0):
        turned[:, start : start + rows] = value.T

    def weight_grad(right, first, stage, depth):
        def step(k):
            value = dot_nn(turned[:, :depth], right[:, lanes(first + k * TILE, TILE)])
            shape = stage.shape[:-1] + (TILE,)
            stage[..., lanes(k * TILE, TILE)] = value.reshape(shape).astype(LOW)

        each(model // TILE, step, unroll=3)

    w_fc2, slope = b[N.w_fc2], b[N.slope]
    chunks = slope.shape[1] // model
    turn(b[N.inner][...])
    bring(N.inner)
    for chunk in range(chunks):
        part = slice(chunk * model, (chunk + 1) * model)

        def hidden_rows(r):
            value = dot_nt(gm[r, :], flat(w_fc2[chunk]))
            low = (value * slope[r, part].astype(WIDE)).astype(LOW)
            slope[r, part] = low
            add_rows(sums, 20 + 4 * block + chunk, low)

        row_blocks(rows, 256, hidden_rows)
        stage = N.stage + str(chunk % 2)
        b.saved(stage)
        weight_grad(slope, chunk * model, b[stage], rows)
        emit(N.fc1, chunk, stage)
        spend(3.2)
    bring(N.w_fc2)
    active = b[N.active]
    for chunk in range(chunks):
        turn(active[:, chunk * model : (chunk + 1) * model])
        b.saved(N.stage2)
        weight_grad(gm, 0, b[N.stage2], rows)
        emit(N.fc2, chunk, N.stage2)
        spend(2.2)
    bring(N.active)
    w_fc1 = b[N.w_fc1]
    for chunk in range(chunks):
        part = slice(chunk * model, (chunk + 1) * model)

        def inner_rows(r):
            value = dot_nt(slope[r, part], flat(w_fc1[:, :, :, part]))
            if chunk:
                value = acc[r, :] + value
            acc[r, :] = value

        row_blocks(rows, 256, inner_rows)
        spend(1.4)
    bring(N.slope)
    b.load(N.w_proj, b[N.w_ + N.proj + str(block)], w_fc1.at[:, :, :, 3 * model :])
    b.load(N.w_qkv, b[N.w_ + N.qkv + str(block)], w_fc1.at[:, :, :, : 3 * model])
    branch = b[N.br]

    def middle_rows(r):
        back = norm_back(
            b[N.mid][r, :], acc[r, :], row(vec, 2 * block + 1), sums, 2 * block + 1, 4 + 2 * block + 1
        )
        grad = res[r, :] + back
        res[r, :] = grad
        add_rows(sums, scale_row, grad * branch[r, :].astype(WIDE))
        low = (row(vec, scale_row) * grad).astype(LOW)
        gm[r, :] = low
        add_rows(sums, 12 + block, low)

    b[N.mid]
    row_blocks(rows, 64, middle_rows)
    b.load(N.mid, b[N.query_out if block else N.start_out])
    bring(N.br)
    spend(3)
    turn(b[N.mix][...])
    b.saved(N.stage0)
    weight_grad(gm, 0, b[N.stage0], rows)
    emit(N.proj, 0, N.stage0)
    spend(2.2)
    b.wait(N.w_proj)
    w_qkv, w_proj = w_fc1.at[:, :, :, : 3 * model], w_fc1.at[:, :, :, 3 * model :]

    def mixed_rows(r):
        b[N.mix][r, :] = dot_nt(gm[r, :], flat(w_proj[...])).astype(LOW)

    row_blocks(rows, 256, mixed_rows)
    spend(1.2)
    query, key, value = b[N.query], b[N.key], b[N.value]
    b.wait(N.key2, N.value2)
    queries = b[N.aq]
    key_parts = [key.at[pl.ds(k * rows, rows)] for k in range(keys)]
    value_parts = [value.at[pl.ds(k * rows, rows)] for k in range(keys)]
    attend_back(
        b[N.mix], query, key_parts, value_parts, query, key_parts, value_parts,
        lambda: spend(1.7 + 0.5 * keys),
    )
    bring(N.mix)

    def bias_rows(r):
        add_rows(sums, 16 + 2 * block, query[r, :])
        for k in range(keys):
            add_rows(sums, 17 + 2 * block, value_parts[k][r, :])

    row_blocks(rows, 128, bias_rows)
    if block:
        turn(b[N.fd][...])
        turn(queries[...], rows)
        bring(N.fd)
    else:
        turn(queries[...])
    depth = pl.ds(0, keys * rows)
    for chunk, right in ((1, key.at[depth]), (2, value.at[depth])):
        stage = N.stage + str(chunk % 2)
        b.saved(stage)
        weight_grad(right, 0, b[stage], keys * rows)
        emit(N.qkv, chunk, stage)
        spend(1 + 1.3 * keys)
    if block:
        turn(queries[...])
    bring(N.aq)
    b.saved(N.stage1)
    weight_grad(query, 0, b[N.stage1], rows)
    emit(N.qkv, 0, N.stage1)
    spend(2.2)
    b.wait(N.w_qkv)

    def back(parts):
        def step(r):
            total = 0.0
            for ref, chunk in parts:
                total = total + dot_nt(ref[r, :], flat(w_qkv[:, :, :, chunk * model : (chunk + 1) * model]))
            acc[r, :] = total

        row_blocks(rows, 256, step)

    gain, shift = 2 * block, 4 + 2 * block
    back([(query, 0), (key_parts[keys - 1], 1), (value_parts[keys - 1], 2)])
    spend(3.3)
    b[N.mid]

    def start_rows(r):
        grad = res[r, :] + norm_back(b[N.mid][r, :], acc[r, :], row(vec, gain), sums, gain, shift)
        res[r, :] = grad
        gm[r, :] = grad.astype(LOW)

    row_blocks(rows, 64, start_rows)
    if block:
        b.load(N.mid, b[N.lat_out])
        b.load(N.res, b[N.grad_latent])
    spend(2.5)
    fill_picks(b[N.marks], rows // SET * block, b[N.pick])
    table = dot_tn(gm[...], b[N.pick][...])
    if block:
        b[N.table][...] = table
        back([(key_parts[0], 1), (value_parts[0], 2)])
        bring(N.query, N.key, N.value, N.w_fc1)
        spend(3)
        b[N.mid], b[N.res]

        def latent_pair(k):
            for part in range(2):
                r = pl.ds(pl.multiple_of(k * SET + part * 64, 64), 64)
                grad = res[r, :]
                live = lax.broadcasted_iota(jnp.int32, grad.shape, 0) + part * 64 < VIS
                res[r, :] = jnp.where(live, grad, 0.0) + norm_back(
                    b[N.mid][r, :], acc[r, :], row(vec, gain), sums, gain, shift
                )

        each(rows // SET, latent_pair)
        bring(N.mid)
        spend(2.5)
    else:
        b[N.table][...] += table


def table_of_sums(b, parts):
    table, sums = b[N.table], b[N.sums]
    pick = selection(PATCHES, table.shape[1])
    plain = lax.broadcasted_iota(jnp.int32, sums.shape, 0) < 16
    table[...] += dot_tn(jnp.where(plain, sums[...], 0.0).astype(LOW), pick)
    at = 16
    lines = lax.broadcasted_iota(jnp.int32, sums.shape, 0)
    for count, spots, which in ((parts[0], b[N.spots_q], b[N.which_q]), (parts[1], b[N.spots_f], b[N.which_f])):
        rows = spots.shape[0]
        for chunk in range(count):
            spread = jnp.zeros(sums.shape, WIDE)
            for block in range(2):
                base = at + block * count
                for j in range(count):
                    entry = sums[base + chunk : base + chunk + 1, :] * which[j : j + 1, :]
                    spread = spread + jnp.where(lines == base + j, entry, 0.0)
            held = dot_nt(spots[...], spread.astype(LOW)).astype(LOW)
            table[pl.ds(chunk * rows, rows), :] += dot_nn(held, pick)
        at += 2 * count


HELD = (
    {
        N.fd: N.fd0, N.active: N.active0, N.slope: N.slope0, N.inner: N.a20, N.mid: N.mid0, N.br: N.br0,
        N.mix: N.mix0, N.query: N.q0, N.key: N.k0, N.value: N.v0, N.aq: N.a0,
    },
    {
        N.fd: N.fd1, N.active: N.active1, N.slope: N.slope1, N.inner: N.a21, N.mid: N.mid1, N.br: N.br1,
        N.mix: N.mix1, N.query: N.q1, N.key: N.k1, N.value: N.v1, N.aq: N.aq,
    },
)


def backward(f, grad_out, grad_latent, marks, line, tables):
    rows, model = f[N.mid0_out].shape
    hidden = f[N.active0_out].shape[1]
    wide = f[N.extra0].shape[3]
    shapes = {
        N.fc2: (hidden // (4 * line), model),
        N.fc1: (model // (4 * line), hidden),
        N.proj: (model // (4 * line), model),
        N.qkv: (model // (4 * line), 3 * model),
        N.extra: (model // (4 * line), wide),
    }
    whole = {kind: (line, 4) + shape for kind, shape in shapes.items()}
    pieces = {kind: [] for kind in shapes}
    for kind, piece, first, columns in cut(shapes):
        pieces[kind].append((piece, first, columns))
    pieces[N.extra] = [(0, 0, wide)]
    pieces[N.qkv] = pieces[N.qkv][1:] + pieces[N.qkv][:1]
    made = [N.fc1, N.fc2, N.proj, N.qkv]
    order_of = [(kind, block) for block in (1, 0) for kind in made] + [(N.extra, 0)]
    items, owners, counts, slots = [], [], {}, []
    for kind, block in order_of:
        for piece, first, columns in pieces[kind]:
            items.append((shapes[kind][0], first, columns))
            owners.append((kind, block, piece))
            shape = (shapes[kind][0], columns // 2)
            counts[shape] = counts.get(shape, 0) + 1
            slots.append((shape, (counts[shape] - 1) % (3 if kind == N.fc2 else 4)))
    held = sorted(set(slots))
    slots = [held.index(slot) for slot in slots]
    ins = {N.res_in: grad_out, N.grad_latent: grad_latent}
    for name in (N.query, N.start, N.lat, N.k2, N.v2, N.ak, N.vec):
        ins[name + N._out] = f[name + N._out]
    for block in (1, 0):
        for kind in made:
            ins[N.w_ + kind + str(block)] = f[kind + str(block)]
        for source in HELD[block].values():
            ins[N.in_ + source] = f[source + N._out]
    small = {N.marks: marks}
    small.update(dict(zip((N.spots_q, N.which_q, N.spots_f, N.which_f), tables)))
    outs = {N.g_ + kind + str(block): shape_of(whole[kind], LOW) for kind, block in order_of}
    for kind in made:
        outs[N.out_ + kind] = shape_of((2, shapes[kind][0] // 2, shapes[kind][1]), WIDE)
    outs[N.out_extra] = shape_of((wide, shapes[N.extra][0] // 2), WIDE)
    outs[N.res_out] = shape_of((rows, model), WIDE)
    scratch = {name: ((rows, model), WIDE) for name in (N.res, N.acc, N.mid)}
    for name in (N.fd, N.inner, N.br, N.mix, N.query, N.gm, N.aq):
        scratch[name] = ((rows, model), LOW)
    scratch[N.key] = scratch[N.value] = ((2 * rows, model), LOW)
    scratch[N.turn] = ((model, 2 * rows), LOW)
    scratch[N.active] = scratch[N.slope] = ((rows, hidden), LOW)
    scratch[N.w_fc1], scratch[N.w_fc2] = (whole[N.fc1], LOW), (whole[N.fc2], LOW)
    scratch[N.stage0] = scratch[N.stage1] = (whole[N.proj], LOW)
    scratch[N.stage2] = (whole[N.fc2][1:], LOW)
    scratch[N.vec] = scratch[N.sums] = ((32, model), WIDE)
    scratch[N.table] = ((model, wide), WIDE)
    scratch[N.pick] = ((rows, wide), LOW)
    scratch[N.rows_extra] = ((wide, shapes[N.extra][0] // 2), WIDE)
    scratch[N.table4] = (whole[N.extra], LOW)
    for kind, block in order_of:
        scratch[N.shard_ + kind + str(block)] = ((shapes[kind][0] // 2, shapes[kind][1]), WIDE)
    extra = []
    for (r, half), _ in held:
        extra += [pltpu.VMEM((line, 4, r, half), LOW)] * 2
        extra += [pltpu.VMEM((line, r, half), LOW), pltpu.VMEM((r, half), WIDE)]
        extra += [pltpu.VMEM((r // 2, half), WIDE)]
    for r, _, columns in items:
        half = columns // 2
        extra += [pltpu.VMEM((line, r, half), LOW)] * 3 + [pltpu.VMEM((line - 1, r, half), LOW)]
    pairs = len(items) * (line + 5)
    extra += [pltpu.SemaphoreType.DMA((pairs,))] * 2 + [pltpu.SemaphoreType.REGULAR((len(held),))]

    def body(b, *refs):
        shared = [refs[5 * k : 5 * k + 5] for k in range(len(held))]
        rest = refs[5 * len(held) :]
        single = [rest[4 * k : 4 * k + 4] for k in range(len(items))]
        send, recv, credit = rest[-3:]

        def fetch(name, block):
            if name in (N.w_fc1, N.w_fc2):
                b.load(name, b[name + str(block)])
            elif name in (N.key, N.value):
                b.load(name, b[N.in_ + HELD[block][name]], b.refs[name].at[pl.ds(0, rows)])
            else:
                b.load(name, b[N.in_ + HELD[block][name]])

        b.load(N.res, b[N.res_in])
        fetch(N.fd, 1)
        b.load(N.vec, b[N.vec_out])
        for name in (N.inner, N.w_fc2, N.slope, N.active, N.w_fc1, N.mid, N.br, N.mix, N.query, N.key, N.value, N.aq):
            fetch(name, 1)
        b.load(N.key2, b[N.k2_out], b.refs[N.key].at[pl.ds(rows, rows)])
        b.load(N.value2, b[N.v2_out], b.refs[N.value].at[pl.ds(rows, rows)])
        b[N.sums][...] = jnp.zeros(b[N.sums].shape, WIDE)
        left = {}
        for kind, block, _ in owners:
            left[kind, block] = left.get((kind, block), 0) + 1

        def ended(i):
            kind, block, _ = owners[i]
            left[kind, block] -= 1
            if left[kind, block] == 0:
                name, out = N.shard_ + kind + str(block), b[N.out_ + kind]
                if kind == N.extra:
                    held_rows = b[name][...]
                    name = N.rows_extra
                    b[name][...] = lax.dot_general(
                        held_rows, unit_matrix(held_rows.shape[0]), (((0,), (0,)), ((), ())),
                        precision=lax.Precision.HIGHEST, preferred_element_type=WIDE,
                    )
                b.save(name, out if kind == N.extra else out.at[block])

        reducer = Reducer(
            line, items, slots, [b[N.g_ + kind + str(block)] for kind, block, _ in owners],
            [b[N.shard_ + kind + str(block)] for kind, block, _ in owners],
            shared, single, send, recv, credit, ended,
        )
        waiting, fresh = [], [0]

        def settle(count):
            for _ in range(count):
                kind, block, chunk, entry = waiting.pop(0)
                b.settle([entry])
                for i, owner in enumerate(owners):
                    if owner[:2] == (kind, block):
                        if chunk == (hidden // model - 1 if kind == N.fc2 else owner[2]):
                            reducer.ready.add(i)

        def spend(time):
            settle(len(waiting) - fresh[0])
            reducer.spend(time)
            fresh[0] = 0

        def emitter(block):
            def emit(kind, chunk, stage):
                out = b[N.g_ + kind + str(block)]
                target = out.at[chunk] if kind == N.fc2 else out
                if kind in (N.fc1, N.qkv):
                    target = out.at[:, :, :, pl.ds(chunk * model, model)]
                b.save(stage, target)
                waiting.append((kind, block, chunk, b.saving[-1]))
                fresh[0] += 1

            return emit

        def bring(*names):
            for name in names:
                fetch(name, 0)

        b[N.res]
        backward_compute(b, 1, 2, spend, emitter(1), bring)
        backward_compute(b, 0, 1, spend, emitter(0), lambda *names: None)
        b.save(N.res, b[N.res_out])
        table_of_sums(b, (2, 4))
        b[N.table4][...] = b[N.table][...].astype(LOW).reshape(b[N.table4].shape)
        emitter(0)(N.extra, 0, N.table4)
        settle(len(waiting))
        reducer.complete()
        b.drain()

    return call(body, ins, small, outs, scratch, 128, extra, N.backward, 1, 64 << 20)


def fused(
    devices, patches, order, grad_latent, grad_out, pos_embed, ln_gain, ln_bias, w_qkv, b_qkv, w_proj, b_proj,
    w_fc1, b_fc1, w_fc2, b_fc2, layer_scale,
):
    line = devices // 8
    model = patches.shape[1]
    own = pos_embed.shape[1]
    marks = jnp.concatenate([order[:, :VIS], order[:, VIS:]], axis=0)
    marks = jnp.pad(marks, ((0, 0), (0, SET - VIS)), constant_values=-1)
    vectors = (ln_gain, ln_bias, layer_scale, b_proj, b_fc2, b_qkv, b_fc1)
    held = [pos_embed] + list(vectors)
    counts = [array.size // own for array in held]
    wide = -(-sum(counts) // 128) * 128
    tables = fold_tables(model, own, b_qkv.shape[1] // own) + fold_tables(model, own, b_fc1.shape[1] // own)
    kept = forward(patches, marks, held, wide, (w_qkv, w_proj, w_fc1, w_fc2), line, tables)
    made = backward(kept, grad_out, grad_latent, marks, line, tables)
    parts, at = [], 0
    for array, count in zip((pos_embed,) + vectors, counts):
        parts.append(made[N.out_extra][at : at + count].reshape(array.shape))
        at += count
    pos_shard, gains, shifts, scales, proj_b, fc2_b, qkv_b, fc1_b = parts
    return (
        kept[N.latent_out], kept[N.regressed_out], made[N.res_out], pos_shard,
        gains, shifts, made[N.out_qkv], qkv_b, made[N.out_proj], proj_b,
        made[N.out_fc1], fc1_b, made[N.out_fc2], fc2_b, scales,
    )


def norm_forward(value, gain, shift):
    center = jnp.mean(value, axis=-1, keepdims=True)
    centered = value - center
    inverse = lax.rsqrt(jnp.mean(centered * centered, axis=-1, keepdims=True) + 1e-06)
    normed = centered * inverse
    return (normed * gain + shift, normed, inverse)


def norm_backward(grad, normed, inverse, gain):
    scaled = grad * gain
    first_mean = jnp.mean(scaled, axis=-1, keepdims=True)
    second_mean = jnp.mean(scaled * normed, axis=-1, keepdims=True)
    back = inverse * (scaled - first_mean - normed * second_mean)
    return (back, jnp.sum(grad * normed, axis=0), jnp.sum(grad, axis=0))


def unpack(pieces):
    gains, shifts, w_qkv, b_qkv, w_proj, b_proj, w_fc1, b_fc1, w_fc2, b_fc2, scales = pieces
    wide = jnp.float32
    return (
        gains.astype(wide),
        shifts.astype(wide),
        w_qkv,
        b_qkv.astype(wide),
        w_proj,
        b_proj.astype(wide),
        w_fc1,
        b_fc1.astype(wide),
        w_fc2,
        b_fc2.astype(wide),
        scales.astype(wide),
    )


def fetch(block, arrays):
    ln_gain, ln_bias, w_qkv, b_qkv, w_proj, b_proj, w_fc1, b_fc1, w_fc2, b_fc2, layer_scale = arrays
    gathered = (
        lax.all_gather(ln_gain[block], ("dp", "fsdp"), axis=1, tiled=True),
        lax.all_gather(ln_bias[block], ("dp", "fsdp"), axis=1, tiled=True),
        lax.all_gather(w_qkv[block], ("dp", "fsdp"), axis=0, tiled=True),
        lax.all_gather(b_qkv[block], ("dp", "fsdp"), axis=0, tiled=True),
        lax.all_gather(w_proj[block], ("dp", "fsdp"), axis=0, tiled=True),
        lax.all_gather(b_proj[block], ("dp", "fsdp"), axis=0, tiled=True),
        lax.all_gather(w_fc1[block], ("dp", "fsdp"), axis=0, tiled=True),
        lax.all_gather(b_fc1[block], ("dp", "fsdp"), axis=0, tiled=True),
        lax.all_gather(w_fc2[block], ("dp", "fsdp"), axis=0, tiled=True),
        lax.all_gather(b_fc2[block], ("dp", "fsdp"), axis=0, tiled=True),
        lax.all_gather(layer_scale[block], ("dp", "fsdp"), axis=1, tiled=True),
    )
    return unpack(gathered)


def column_sum(value):
    return jnp.sum(value.astype(jnp.float32), axis=0)


def outer_rows(left, right):
    return jnp.einsum("rd,rf->df", left, right, preferred_element_type=jnp.float32)


def attend_scores(queries, keys, key_live):
    scores = jnp.einsum("gqhe,gkhe->ghqk", queries, keys, preferred_element_type=jnp.float32) * (
        1.0 / math.sqrt(HEAD_DIM)
    )
    return jnp.where(key_live, scores, -1e30)


def attend_forward(query_in, key_in, images, key_live, weights):
    w_qkv, b_qkv, w_proj, b_proj = (weights[2], weights[3], weights[4], weights[5])
    model = query_in.shape[1]
    heads = model // HEAD_DIM
    queries = (
        jnp.dot(query_in, w_qkv[:, :model], preferred_element_type=jnp.float32) + b_qkv[:model]
    ).astype(jnp.bfloat16)
    paired = jnp.dot(key_in, w_qkv[:, model:], preferred_element_type=jnp.float32)
    keys = paired[:, :model].astype(jnp.bfloat16).reshape(images, -1, heads, HEAD_DIM)
    values = (
        (paired[:, model:] + b_qkv[model:])
        .astype(jnp.bfloat16)
        .reshape(images, -1, heads, HEAD_DIM)
    )
    queries = queries.reshape(images, -1, heads, HEAD_DIM)
    scores = attend_scores(queries, keys, key_live)
    highest_score = jnp.max(scores, axis=-1, keepdims=True)
    weighted = jnp.exp(scores - highest_score)
    summed = jnp.sum(weighted, axis=-1, keepdims=True)
    softmax_out = (weighted / summed).astype(jnp.bfloat16)
    mixed = jnp.einsum("ghqk,gkhe->gqhe", softmax_out, values, preferred_element_type=jnp.float32)
    mixed = mixed.reshape(-1, model).astype(jnp.bfloat16)
    branch = jnp.dot(mixed, w_proj, preferred_element_type=jnp.float32) + b_proj
    return (branch, (queries, keys, values, highest_score + jnp.log(summed), mixed))


def attend_backward(grad_branch, query_in, key_in, key_live, kept, weights):
    w_qkv, w_proj = (weights[2], weights[4])
    queries, keys, values, log_total, mixed = kept
    model = query_in.shape[1]
    grad_low = grad_branch.astype(jnp.bfloat16)
    grad_w_proj = outer_rows(mixed, grad_low)
    grad_b_proj = column_sum(grad_low)
    grad_mixed = (
        jnp.dot(grad_low, w_proj.T, preferred_element_type=jnp.float32)
        .astype(jnp.bfloat16)
        .reshape(queries.shape)
    )
    softmax_out = jnp.exp(attend_scores(queries, keys, key_live) - log_total)
    grad_values = jnp.einsum(
        "ghqk,gqhe->gkhe",
        softmax_out.astype(jnp.bfloat16),
        grad_mixed,
        preferred_element_type=jnp.float32,
    )
    grad_soft = jnp.einsum(
        "gqhe,gkhe->ghqk", grad_mixed, values, preferred_element_type=jnp.float32
    )
    grad_scores = (
        softmax_out * (grad_soft - jnp.sum(grad_soft * softmax_out, axis=-1, keepdims=True))
    ).astype(jnp.bfloat16)
    factor = 1.0 / math.sqrt(HEAD_DIM)
    grad_queries = (
        (
            jnp.einsum("ghqk,gkhe->gqhe", grad_scores, keys, preferred_element_type=jnp.float32)
            * factor
        )
        .astype(jnp.bfloat16)
        .reshape(-1, model)
    )
    grad_keys = (
        (
            jnp.einsum("ghqk,gqhe->gkhe", grad_scores, queries, preferred_element_type=jnp.float32)
            * factor
        )
        .astype(jnp.bfloat16)
        .reshape(-1, model)
    )
    grad_values = grad_values.astype(jnp.bfloat16).reshape(-1, model)
    grad_pairs = jnp.concatenate([grad_keys, grad_values], axis=1)
    grad_w_qkv = jnp.concatenate(
        [outer_rows(query_in, grad_queries), outer_rows(key_in, grad_pairs)], axis=1
    )
    grad_b_qkv = jnp.concatenate([column_sum(grad_queries), column_sum(grad_values)])
    grad_query_in = jnp.dot(grad_queries, w_qkv[:, :model].T, preferred_element_type=jnp.float32)
    grad_key_in = jnp.dot(grad_pairs, w_qkv[:, model:].T, preferred_element_type=jnp.float32)
    return (grad_query_in, grad_key_in, (grad_w_qkv, grad_b_qkv, grad_w_proj, grad_b_proj))


def feed_forward(middle, weights):
    gains, shifts, w_fc1, b_fc1, w_fc2, b_fc2 = (
        weights[0],
        weights[1],
        weights[6],
        weights[7],
        weights[8],
        weights[9],
    )
    normed_out, normed, inverse = norm_forward(middle, gains[1], shifts[1])
    inner_in = normed_out.astype(jnp.bfloat16)
    hidden = jnp.dot(inner_in, w_fc1, preferred_element_type=jnp.float32) + b_fc1
    active = jax.nn.gelu(hidden, approximate=True).astype(jnp.bfloat16)
    branch = jnp.dot(active, w_fc2, preferred_element_type=jnp.float32) + b_fc2
    return (branch, (normed, inverse, inner_in, hidden, active))


def feed_backward(grad_branch, kept, weights):
    gains, w_fc1, w_fc2 = (weights[0], weights[6], weights[8])
    normed, inverse, inner_in, hidden, active = kept
    grad_low = grad_branch.astype(jnp.bfloat16)
    grad_w_fc2 = outer_rows(active, grad_low)
    grad_b_fc2 = column_sum(grad_low)
    grad_active = jnp.dot(grad_low, w_fc2.T, preferred_element_type=jnp.float32)
    gelu_back = jax.vjp(functools.partial(jax.nn.gelu, approximate=True), hidden)[1]
    grad_hidden = gelu_back(grad_active)[0].astype(jnp.bfloat16)
    grad_w_fc1 = outer_rows(inner_in, grad_hidden)
    grad_b_fc1 = column_sum(grad_hidden)
    grad_normed = jnp.dot(grad_hidden, w_fc1.T, preferred_element_type=jnp.float32)
    grad_middle, grad_gain, grad_shift = norm_backward(grad_normed, normed, inverse, gains[1])
    return (grad_middle, grad_gain, grad_shift, (grad_w_fc1, grad_b_fc1, grad_w_fc2, grad_b_fc2))


def local(
    patches,
    order,
    grad_latent,
    grad_out,
    pos_embed,
    ln_gain,
    ln_bias,
    w_qkv,
    b_qkv,
    w_proj,
    b_proj,
    w_fc1,
    b_fc1,
    w_fc2,
    b_fc2,
    layer_scale,
):
    arrays = (
        ln_gain,
        ln_bias,
        w_qkv,
        b_qkv,
        w_proj,
        b_proj,
        w_fc1,
        b_fc1,
        w_fc2,
        b_fc2,
        layer_scale,
    )
    images = order.shape[0]
    model = patches.shape[1]
    highest = lax.Precision.HIGHEST
    live = jnp.arange(SET) < VIS
    live_rows = jnp.tile(live, images).astype(jnp.float32)[:, None]
    patch_slots = jnp.arange(PATCHES)

    def picker(index):
        padded = jnp.pad(index, ((0, 0), (0, SET - VIS)))
        chosen = (padded[:, :, None] == patch_slots[None, None, :]) & live[None, :, None]
        return chosen.astype(jnp.float32).reshape(-1, PATCHES)

    pick_visible = picker(order[:, :VIS])
    pick_masked = picker(order[:, VIS:])
    pos_table = lax.all_gather(pos_embed, ("dp", "fsdp"), axis=1, tiled=True).astype(jnp.float32)
    enc_weights, reg_weights = fetch(0, arrays), fetch(1, arrays)
    start = patches.astype(jnp.float32) + jnp.dot(pick_visible, pos_table, precision=highest)
    enc_out, enc_normed, enc_inverse = norm_forward(start, enc_weights[0][0], enc_weights[1][0])
    enc_attn_in = enc_out.astype(jnp.bfloat16)
    enc_branch, enc_attn_kept = attend_forward(enc_attn_in, enc_attn_in, images, live, enc_weights)
    enc_middle = start + enc_weights[10][0] * enc_branch
    enc_feed, enc_feed_kept = feed_forward(enc_middle, enc_weights)
    latent_f = enc_middle + enc_weights[10][1] * enc_feed
    query_start = jnp.dot(pick_masked, pos_table, precision=highest)
    query_out, query_normed, query_inverse = norm_forward(
        query_start, reg_weights[0][0], reg_weights[1][0]
    )
    latent_out, latent_normed, latent_inverse = norm_forward(
        latent_f, reg_weights[0][0], reg_weights[1][0]
    )
    query_in = query_out.astype(jnp.bfloat16)
    key_in = jnp.concatenate(
        [
            latent_out.astype(jnp.bfloat16).reshape(images, SET, model),
            query_in.reshape(images, SET, model),
        ],
        axis=1,
    ).reshape(-1, model)
    key_live = jnp.concatenate([live, live])
    reg_branch, reg_attn_kept = attend_forward(query_in, key_in, images, key_live, reg_weights)
    reg_middle = query_start + reg_weights[10][0] * reg_branch
    reg_feed, reg_feed_kept = feed_forward(reg_middle, reg_weights)
    regressed_f = reg_middle + reg_weights[10][1] * reg_feed
    reg_back = reg_weights
    grad_final = grad_out * live_rows
    reg_scale_late = jnp.sum(grad_final * reg_feed, axis=0)
    grad_from_feed, reg_gain_late, reg_shift_late, reg_feed_grads = feed_backward(
        reg_back[10][1] * grad_final, reg_feed_kept, reg_back
    )
    grad_reg_middle = grad_final + grad_from_feed
    reg_scale_early = jnp.sum(grad_reg_middle * reg_branch, axis=0)
    grad_query_in, grad_key_in, reg_attn_grads = attend_backward(
        reg_back[10][0] * grad_reg_middle, query_in, key_in, key_live, reg_attn_kept, reg_back
    )
    grad_key_in = grad_key_in.reshape(images, 2 * SET, model)
    grad_query_norm = grad_query_in + grad_key_in[:, SET:].reshape(-1, model)
    grad_latent_norm = grad_key_in[:, :SET].reshape(-1, model)
    back_query, reg_gain_query, reg_shift_query = norm_backward(
        grad_query_norm, query_normed, query_inverse, reg_back[0][0]
    )
    back_latent, reg_gain_key, reg_shift_key = norm_backward(
        grad_latent_norm, latent_normed, latent_inverse, reg_back[0][0]
    )
    grad_query_start = grad_reg_middle + back_query
    reg_grads = (
        (
            jnp.stack([reg_gain_query + reg_gain_key, reg_gain_late]),
            jnp.stack([reg_shift_query + reg_shift_key, reg_shift_late]),
        )
        + reg_attn_grads
        + reg_feed_grads
        + (jnp.stack([reg_scale_early, reg_scale_late]),)
    )
    enc_back = enc_weights
    grad_finish = grad_latent * live_rows + back_latent
    enc_scale_late = jnp.sum(grad_finish * enc_feed, axis=0)
    grad_from_feed, enc_gain_late, enc_shift_late, enc_feed_grads = feed_backward(
        enc_back[10][1] * grad_finish, enc_feed_kept, enc_back
    )
    grad_enc_middle = grad_finish + grad_from_feed
    enc_scale_early = jnp.sum(grad_enc_middle * enc_branch, axis=0)
    grad_as_query, grad_as_key, enc_attn_grads = attend_backward(
        enc_back[10][0] * grad_enc_middle, enc_attn_in, enc_attn_in, live, enc_attn_kept, enc_back
    )
    back_start, enc_gain_early, enc_shift_early = norm_backward(
        grad_as_query + grad_as_key, enc_normed, enc_inverse, enc_back[0][0]
    )
    grad_start = grad_enc_middle + back_start
    grad_table = jnp.dot(pick_visible.T, grad_start, precision=highest) + jnp.dot(
        pick_masked.T, grad_query_start, precision=highest
    )
    enc_grads = (
        (jnp.stack([enc_gain_early, enc_gain_late]), jnp.stack([enc_shift_early, enc_shift_late]))
        + enc_attn_grads
        + enc_feed_grads
        + (jnp.stack([enc_scale_early, enc_scale_late]),)
    )
    reg_shards = (
        lax.psum_scatter(reg_grads[0], ("dp", "fsdp"), scatter_dimension=1, tiled=True),
        lax.psum_scatter(reg_grads[1], ("dp", "fsdp"), scatter_dimension=1, tiled=True),
        lax.psum_scatter(reg_grads[2], ("dp", "fsdp"), scatter_dimension=0, tiled=True),
        lax.psum_scatter(reg_grads[3], ("dp", "fsdp"), scatter_dimension=0, tiled=True),
        lax.psum_scatter(reg_grads[4], ("dp", "fsdp"), scatter_dimension=0, tiled=True),
        lax.psum_scatter(reg_grads[5], ("dp", "fsdp"), scatter_dimension=0, tiled=True),
        lax.psum_scatter(reg_grads[6], ("dp", "fsdp"), scatter_dimension=0, tiled=True),
        lax.psum_scatter(reg_grads[7], ("dp", "fsdp"), scatter_dimension=0, tiled=True),
        lax.psum_scatter(reg_grads[8], ("dp", "fsdp"), scatter_dimension=0, tiled=True),
        lax.psum_scatter(reg_grads[9], ("dp", "fsdp"), scatter_dimension=0, tiled=True),
        lax.psum_scatter(reg_grads[10], ("dp", "fsdp"), scatter_dimension=1, tiled=True),
    )
    enc_shards = (
        lax.psum_scatter(grad_table, ("dp", "fsdp"), scatter_dimension=1, tiled=True),
        lax.psum_scatter(enc_grads[0], ("dp", "fsdp"), scatter_dimension=1, tiled=True),
        lax.psum_scatter(enc_grads[1], ("dp", "fsdp"), scatter_dimension=1, tiled=True),
        lax.psum_scatter(enc_grads[2], ("dp", "fsdp"), scatter_dimension=0, tiled=True),
        lax.psum_scatter(enc_grads[3], ("dp", "fsdp"), scatter_dimension=0, tiled=True),
        lax.psum_scatter(enc_grads[4], ("dp", "fsdp"), scatter_dimension=0, tiled=True),
        lax.psum_scatter(enc_grads[5], ("dp", "fsdp"), scatter_dimension=0, tiled=True),
        lax.psum_scatter(enc_grads[6], ("dp", "fsdp"), scatter_dimension=0, tiled=True),
        lax.psum_scatter(enc_grads[7], ("dp", "fsdp"), scatter_dimension=0, tiled=True),
        lax.psum_scatter(enc_grads[8], ("dp", "fsdp"), scatter_dimension=0, tiled=True),
        lax.psum_scatter(enc_grads[9], ("dp", "fsdp"), scatter_dimension=0, tiled=True),
        lax.psum_scatter(enc_grads[10], ("dp", "fsdp"), scatter_dimension=1, tiled=True),
    )
    pos_shard = enc_shards[0]
    weight_shards = tuple(
        (jnp.stack([early, late]) for early, late in zip(enc_shards[1:], reg_shards))
    )
    return (
        latent_f.astype(jnp.bfloat16),
        regressed_f.astype(jnp.bfloat16),
        grad_start,
        pos_shard,
    ) + weight_shards


def solution(mesh):
    in_specs = (
        P(("dp", "fsdp"), None),
        P(("dp", "fsdp"), None),
        P(("dp", "fsdp"), None),
        P(("dp", "fsdp"), None),
        P(None, ("dp", "fsdp")),
        P(None, None, ("dp", "fsdp")),
        P(None, None, ("dp", "fsdp")),
        P(None, ("dp", "fsdp"), None),
        P(None, ("dp", "fsdp")),
        P(None, ("dp", "fsdp"), None),
        P(None, ("dp", "fsdp")),
        P(None, ("dp", "fsdp"), None),
        P(None, ("dp", "fsdp")),
        P(None, ("dp", "fsdp"), None),
        P(None, ("dp", "fsdp")),
        P(None, None, ("dp", "fsdp")),
    )
    out_specs = (
        P(("dp", "fsdp"), None),
        P(("dp", "fsdp"), None),
        P(("dp", "fsdp"), None),
        P(None, ("dp", "fsdp")),
        P(None, None, ("dp", "fsdp")),
        P(None, None, ("dp", "fsdp")),
        P(None, ("dp", "fsdp"), None),
        P(None, ("dp", "fsdp")),
        P(None, ("dp", "fsdp"), None),
        P(None, ("dp", "fsdp")),
        P(None, ("dp", "fsdp"), None),
        P(None, ("dp", "fsdp")),
        P(None, ("dp", "fsdp"), None),
        P(None, ("dp", "fsdp")),
        P(None, None, ("dp", "fsdp")),
    )
    devices = mesh.shape["dp"] * mesh.shape["fsdp"]

    def step(*args):
        rows = args[7].shape[1]
        kernels = mesh.shape["fsdp"] == 4 and rows // (devices // 2) % 16 == 0
        run = jax.shard_map(
            functools.partial(fused, devices) if kernels else local,
            mesh=mesh,
            in_specs=in_specs,
            out_specs=out_specs,
            check_vma=False,
        )
        return run(*args)

    return step
```
